256 devices in a mesh: dp: 32 (over y, x, z_hi), expert: 8 (over z_lo, core).
Axes of the slice: x: 4, y: 4, z: 8 (z_hi: 2, z_lo: 4; z = z_hi * 4 + z_lo), core: 2. Of those that a mesh axis runs over, the one named last changes fastest.
Arguments:
- tokens: bfloat16 [32768, 768], P(('dp', 'expert')), may hold values from -6 to 6
- expert_ids: int32 [32768, 1], P(('dp', 'expert')), may hold values from 0 to 7
- gate: float32 [32768], P(('dp', 'expert')), may hold values from 0.2 to 1
- ln_gain: float32 [768], replicated, may hold values from 0.25 to 1.75
- w_in: bfloat16 [8, 768, 3072], P('expert', 'dp'), may hold values from -0.21875 to 0.21875
- w_out: bfloat16 [8, 3072, 768], P('expert', 'dp'), may hold values from -0.109375 to 0.109375
- image_emb: bfloat16 [2048, 768], P(('dp', 'expert')), may hold values from -6 to 6
Outputs:
- token_grad: bfloat16 [32768, 768], P(('dp', 'expert'))
- gate_grad: float32 [32768], P(('dp', 'expert'))
- w_in_grad: float32 [8, 768, 3072], P('expert', 'dp')
- w_out_grad: float32 [8, 3072, 768], P('expert', 'dp')
The draws below stay inside these ranges and needn't reach their ends.
Inputs may be any that keep to these rules, and one draw needn't show every extreme that they name: `expert_ids`: each token names one expert.
All inputs are finite; a program needn't handle non-finite values.
Results may differ from the reference program's by a relative error of at most 0.028.
Values may be sent and summed in bfloat16 or wider, within the bound.
A program may use at most 64 MiB of HBM per device.

```python
import jax
import jax.numpy as jnp
from jax import lax

D = 768
H = 3072
E = 8
TEXT_LEN = 16
TOK_DEV = 128
CAP = 20
TOKENS = 32768
PAIRS = 2048
N_DP = 32
N_EXPERT = 8


def shared_direction(key):
    return jax.random.normal(jax.random.fold_in(key, 101), (D,), jnp.float32)


def draw_tokens(key, part):
    common = shared_direction(key)
    key = jax.random.fold_in(key, 7)
    noise_key, pair_key = jax.random.split(key)
    noise = jax.random.normal(noise_key, (TOKENS, D), jnp.float32)
    top = 0.02
    blocks = TOKENS // TOK_DEV
    row_block = jnp.arange(TOKENS, dtype=jnp.int32) // TOK_DEV
    rise = top * row_block.astype(jnp.float32) / max(blocks - 1, 1)
    pairing = jax.random.permutation(pair_key, N_DP)
    column_block = jnp.arange(D, dtype=jnp.int32) // (D // N_DP)
    owner_block = pairing[row_block // N_EXPERT]
    spike = jnp.where(column_block[None, :] == owner_block[:, None], 3.0, 1.0)
    values = noise * spike + rise[:, None] * common[None, :]
    return jnp.clip(values, -6.0, 6.0).astype(jnp.bfloat16)


def draw_image_emb(key, part):
    common = shared_direction(key)
    key = jax.random.fold_in(key, 9)
    noise = jax.random.normal(key, (PAIRS, D), jnp.float32)
    values = noise + common[None, :]
    return jnp.clip(values, -6.0, 6.0).astype(jnp.bfloat16)


def shard_levels(own_key, shape, shards, low, high):
    factor_of = 1.0
    for axis_at, parts in shards:
        draws = jax.random.uniform(jax.random.fold_in(jax.random.fold_in(own_key, 6), axis_at), (parts,), jnp.float32, low / len(shards), high / len(shards))
        factor_of = factor_of * jnp.repeat(jnp.exp(draws), shape[axis_at] // parts).reshape((-1,) + (1,) * (len(shape) - 1 - axis_at))
    return factor_of


def picks_of(rng, rows, amount, top, lift):
    sequence = jax.random.permutation(jax.random.fold_in(rng, 1), amount)
    pull = sequence
    for power in range(3):
        pull = pull * pull // amount
    pull = pull * lift // amount
    tickets = jax.random.randint(jax.random.fold_in(rng, 2), (rows, amount), 0, 4096) + pull
    holders = jax.random.permutation(jax.random.fold_in(rng, 3), rows)[jnp.arange(amount) % rows]
    tickets = jnp.where(jnp.arange(rows)[:, None] == holders[None, :], 1 << 14, tickets)
    merit = tickets * amount + jnp.arange(amount)
    return lax.top_k(merit.astype(jnp.int32), top)[1].astype(jnp.int32)


def bell_draw(own_key, extent, scale, limit, pieces=(), kind=jnp.bfloat16):
    entries = scale * jax.random.normal(own_key, extent, jnp.float32)
    if pieces:
        entries = entries * shard_levels(own_key, extent, pieces, -0.22, 0.18)
    return jnp.clip(entries, -limit, limit).astype(kind)


def setup_inputs(seed: int = 0) -> dict:
    splits = jax.random.split(jax.random.key(seed), 8)
    tokens = draw_tokens(jax.random.fold_in(splits[7], 71), 0)
    expert_ids = picks_of(splits[1], TOKENS, E, 1, 1024)
    gate = jnp.clip(0.2 + 0.8 * jax.random.uniform(splits[2], (TOKENS,), jnp.float32) ** shard_levels(splits[2], (TOKENS,), ((0, 256),), -0.2, 0.2), 0.2, 1.0)
    ln_gain = jnp.clip(1.0 + 0.15 * jax.random.normal(splits[3], (D,), jnp.float32), 0.25, 1.75)
    w_in = bell_draw(splits[4], (E, D, H), D ** -0.5, 0.21875, ((0, 8), (1, 32)))
    w_out = bell_draw(splits[5], (E, H, D), H ** -0.5, 0.109375, ((0, 8), (1, 32)))
    image_emb = draw_image_emb(jax.random.fold_in(splits[7], 71), 0)
    return dict(tokens=tokens, expert_ids=expert_ids, gate=gate, ln_gain=ln_gain, w_in=w_in, w_out=w_out, image_emb=image_emb)


logit_scale = 100.0
norm_eps = 1e-06

def exact_gelu(values):
    return jax.nn.gelu(values, approximate=False)

def layer_norm(inputs, ln_gain):
    average = lax.optimization_barrier(jnp.mean(inputs, axis=-1, keepdims=True))
    centred = inputs - average
    variance = lax.optimization_barrier(jnp.mean(centred * centred, axis=-1, keepdims=True))
    inverse = lax.rsqrt(variance + norm_eps)
    scaled = centred * inverse
    return (scaled, inverse, (scaled * ln_gain).astype(jnp.bfloat16))

def unit_rows(values):
    inverse = lax.rsqrt(lax.optimization_barrier(jnp.sum(values * values, axis=-1, keepdims=True)) + norm_eps)
    return (values * inverse, inverse)

def reference(tokens, expert_ids, gate, ln_gain, w_in, w_out, image_emb):
    inputs = tokens.astype(jnp.float32)
    scaled, inverse, normed = layer_norm(inputs, ln_gain)
    choose = expert_ids[:, 0].astype(jnp.int32)
    blocks = TOKENS // TOK_DEV
    onehot = (choose.reshape(blocks, TOK_DEV)[:, :, None] == jnp.arange(E, dtype=jnp.int32)[None, None, :]).astype(jnp.int32)
    before = jnp.cumsum(onehot, axis=1) - onehot
    slot = lax.optimization_barrier(jnp.sum(before * onehot, axis=2)).reshape(TOKENS)
    kept = slot < CAP
    source = jnp.arange(TOKENS, dtype=jnp.int32) // TOK_DEV
    total_rows = blocks * CAP
    place = jnp.where(kept, source * CAP + slot, total_rows).astype(jnp.int32)
    safe_place = jnp.minimum(place, total_rows - 1).astype(jnp.int32)
    buffers = jnp.zeros((E, total_rows, D), jnp.bfloat16).at[choose, place].set(normed, mode='drop')

    def forward(operands):
        slots_in, first, second = operands
        pre = jnp.dot(slots_in, first, preferred_element_type=jnp.float32)
        activated = exact_gelu(pre).astype(jnp.bfloat16)
        return jnp.dot(activated, second, preferred_element_type=jnp.float32).astype(jnp.bfloat16)
    outputs = lax.map(forward, (buffers, w_in, w_out))
    expert_out = jnp.where(kept[:, None], outputs[choose, safe_place], jnp.zeros((), jnp.bfloat16)).astype(jnp.float32)
    layer_out = inputs + gate[:, None] * expert_out
    pooled = lax.optimization_barrier(jnp.mean(layer_out.reshape(PAIRS, TEXT_LEN, D), axis=1))
    text_unit, text_inverse = unit_rows(pooled)
    text_emb = text_unit.astype(jnp.bfloat16)
    image_norm = unit_rows(image_emb.astype(jnp.float32))[0].astype(jnp.bfloat16)
    scores = logit_scale * jnp.dot(text_emb, image_norm.T, preferred_element_type=jnp.float32)
    expscores = jnp.exp(scores)
    row_total = lax.optimization_barrier(jnp.sum(expscores, axis=1))
    col_total = lax.optimization_barrier(jnp.sum(expscores, axis=0))
    coefs = (0.5 * (expscores / row_total[:, None] + expscores / col_total[None, :]) - jnp.eye(PAIRS, dtype=jnp.float32)).astype(jnp.bfloat16)
    text_back = logit_scale * jnp.dot(coefs, image_norm, preferred_element_type=jnp.float32)
    pooled_back = text_inverse * (text_back - text_unit * lax.optimization_barrier(jnp.sum(text_unit * text_back, axis=1, keepdims=True)))
    layer_back = jnp.repeat(pooled_back / TEXT_LEN, TEXT_LEN, axis=0)
    gate_grad = lax.optimization_barrier(jnp.sum(layer_back * expert_out, axis=1))
    out_back = (gate[:, None] * layer_back).astype(jnp.bfloat16)
    back_buffers = jnp.zeros((E, total_rows, D), jnp.bfloat16).at[choose, place].set(out_back, mode='drop')
    group_rows = total_rows // N_DP

    def backward(operands):
        slots_in, slots_back, first, second = operands
        pre = jnp.dot(slots_in, first, preferred_element_type=jnp.float32)
        activated, gelu_back = jax.vjp(exact_gelu, pre)
        activated = activated.astype(jnp.bfloat16)
        act_back = jnp.dot(slots_back, second.T, preferred_element_type=jnp.float32)
        pre_back = gelu_back(act_back)[0].astype(jnp.bfloat16)
        in_back = jnp.dot(pre_back, first.T, preferred_element_type=jnp.float32).astype(jnp.bfloat16)
        grouped_in = slots_in.reshape(N_DP, group_rows, D).astype(jnp.float32)
        grouped_pre = pre_back.reshape(N_DP, group_rows, H).astype(jnp.float32)
        grouped_act = activated.reshape(N_DP, group_rows, H).astype(jnp.float32)
        grouped_back = slots_back.reshape(N_DP, group_rows, D).astype(jnp.float32)
        part_in = jnp.einsum('gkd,gkh->gdh', grouped_in, grouped_pre)
        part_in = lax.optimization_barrier(part_in.astype(jnp.bfloat16)).astype(jnp.float32)
        part_out = jnp.einsum('gkh,gkd->ghd', grouped_act, grouped_back)
        part_out = lax.optimization_barrier(part_out.astype(jnp.bfloat16)).astype(jnp.float32)
        return (in_back, lax.optimization_barrier(jnp.sum(part_in, axis=0)), lax.optimization_barrier(jnp.sum(part_out, axis=0)))
    in_backs, grad_in, grad_out = lax.map(backward, (buffers, back_buffers, w_in, w_out))
    normed_back = jnp.where(kept[:, None], in_backs[choose, safe_place], jnp.zeros((), jnp.bfloat16)).astype(jnp.float32)
    gained = normed_back * ln_gain
    token_back = layer_back + inverse * (gained - lax.optimization_barrier(jnp.mean(gained, axis=1, keepdims=True)) - scaled * lax.optimization_barrier(jnp.mean(gained * scaled, axis=1, keepdims=True)))
    return (token_back.astype(jnp.bfloat16), gate_grad, grad_in, grad_out)
```

```python
import jax
import jax.numpy as jnp
from jax import lax
from jax.experimental import pallas as pl
from jax.experimental.pallas import tpu as pltpu
from jax.sharding import PartitionSpec as P

MESH = pl.DeviceIdType.MESH
F32 = jnp.float32
BF16 = jnp.bfloat16

D = 768
H = 3072
HALF = 1536
TOK = 128
CAP = 20
PAIR = 8
TEXT = 16
N = 16
R = 4
RO = 96
RI = 48
SLOTS = 320
SP = 384
EPS = 1e-6
SCALE = 100.0


def dot(a, b, ca=1, cb=0):
    return lax.dot_general(a, b, (((ca,), (cb,)), ((), ())), preferred_element_type=F32)


def iota(shape, axis):
    return lax.broadcasted_iota(jnp.int32, shape, axis)


def hot(mask):
    return jnp.where(mask, 1.0, 0.0).astype(BF16)


def split2(v):
    hi = v.astype(BF16)
    return hi, (v - hi.astype(F32)).astype(BF16)


def wrap(v):
    return lax.rem(v + 2 * R, R)


class Gather:
    def __init__(self, block, c1, c2, dev1, dev2, sem):
        self.block, self.c1, self.c2 = block, c1, c2
        self.dev1, self.dev2, self.sem = dev1, dev2, sem
        self.bs = [c1, wrap(c1 - 1), wrap(c1 + 1), wrap(c1 + 2)]

    def copy(self, k, ref, dev):
        return pltpu.make_async_remote_copy(
            src_ref=ref, dst_ref=ref, send_sem=self.sem.at[0, k], recv_sem=self.sem.at[1, k],
            device_id=dev, device_id_type=MESH,
        )

    def at(self, a, b, half=None):
        return self.block(wrap(a), wrap(b), half)

    def second(self, i):
        ref = self.at(self.bs[i], self.c2)
        self.copy(4 + 4 * i, ref, self.dev2(1)).start()
        self.copy(5 + 4 * i, ref, self.dev2(-1)).start()

    def start(self):
        ref = self.at(self.c1, self.c2)
        self.copy(0, ref, self.dev1(1)).start()
        self.copy(1, ref, self.dev1(-1)).start()
        self.second(0)

    def stage1(self):
        c1, c2 = self.c1, self.c2
        self.copy(0, self.at(c1 - 1, c2), self.dev1(1)).wait_recv()
        self.copy(2, self.at(c1 - 1, c2, 0), self.dev1(1)).start()
        self.second(1)
        self.copy(1, self.at(c1 + 1, c2), self.dev1(1)).wait_recv()
        self.copy(3, self.at(c1 + 1, c2, 1), self.dev1(-1)).start()
        self.second(2)

    def stage2(self):
        c1, c2 = self.c1, self.c2
        self.copy(2, self.at(c1 + 2, c2, 0), self.dev1(1)).wait_recv()
        self.copy(3, self.at(c1 + 2, c2, 1), self.dev1(1)).wait_recv()
        self.second(3)

    def stage3(self, i):
        b, c2 = self.bs[i], self.c2
        self.copy(4 + 4 * i, self.at(b, c2 - 1), self.dev2(1)).wait_recv()
        self.copy(6 + 4 * i, self.at(b, c2 - 1, 0), self.dev2(1)).start()
        self.copy(5 + 4 * i, self.at(b, c2 + 1), self.dev2(1)).wait_recv()
        self.copy(7 + 4 * i, self.at(b, c2 + 1, 1), self.dev2(-1)).start()

    def stage4(self):
        for i in range(4):
            self.copy(6 + 4 * i, self.at(self.bs[i], self.c2 + 2, 0), self.dev2(1)).wait_recv()
            self.copy(7 + 4 * i, self.at(self.bs[i], self.c2 + 2, 1), self.dev2(1)).wait_recv()

    def sent(self):
        c1, c2 = self.c1, self.c2
        for k in (0, 1):
            self.copy(k, self.at(c1, c2), self.dev1(1)).wait_send()
            self.copy(2 + k, self.at(c1, c2, k), self.dev1(1)).wait_send()
        for i in range(4):
            for k in (0, 1):
                self.copy(4 + 4 * i + k, self.at(c1, c2), self.dev1(1)).wait_send()
                self.copy(6 + 4 * i + k, self.at(c1, c2, k), self.dev1(1)).wait_send()


class Scatter:
    def __init__(self, block, c1, c2, dev1, dev2, halves, fulls, sem):
        self.block, self.c1, self.c2 = block, c1, c2
        self.dev1, self.dev2, self.sem = dev1, dev2, sem
        self.halves, self.fulls = halves, fulls
        self.bs = [wrap(c2 + 2), wrap(c2 + 1), wrap(c2 - 1), c2]

    def copy(self, k, src, dst, dev):
        return pltpu.make_async_remote_copy(
            src_ref=src, dst_ref=dst, send_sem=self.sem.at[0, k], recv_sem=self.sem.at[1, k],
            device_id=dev, device_id_type=MESH,
        )

    def at(self, a, b, half=None):
        return self.block(wrap(a), wrap(b), half)

    def add(self, ref, *others):
        total = ref[...].astype(F32)
        for other in others:
            total = total + other[...].astype(F32)
        ref[...] = total.astype(BF16)

    def start(self):
        for i in range(4):
            self.copy(4 * i, self.at(self.c1 + 2, self.bs[i], 0), self.halves.at[i, 0], self.dev1(1)).start()
            self.copy(4 * i + 1, self.at(self.c1 + 2, self.bs[i], 1), self.halves.at[i, 1], self.dev1(-1)).start()

    def got_half(self, i, k):
        ref = self.halves.at[i, k]
        self.copy(4 * i + k, ref, ref, self.dev1(1)).wait_recv()
        return ref

    def got_full(self, i, k):
        ref = self.fulls.at[i, k]
        self.copy(4 * i + 2 + k, ref, ref, self.dev1(1)).wait_recv()
        return ref

    def mid(self, i):
        b = self.bs[i]
        self.add(self.at(self.c1 + 1, b, 0), self.got_half(i, 0))
        self.copy(4 * i + 2, self.at(self.c1 + 1, b), self.fulls.at[i, 0], self.dev1(1)).start()
        self.add(self.at(self.c1 - 1, b, 1), self.got_half(i, 1))
        self.copy(4 * i + 3, self.at(self.c1 - 1, b), self.fulls.at[i, 1], self.dev1(-1)).start()

    def end(self, i):
        c1, b = self.c1, self.bs[i]
        first, second = self.got_full(i, 0), self.got_full(i, 1)
        if i == 0:
            self.add(self.at(c1, b), first, second)
            self.copy(16, self.at(c1, b, 0), self.halves.at[4, 0], self.dev2(1)).start()
            self.copy(17, self.at(c1, b, 1), self.halves.at[4, 1], self.dev2(-1)).start()
        elif i == 1:
            self.add(self.at(c1, b), first, second)
            self.add(self.at(c1, b, 0), self.got_half(4, 0))
            self.copy(18, self.at(c1, b), self.fulls.at[4, 0], self.dev2(1)).start()
        elif i == 2:
            self.add(self.at(c1, b), first, second)
            self.add(self.at(c1, b, 1), self.got_half(4, 1))
            self.copy(19, self.at(c1, b), self.fulls.at[4, 1], self.dev2(-1)).start()
        else:
            total = self.at(c1, b)[...].astype(F32) + first[...].astype(F32) + second[...].astype(F32)
            for k in (0, 1):
                total = total + self.got_full(4, k)[...].astype(F32)
            return total

    def sent(self):
        for i in range(5):
            for k in (0, 1):
                self.copy(4 * i + k, self.halves.at[i, k], self.halves.at[i, k], self.dev1(1)).wait_send()
                self.copy(4 * i + 2 + k, self.fulls.at[i, k], self.fulls.at[i, k], self.dev1(1)).wait_send()


def kernel(
    tok, ids, gate, gain, win, wout, img,
    tg, gg, dwin, dwout,
    sel, vsend, v32, v32b, full_in, full_out, img32, imgb,
    xsend, gsend, xr, gall, xs, xt, pre, cdf, act, actt, out32,
    contrib, crecv, tall, rsum, rrecv, csum, ccrecv, tb, tbrecv, lb, ob, pb,
    ggs, ggrecv, ib, ibrecv, gi, go, hi_buf, fi_buf, ho_buf, fo_buf,
    ag_i, ag_o, rs_i, rs_o, pair_sem, pair2_sem,
    s_img, s_x, s_g, s_c, s_t, s_r, s_cc, s_tb, s_lb, s_gg, s_ib,
):
    dp, ex = lax.axis_index("dp"), lax.axis_index("expert")
    xy, h = dp // 2, lax.rem(dp, 2)
    y, x = xy // R, lax.rem(xy, R)
    j = 8 * h + ex

    def z_dev(q):
        return (2 * xy + q // 8, lax.rem(q, 8))

    def p_dev(k):
        return (2 * k + h, ex)

    def x_dev(step):
        return p_dev(R * y + wrap(x + step))

    def y_dev(step):
        return p_dev(R * wrap(y + step) + x)

    def each(fn):
        def step(i, carry):
            fn(i)
            return carry

        lax.fori_loop(1, N, step, 0)

    class Exchange:
        def __init__(self, me, dev, src, dst, sem):
            self.me, self.dev, self.src, self.dst, self.sem = me, dev, src, dst, sem

        def copy(self, i, to, slot):
            return pltpu.make_async_remote_copy(
                src_ref=self.src(to), dst_ref=self.dst(slot), send_sem=self.sem.at[0, i], recv_sem=self.sem.at[1, i],
                device_id=self.dev(to), device_id_type=MESH,
            )

        def start(self):
            def go_on(i):
                self.copy(i, lax.rem(self.me + i, N), self.me).start()

            each(go_on)

        def wait(self):
            def go_on(i):
                self.copy(i, lax.rem(self.me + i, N), lax.rem(self.me + N - i, N)).wait_recv()

            each(go_on)

        def sent(self):
            def go_on(i):
                self.copy(i, lax.rem(self.me + i, N), self.me).wait_send()

            each(go_on)

    def rows(ref, k, n):
        return ref.at[pl.ds(pl.multiple_of(k * n, n), n)]

    barrier = pltpu.get_barrier_semaphore()

    def greet(i):
        pl.semaphore_signal(barrier, inc=1, device_id=z_dev(lax.rem(j + i, N)), device_id_type=MESH)
        pl.semaphore_signal(barrier, inc=1, device_id=p_dev(lax.rem(xy + i, N)), device_id_type=MESH)

    each(greet)

    rows(full_out, xy, RO)[...] = wout[...]
    source = iota((D, SP), 0)
    column = iota((D, SP), 1)
    spot = column + (column // RO) * RO
    sel[0] = hot(source == spot + RO * h)
    sel[1] = hot(source == spot + RO * (1 - h))
    mine = []
    for g in range(4):
        part = win[:, D * g : D * (g + 1)]
        mine.append(dot(part, sel[0]))
        vsend[:, SP * g : SP * (g + 1)] = dot(part, sel[1])
    image = img[...].astype(F32)
    image = image * lax.rsqrt(jnp.sum(image * image, axis=1, keepdims=True) + EPS)
    rows(img32, xy, PAIR)[...] = image.astype(BF16).astype(F32)

    pl.semaphore_wait(barrier, 2 * (N - 1))

    def out_at(buf):
        def block(xc, yc, half=None):
            row = pl.multiple_of((R * yc + xc) * RO, 32)
            if half is None:
                return buf.at[pl.ds(row, RO)]
            return buf.at[pl.ds(pl.multiple_of(row + 48 * half, 16), 48)]

        return block

    def in_at(buf):
        def block(xc, yc, half=None):
            row = pl.multiple_of((R * yc + xc) * RI, 16)
            if half is None:
                return buf.at[pl.ds(row, RI)]
            return buf.at[pl.ds(row, RI), pl.ds(D * half, D)]

        return block

    def swap(block):
        return lambda a, b, half=None: block(b, a, half)

    gather_out = Gather(out_at(full_out), x, y, x_dev, y_dev, ag_o)
    gather_in = Gather(swap(in_at(full_in)), y, x, y_dev, x_dev, ag_i)
    gather_out.start()

    other = (2 * xy + 1 - h, ex)
    pair = pltpu.make_async_remote_copy(
        src_ref=vsend, dst_ref=v32b, send_sem=pair_sem.at[0], recv_sem=pair_sem.at[1], device_id=other, device_id_type=MESH
    )
    pair.start()
    for g in range(4):
        v32[pl.ds(pl.multiple_of(24 * h, 8), 24), SP * g : SP * (g + 1)] = mine[g]

    images = Exchange(xy, p_dev, lambda q: rows(img32, xy, PAIR), lambda s: rows(img32, s, PAIR), s_img)
    images.start()

    inputs = tok[...].astype(F32)
    centred = inputs - jnp.mean(inputs, axis=1, keepdims=True)
    inverse = lax.rsqrt(jnp.mean(centred * centred, axis=1, keepdims=True) + EPS)
    normed = (centred * inverse * gain[...]).astype(BF16)
    token_sum = jnp.sum(inputs.reshape(PAIR, TEXT, D), axis=1)

    chosen = ids[...].astype(F32)
    lane = iota((TOK, TOK), 1).astype(F32)
    onehot = hot(lane == chosen)
    before = dot(hot(iota((TOK, TOK), 0) > iota((TOK, TOK), 1)), onehot)
    slot = jnp.sum(before * onehot.astype(F32), axis=1, keepdims=True)
    is_main = slot < 16.0
    is_extra = jnp.logical_and(slot >= 16.0, slot < float(CAP))
    main = hot(lane == jnp.where(is_main, 16.0 * chosen + slot, -1.0))
    extra = [hot(lane == jnp.where(is_extra, 16.0 * chosen + (4.0 * p - 16.0) + slot, -1.0)) for p in range(3)]
    jf = j.astype(F32)
    place = jnp.where(is_main, 16.0 * jf + slot, jnp.where(is_extra, 240.0 + 4.0 * jf + slot, -1.0))
    spots = hot(iota((TOK, SP), 1).astype(F32) == place)

    xsend[:, :D] = dot(main.T, normed).astype(BF16)
    tail = dot(extra[0].T, normed[:, 0:256]) + dot(extra[1].T, normed[:, 256:512]) + dot(extra[2].T, normed[:, 512:768])
    xsend[:, D:] = tail.astype(BF16)
    chosen_row = jnp.broadcast_to(chosen, (TOK, TOK)).T[: 8 * PAIR]
    row64 = iota((8 * PAIR, TOK), 0)
    lane64 = iota((8 * PAIR, TOK), 1)
    weight = jnp.where(
        jnp.logical_and(chosen_row == (row64 // PAIR).astype(F32), lane64 // TEXT == lax.rem(row64, PAIR)), gate[...], 0.0
    )
    w1 = weight.astype(BF16)
    w2, w3 = split2(weight - w1.astype(F32))
    gsend[...] = dot(w1, spots) + dot(w2, spots) + dot(w3, spots)

    send_x = Exchange(j, z_dev, lambda q: rows(xsend, lax.rem(q, 8), 16), lambda s: rows(xr, s, 16), s_x)
    send_g = Exchange(j, z_dev, lambda q: rows(gsend, lax.rem(q, 8), PAIR), lambda s: rows(gall, s, PAIR), s_g)
    send_x.start()
    send_g.start()
    rows(xr, j, 16)[...] = rows(xsend, ex, 16)[...]
    rows(gall, j, PAIR)[...] = rows(gsend, ex, PAIR)[...]

    gather_out.stage1()
    pair.wait_recv()
    v32[pl.ds(pl.multiple_of(24 * (1 - h), 8), 24), :] = v32b[...]
    rows(full_in, xy, RI)[...] = v32[...].astype(BF16)
    gather_in.start()
    gather_out.stage2()
    gather_out.stage3(0)
    gather_in.stage1()
    gather_out.stage3(1)
    gather_out.stage3(2)
    gather_in.stage2()
    gather_out.stage3(3)
    for i in range(4):
        gather_in.stage3(i)

    send_x.wait()
    send_g.wait()
    picked = [
        hot(iota((64, 256), 1) == 16 * (iota((64, 256), 0) // 4) + 4 * p + lax.rem(iota((64, 256), 0), 4)) for p in range(3)
    ]
    xs[0:256, :] = xr[:, :D]
    for p in range(3):
        xs[256:SLOTS, 256 * p : 256 * (p + 1)] = dot(picked[p], xr[:, D:]).astype(BF16)
    xs[SLOTS:, :] = jnp.zeros((SP - SLOTS, D), BF16)
    xt[...] = xs[...].T
    by_slot = gall[...].T
    gate_col = jnp.sum(by_slot, axis=1, keepdims=True)[:SLOTS]
    pair_of = hot(by_slot > 0.0)[:SLOTS]

    images.wait()
    imgb[...] = img32[...].astype(BF16)
    gather_in.stage4()

    def chunk(n, size):
        return pl.ds(pl.multiple_of(n * size, size), size)

    def forward(n, carry):
        cols = chunk(n, 256)
        value = dot(xs[0:SLOTS, :], full_in[:, cols])
        bell = 0.5 * (1.0 + lax.erf(value * (0.5**0.5)))
        pre[:, cols] = value
        cdf[:, cols] = bell
        act[0:SLOTS, cols] = (value * bell).astype(BF16)
        return carry

    lax.fori_loop(0, HALF // 256, forward, 0)
    act[SLOTS:, :] = jnp.zeros((SP - SLOTS, HALF), BF16)
    gather_out.stage4()

    def project(n, carry):
        cols = chunk(n, 256)
        out32[:, cols] = dot(act[0:SLOTS, :], full_out[:, cols])
        return carry

    lax.fori_loop(0, D // 256, project, 0)

    contrib[...] = dot(pair_of, (gate_col * out32[...]).astype(BF16), 0, 0)
    send_c = Exchange(j, z_dev, lambda q: rows(contrib, q, PAIR), lambda s: crecv.at[s], s_c)
    send_c.start()
    crecv[pl.ds(j, 1)] = rows(contrib, j, PAIR)[...].reshape(1, PAIR, D)

    def slope(n, carry):
        cols = chunk(n, 256)
        value = pre[:, cols]
        pre[:, cols] = cdf[:, cols] + value * (jnp.exp(-0.5 * value * value) * 0.3989422804014327)
        return carry

    lax.fori_loop(0, HALF // 256, slope, 0)

    send_c.wait()
    pooled = (token_sum + jnp.sum(crecv[...], axis=0)) * (1.0 / TEXT)
    q_inv = lax.rsqrt(jnp.sum(pooled * pooled, axis=1, keepdims=True) + EPS)
    unit = pooled * q_inv
    rows(tall, j, PAIR)[...] = unit.astype(BF16).astype(F32)
    send_t = Exchange(j, z_dev, lambda q: rows(tall, j, PAIR), lambda s: rows(tall, s, PAIR), s_t)
    send_t.start()
    actt[...] = act[...].T
    send_t.wait()

    scores = SCALE * dot(tall[...].astype(BF16), imgb[...], 1, 1)
    exped = jnp.exp(scores)
    csum[...] = jnp.broadcast_to(jnp.sum(exped, axis=0, keepdims=True), (8, TOK))
    rsum[...] = jnp.broadcast_to(jnp.sum(exped.T, axis=0, keepdims=True), (8, TOK))
    send_r = Exchange(j, z_dev, lambda q: rsum, lambda s: rrecv.at[s], s_r)
    send_cc = Exchange(xy, p_dev, lambda q: csum, lambda s: ccrecv.at[s], s_cc)
    send_r.start()
    send_cc.start()
    rrecv[pl.ds(j, 1)] = rsum[...].reshape(1, 8, TOK)
    ccrecv[pl.ds(xy, 1)] = csum[...].reshape(1, 8, TOK)
    text_at = iota((TOK, TOK), 0)
    image_at = iota((TOK, TOK), 1)
    diagonal = jnp.where(
        jnp.logical_and(image_at // PAIR == xy, text_at == PAIR * j + lax.rem(image_at, PAIR)), 1.0, 0.0
    )
    send_r.wait()
    send_cc.wait()
    row_total = jnp.broadcast_to(jnp.sum(rrecv[...], axis=0)[0:1], (TOK, TOK)).T
    col_total = jnp.sum(ccrecv[...], axis=0)[0:1]
    coefs = (0.5 * (exped / row_total + exped / col_total) - diagonal).astype(BF16)
    tb[...] = SCALE * dot(coefs, imgb[...])
    send_tb = Exchange(j, z_dev, lambda q: rows(tb, q, PAIR), lambda s: tbrecv.at[s], s_tb)
    send_tb.start()
    tbrecv[pl.ds(j, 1)] = rows(tb, j, PAIR)[...].reshape(1, PAIR, D)
    send_tb.wait()
    text_back = jnp.sum(tbrecv[...], axis=0)
    pooled_back = q_inv * (text_back - unit * jnp.sum(unit * text_back, axis=1, keepdims=True))
    layer_back = pooled_back * (1.0 / TEXT)
    rows(lb, j, PAIR)[...] = layer_back
    send_lb = Exchange(j, z_dev, lambda q: rows(lb, j, PAIR), lambda s: rows(lb, s, PAIR), s_lb)
    send_lb.start()
    send_lb.wait()

    lb_hi, lb_lo = split2(lb[...])
    slot_back = dot(pair_of, lb_hi) + dot(pair_of, lb_lo)
    ob[0:SLOTS, :] = (gate_col * slot_back).astype(BF16)
    ob[SLOTS:, :] = jnp.zeros((SP - SLOTS, D), BF16)
    pb[SLOTS:, :] = jnp.zeros((SP - SLOTS, HALF), BF16)

    def grad_out(n, carry):
        go[chunk(n, 256), :] = dot(actt[chunk(n, 256), :], ob[...]).astype(BF16)
        return carry

    lax.fori_loop(0, HALF // 256, grad_out, 0)
    scatter_out = Scatter(swap(out_at(go)), y, x, y_dev, x_dev, ho_buf, fo_buf, rs_o)
    scatter_out.start()

    def back(n, carry):
        cols = chunk(n, 256)
        act_back = dot(ob[0:SLOTS, :], full_out[cols, :], 1, 1)
        pb[0:SLOTS, cols] = (act_back * pre[:, cols]).astype(BF16)
        return carry

    lax.fori_loop(0, HALF // 256, back, 0)

    def grad_in(n, carry):
        cols = chunk(n, 256)
        gi[:, cols] = dot(xt[...], pb[:, cols]).astype(BF16)
        return carry

    lax.fori_loop(0, HALF // 256, grad_in, 0)
    scatter_in = Scatter(in_at(gi), x, y, x_dev, y_dev, hi_buf, fi_buf, rs_i)
    scatter_in.start()
    scatter_out.mid(0)

    gate_back = jnp.sum(slot_back * out32[...], axis=1, keepdims=True)
    gate_back = jnp.concatenate(
        [jnp.broadcast_to(gate_back, (SLOTS, TOK)), jnp.zeros((SP - SLOTS, TOK), F32)], axis=0
    )
    ggs[...] = gate_back.T[0:8]
    scatter_out.mid(1)

    spread = jnp.zeros((256, 256), F32)
    for p in range(3):
        cols = slice(256 * p, 256 * (p + 1))
        in_back = dot(pb[0:SLOTS, :], full_in[cols, :], 1, 1).astype(BF16)
        ib[:, cols] = in_back[0:256]
        spread = spread + dot(picked[p], in_back[256:SLOTS], 0, 0)
    ib[:, D:] = spread.astype(BF16)
    send_ib = Exchange(j, z_dev, lambda q: rows(ib, q, 16), lambda s: rows(ibrecv, s, 16), s_ib)
    send_gg = Exchange(j, z_dev, lambda q: ggs, lambda s: rows(ggrecv, s, 8), s_gg)
    send_ib.start()
    send_gg.start()
    rows(ibrecv, j, 16)[...] = rows(ib, j, 16)[...]
    rows(ggrecv, j, 8)[...] = ggs[...]

    scatter_in.mid(0)
    scatter_out.mid(2)
    scatter_in.mid(1)
    scatter_out.mid(3)
    scatter_in.mid(2)
    scatter_in.mid(3)
    scatter_out.end(0)
    scatter_in.end(0)
    scatter_out.end(1)
    scatter_in.end(1)
    scatter_out.end(2)
    scatter_in.end(2)

    send_ib.wait()
    send_gg.wait()
    inputs = tok[...].astype(F32)
    centred = inputs - jnp.mean(inputs, axis=1, keepdims=True)
    inverse = lax.rsqrt(jnp.mean(centred * centred, axis=1, keepdims=True) + EPS)
    scaled = centred * inverse
    back_main = dot(jnp.concatenate([main, main], axis=1), ibrecv[:, :D])
    back_tail = [dot(jnp.concatenate([e, e], axis=1), ibrecv[:, D:]) for e in extra]
    normed_back = back_main + jnp.concatenate(back_tail, axis=1)
    gained = normed_back * gain[...]
    repeated = jnp.broadcast_to(layer_back.reshape(PAIR, 1, D), (PAIR, TEXT, D)).reshape(TOK, D)
    tg[...] = (
        repeated
        + inverse * (gained - jnp.mean(gained, axis=1, keepdims=True) - scaled * jnp.mean(gained * scaled, axis=1, keepdims=True))
    ).astype(BF16)
    lane_i = iota((TOK, TOK), 1)
    owner = hot(
        jnp.logical_and(lax.rem(lane_i, 8) == 0, lax.rem(lane_i // 8, 8).astype(F32) == chosen)
    )
    got = ggrecv[...]
    g1 = got.astype(BF16)
    g2, g3 = split2(got - g1.astype(F32))
    gathered = dot(owner, g1) + dot(owner, g2) + dot(owner, g3)
    token_gate = jnp.sum(gathered * spots.astype(F32), axis=1, keepdims=True)
    gg[...] = jnp.broadcast_to(token_gate, (TOK, TOK)).T[0:1]

    vsum = scatter_in.end(3)
    v32[...] = vsum
    back_pair = pltpu.make_async_remote_copy(
        src_ref=v32.at[pl.ds(pl.multiple_of(24 * (1 - h), 8), 24)], dst_ref=v32b,
        send_sem=pair2_sem.at[0], recv_sem=pair2_sem.at[1], device_id=other, device_id_type=MESH,
    )
    back_pair.start()
    dwout[...] = scatter_out.end(3)
    kept = v32[pl.ds(pl.multiple_of(24 * h, 8), 24), :]
    held = []
    for g in range(4):
        hi, lo = split2(kept[:, SP * g : SP * (g + 1)])
        held.append(dot(hi, sel[0], 1, 1) + dot(lo, sel[0], 1, 1))
    back_pair.wait_recv()
    came = v32b[...]
    for g in range(4):
        hi, lo = split2(came[:, SP * g : SP * (g + 1)])
        dwin[:, D * g : D * (g + 1)] = held[g] + dot(hi, sel[1], 1, 1) + dot(lo, sel[1], 1, 1)

    pair.wait_send()
    back_pair.wait_send()
    gather_out.sent()
    gather_in.sent()
    scatter_out.sent()
    scatter_in.sent()
    for exchange in (images, send_x, send_g, send_c, send_t, send_r, send_cc, send_tb, send_lb, send_gg, send_ib):
        exchange.sent()


def body(tokens, expert_ids, gate, ln_gain, w_in, w_out, image_emb):
    vmem = pl.BlockSpec(memory_space=pltpu.VMEM)
    f32 = lambda *shape: pltpu.VMEM(shape, F32)
    b16 = lambda *shape: pltpu.VMEM(shape, BF16)
    sems = lambda *shape: pltpu.SemaphoreType.DMA(shape)
    token_grad, gate_grad, in_grad, out_grad = pl.pallas_call(
        kernel,
        out_shape=(
            jax.ShapeDtypeStruct((TOK, D), BF16),
            jax.ShapeDtypeStruct((1, TOK), F32),
            jax.ShapeDtypeStruct((24, H), F32),
            jax.ShapeDtypeStruct((RO, D), F32),
        ),
        in_specs=[vmem] * 7,
        out_specs=(vmem,) * 4,
        scratch_shapes=[
            b16(2, D, SP),
            f32(24, HALF),
            f32(RI, HALF),
            f32(24, HALF),
            b16(D, HALF),
            b16(HALF, D),
            f32(TOK, D),
            b16(TOK, D),
            b16(TOK, 1024),
            f32(64, SP),
            b16(256, 1024),
            f32(TOK, SP),
            b16(SP, D),
            b16(D, SP),
            f32(SLOTS, HALF),
            f32(SLOTS, HALF),
            b16(SP, HALF),
            b16(HALF, SP),
            f32(SLOTS, D),
            f32(TOK, D),
            f32(N, PAIR, D),
            f32(TOK, D),
            f32(8, TOK),
            f32(N, 8, TOK),
            f32(8, TOK),
            f32(N, 8, TOK),
            f32(TOK, D),
            f32(N, PAIR, D),
            f32(TOK, D),
            b16(SP, D),
            b16(SP, HALF),
            f32(8, SP),
            f32(TOK, SP),
            b16(256, 1024),
            b16(256, 1024),
            b16(D, HALF),
            b16(HALF, D),
            b16(5, 2, RI, D),
            b16(5, 2, RI, HALF),
            b16(5, 2, 48, D),
            b16(5, 2, RO, D),
            sems(2, 20),
            sems(2, 20),
            sems(2, 20),
            sems(2, 20),
            sems(2),
            sems(2),
        ]
        + [sems(2, N)] * 11,
        compiler_params=pltpu.CompilerParams(
            collective_id=0, has_side_effects=True, vmem_limit_bytes=56 * 1024 * 1024
        ),
        cost_estimate=pl.CostEstimate(flops=5_000_000_000, bytes_accessed=2_000_000, transcendentals=1_000_000),
    )(tokens, expert_ids, gate.reshape(1, TOK), ln_gain.reshape(1, D), w_in[0], w_out[0], image_emb)
    return token_grad, gate_grad.reshape(TOK), in_grad[None], out_grad[None]


def solution(mesh):
    in_specs = (
        P(("dp", "expert"), None),
        P(("dp", "expert"), None),
        P(("dp", "expert")),
        P(),
        P("expert", "dp", None),
        P("expert", "dp", None),
        P(("dp", "expert"), None),
    )
    out_specs = (
        P(("dp", "expert"), None),
        P(("dp", "expert")),
        P("expert", "dp", None),
        P("expert", "dp", None),
    )
    return jax.shard_map(body, mesh=mesh, in_specs=in_specs, out_specs=out_specs, check_vma=False)
```

```python
import jax
import jax.numpy as jnp
from jax import lax
from jax.experimental import pallas as pl
from jax.experimental.pallas import tpu as pltpu
from jax.sharding import PartitionSpec as P

MESH = pl.DeviceIdType.MESH
F32 = jnp.float32
BF16 = jnp.bfloat16

D = 768
H = 3072
HALF = 1536
TOK = 128
CAP = 20
PAIR = 8
TEXT = 16
N = 16
R = 4
RO = 96
RI = 48
SLOTS = 320
SP = 384
EPS = 1e-6
SCALE = 100.0


def dot(a, b, ca=1, cb=0):
    return lax.dot_general(a, b, (((ca,), (cb,)), ((), ())), preferred_element_type=F32)


def iota(shape, axis):
    return lax.broadcasted_iota(jnp.int32, shape, axis)


def hot(mask):
    return jnp.where(mask, 1.0, 0.0).astype(BF16)


def split2(v):
    hi = v.astype(BF16)
    return hi, (v - hi.astype(F32)).astype(BF16)


def fold(v):
    m = v.shape[0] // 8
    v = v.reshape(m, 8, D)
    return jnp.concatenate([v[:, :, : D // 2], v[:, :, D // 2 :]], axis=1).reshape(16 * m, D // 2).astype(BF16)


def unfold(v):
    m = v.shape[0] // 16
    v = v.astype(F32).reshape(m, 16, D // 2)
    return jnp.concatenate([v[:, :8], v[:, 8:]], axis=2).reshape(8 * m, D)


def stack(v):
    return jnp.concatenate([v[:, :D], v[:, D:]], axis=0).astype(BF16)


def unstack(v):
    v = v.astype(F32)
    return jnp.concatenate([v[:24], v[24:]], axis=1)


def wrap(v):
    return lax.rem(v + 2 * R, R)


class Gather:
    def __init__(self, block, c1, c2, dev1, dev2, four, fifteen, sem, g):
        self.block, self.c1, self.c2 = block, c1, c2
        self.dev1, self.dev2, self.sem, self.g = dev1, dev2, sem, g
        self.four, self.fifteen = four, fifteen
        self.bs = [c1, wrap(c1 - 1), wrap(c1 + 1), wrap(c1 + 2)]

    def copy(self, k, ref, dev):
        return pltpu.make_async_remote_copy(
            src_ref=ref, dst_ref=ref, send_sem=self.sem.at[self.g, 12], recv_sem=self.sem.at[self.g, k],
            device_id=dev, device_id_type=MESH,
        )

    def got(self, k, ref):
        self.copy(k, ref, self.dev1(1)).wait_recv()
        return ref

    def at(self, a, b, half=None):
        return self.block(wrap(a), wrap(b), half)

    def second(self, i):
        ref = self.at(self.bs[i], self.c2)
        self.copy(3 + 2 * i, ref, self.dev2(1)).start()
        self.copy(4 + 2 * i, ref, self.dev2(-1)).start()

    def start(self):
        ref = self.at(self.c1, self.c2)
        self.copy(0, ref, self.dev1(1)).start()
        self.copy(1, ref, self.dev1(-1)).start()

    def stage1(self):
        c1, c2 = self.c1, self.c2
        self.got(0, self.at(c1 - 1, c2))
        self.copy(2, self.at(c1 - 1, c2, 0), self.dev1(1)).start()
        self.second(1)
        self.got(1, self.at(c1 + 1, c2))
        self.copy(2, self.at(c1 + 1, c2, 1), self.dev1(-1)).start()
        self.second(2)

    def stage2(self):
        self.got(2, self.at(self.c1 + 2, self.c2))
        self.second(3)

    def stage3(self, i):
        b, c2 = self.bs[i], self.c2
        self.got(3 + 2 * i, self.at(b, c2 - 1))
        self.copy(11, self.at(b, c2 - 1, 0), self.dev2(1)).start()
        self.got(4 + 2 * i, self.at(b, c2 + 1))
        self.copy(11, self.at(b, c2 + 1, 1), self.dev2(-1)).start()

    def stage4(self):
        self.got(11, self.four)

    def sent(self):
        self.copy(12, self.fifteen, self.dev1(1)).wait_send()


class Scatter:
    def __init__(self, block, c1, c2, dev1, dev2, halves, fulls, fifteen, sem, g):
        self.block, self.c1, self.c2 = block, c1, c2
        self.dev1, self.dev2, self.sem, self.g = dev1, dev2, sem, g
        self.halves, self.fulls, self.fifteen = halves.at[g], fulls.at[g], fifteen
        self.bs = [wrap(c2 + 2), wrap(c2 + 1), wrap(c2 - 1), c2]

    def copy(self, k, src, dst, dev):
        return pltpu.make_async_remote_copy(
            src_ref=src, dst_ref=dst, send_sem=self.sem.at[self.g, 15], recv_sem=self.sem.at[self.g, k],
            device_id=dev, device_id_type=MESH,
        )

    def got(self, k, ref):
        self.copy(k, ref, ref, self.dev1(1)).wait_recv()
        return ref

    def at(self, a, b, half=None):
        return self.block(wrap(a), wrap(b), half)

    def add(self, ref, *others):
        total = ref[...].astype(F32)
        for other in others:
            total = total + other[...].astype(F32)
        ref[...] = total.astype(BF16)

    def start(self):
        for i in range(4):
            self.copy(2 * i, self.at(self.c1 + 2, self.bs[i], 0), self.halves.at[i, 0], self.dev1(1)).start()
            self.copy(2 * i + 1, self.at(self.c1 + 2, self.bs[i], 1), self.halves.at[i, 1], self.dev1(-1)).start()

    def mid(self, i):
        b = self.bs[i]
        self.add(self.at(self.c1 + 1, b, 0), self.got(2 * i, self.halves.at[i, 0]))
        self.copy(8 + i, self.at(self.c1 + 1, b), self.fulls.at[i, 0], self.dev1(1)).start()
        self.add(self.at(self.c1 - 1, b, 1), self.got(2 * i + 1, self.halves.at[i, 1]))
        self.copy(8 + i, self.at(self.c1 - 1, b), self.fulls.at[i, 1], self.dev1(-1)).start()

    def end(self, i):
        c1, b = self.c1, self.bs[i]
        self.got(8 + i, self.fulls.at[i])
        first, second = self.fulls.at[i, 0], self.fulls.at[i, 1]
        if i == 0:
            self.add(self.at(c1, b), first, second)
            self.copy(12, self.at(c1, b, 0), self.halves.at[4, 0], self.dev2(1)).start()
            self.copy(13, self.at(c1, b, 1), self.halves.at[4, 1], self.dev2(-1)).start()
        elif i == 1:
            self.add(self.at(c1, b), first, second)
            self.add(self.at(c1, b, 0), self.got(12, self.halves.at[4, 0]))
            self.copy(14, self.at(c1, b), self.fulls.at[4, 0], self.dev2(1)).start()
        elif i == 2:
            self.add(self.at(c1, b), first, second)
            self.add(self.at(c1, b, 1), self.got(13, self.halves.at[4, 1]))
            self.copy(14, self.at(c1, b), self.fulls.at[4, 1], self.dev2(-1)).start()
        else:
            total = self.at(c1, b)[...].astype(F32) + first[...].astype(F32) + second[...].astype(F32)
            self.got(14, self.fulls.at[4])
            for k in (0, 1):
                total = total + self.fulls[4, k].astype(F32)
            return total

    def sent(self):
        self.copy(15, self.fifteen, self.fifteen, self.dev1(1)).wait_send()


def kernel(
    tok, ids, gate, gain, win, wout, img,
    tg, gg, dwin, dwout,
    sel, vsend, v32, vcame, vback, vfinal, full_in, full_out, imgs, imgb,
    xsend, xr, xs, xt, pre, cdf, act, actt, out32,
    contrib, cjoin, csend, crecv, tall, rsum, rrecv, csum, ccrecv, tb, tbrecv, lb, ob, pb,
    ib, ibrecv, gi, go, halves, fulls,
    ag_sem, rs_sem, pair_sem, pair2_sem,
    s_img, s_x, s_c, s_t, s_r, s_cc, s_tb, s_lb, s_ib, s_join, s_share,
):
    dp, ex = lax.axis_index("dp"), lax.axis_index("expert")
    xy, h = dp // 2, lax.rem(dp, 2)
    y, x = xy // R, lax.rem(xy, R)
    j = 8 * h + ex

    def z_dev(q):
        return (2 * xy + q // 8, lax.rem(q, 8))

    def p_dev(k):
        return (2 * k + h, ex)

    chip, core = 4 * h + ex // 2, lax.rem(ex, 2)
    seat = 8 * core + chip

    def c_dev(k):
        return (2 * xy + k // 4, 2 * lax.rem(k, 4) + core)

    twin = (dp, ex + 1 - 2 * core)

    def x_dev(step):
        return p_dev(R * y + wrap(x + step))

    def y_dev(step):
        return p_dev(R * wrap(y + step) + x)

    def each(fn):
        def step(i, carry):
            fn(i)
            return carry

        lax.fori_loop(1, N, step, 0)

    class Exchange:
        def __init__(self, me, dev, src, dst, all_but_one, sem, size=N):
            self.me, self.dev, self.src, self.dst, self.sem = me, dev, src, dst, sem
            self.all_but_one, self.size = all_but_one, size

        def copy(self, src, dst, to):
            return pltpu.make_async_remote_copy(
                src_ref=src, dst_ref=dst, send_sem=self.sem.at[0], recv_sem=self.sem.at[1],
                device_id=self.dev(to), device_id_type=MESH,
            )

        def start(self):
            def step(i, carry):
                to = lax.rem(self.me + i, self.size)
                self.copy(self.src(to), self.dst(self.me), to).start()
                return carry

            lax.fori_loop(1, self.size, step, 0)

        def wait(self):
            self.copy(self.all_but_one, self.all_but_one, lax.rem(self.me + 1, self.size)).wait_recv()

        def sent(self):
            self.copy(self.all_but_one, self.all_but_one, lax.rem(self.me + 1, self.size)).wait_send()

    def rows(ref, k, n):
        return ref.at[pl.ds(pl.multiple_of(k * n, n), n)]

    barrier = pltpu.get_barrier_semaphore()

    def greet(i):
        pl.semaphore_signal(barrier, inc=1, device_id=z_dev(lax.rem(j + i, N)), device_id_type=MESH)
        pl.semaphore_signal(barrier, inc=1, device_id=p_dev(lax.rem(xy + i, N)), device_id_type=MESH)

    each(greet)

    rows(full_out, xy, RO)[...] = wout[...]
    source = iota((D, SP), 0)
    column = iota((D, SP), 1)
    spot = column + (column // RO) * RO
    sel[0] = hot(source == spot + RO * h)
    sel[1] = hot(source == spot + RO * (1 - h))
    mine, theirs = [], []
    for g in range(4):
        part = win[:, D * g : D * (g + 1)]
        mine.append(dot(part, sel[0]))
        theirs.append(dot(part, sel[1]))
    vsend[...] = stack(jnp.concatenate(theirs, axis=1))
    for g in range(4):
        v32[pl.ds(pl.multiple_of(24 * h, 8), 24), SP * g : SP * (g + 1)] = mine[g]
    image = img[...].astype(F32)
    image = image * lax.rsqrt(jnp.sum(image * image, axis=1, keepdims=True) + EPS)
    rows(imgs, j, 16)[...] = fold(image)

    inputs = tok[...].astype(F32)
    centred = inputs - jnp.mean(inputs, axis=1, keepdims=True)
    inverse = lax.rsqrt(jnp.mean(centred * centred, axis=1, keepdims=True) + EPS)
    normed = (centred * inverse * gain[...].reshape(1, D)).astype(BF16)
    token_sum = jnp.sum(inputs.reshape(PAIR, TEXT, D), axis=1)

    chosen_row = jnp.broadcast_to(ids[...].astype(F32), (TOK, TOK))
    chosen = chosen_row.T[:, 0:1]
    lane = iota((TOK, TOK), 1).astype(F32)
    onehot = hot(lane == chosen)
    before = dot(hot(iota((TOK, TOK), 0) > iota((TOK, TOK), 1)), onehot)
    slot = jnp.sum(before * onehot.astype(F32), axis=1, keepdims=True)
    is_main = slot < 16.0
    is_extra = jnp.logical_and(slot >= 16.0, slot < float(CAP))
    main = hot(lane == jnp.where(is_main, 16.0 * chosen + slot, -1.0))
    extra = [hot(lane == jnp.where(is_extra, 16.0 * chosen + (4.0 * p - 16.0) + slot, -1.0)) for p in range(3)]
    at_slot = iota((TOK, 256), 1).astype(F32) == jnp.where(slot < float(CAP), slot, -1.0)

    xsend[:, :D] = dot(main.T, normed).astype(BF16)
    tail = dot(extra[0].T, normed[:, 0:256]) + dot(extra[1].T, normed[:, 256:512]) + dot(extra[2].T, normed[:, 512:768])
    gate_row = gate[...]
    gate1 = gate_row.astype(BF16).astype(F32)
    gate2 = (gate_row - gate1).astype(BF16).astype(F32)
    gate3 = gate_row - gate1 - gate2
    line = iota((TOK, TOK), 0)
    kind = lax.rem(line, 16)
    pair_row = (iota((TOK, TOK), 1) // TEXT).astype(F32)
    notes = jnp.where(kind == 12, gate1, jnp.where(kind == 13, gate2, jnp.where(kind == 14, gate3, jnp.where(kind == 15, pair_row, 0.0))))
    notes = jnp.where((line // 16).astype(F32) == chosen_row, notes, 0.0)
    xsend[:, D:] = (tail + dot(notes.astype(BF16), hot(at_slot))).astype(BF16)
    rows(xr, j, 16)[...] = rows(xsend, ex, 16)[...]

    pl.semaphore_wait(barrier, 2 * (N - 1))

    def out_at(buf, part):
        def block(xc, yc, half=None):
            row = pl.multiple_of((R * yc + xc) * RO + 48 * part, 16)
            if half is None:
                return buf.at[pl.ds(row, 48)]
            return buf.at[pl.ds(row, 48), pl.ds(SP * half, SP)]

        return block

    def in_at(buf, part):
        def block(xc, yc, half=None):
            row = pl.multiple_of((R * yc + xc) * RI, 16)
            if half is None:
                return buf.at[pl.ds(row, RI), pl.ds(D * part, D)]
            return buf.at[pl.ds(row, RI), pl.ds(D * part + SP * half, SP)]

        return block

    def both(make, buf, at, first, *args):
        other_way = at(buf, 1)
        return (
            make(at(buf, 0), x, y, x_dev, y_dev, *args, first),
            make(lambda a, b, half=None: other_way(b, a, half), y, x, y_dev, x_dev, *args, first + 1),
        )

    fifteen = full_out.at[pl.ds(0, 15 * 48)]
    outs = both(Gather, full_out, out_at, 0, full_out.at[pl.ds(0, 192)], fifteen, ag_sem)
    ins = both(Gather, full_in, in_at, 2, full_in.at[pl.ds(0, 96)], fifteen, ag_sem)

    other = (2 * xy + 1 - h, ex)
    pair = pltpu.make_async_remote_copy(
        src_ref=vsend, dst_ref=vcame, send_sem=pair_sem.at[0], recv_sem=pair_sem.at[1], device_id=other, device_id_type=MESH
    )
    pair.start()
    for part in outs:
        part.start()
    for part in outs:
        part.second(0)

    images = Exchange(j, z_dev, lambda q: rows(imgs, j, 16), lambda s: rows(imgs, s, 16), imgs.at[pl.ds(0, 240)], s_img)
    images.start()

    send_x = Exchange(j, z_dev, lambda q: rows(xsend, lax.rem(q, 8), 16), lambda s: rows(xr, s, 16), xr.at[pl.ds(0, 240)], s_x)
    send_x.start()

    for part in outs:
        part.stage1()
    for part in outs:
        part.stage2()
    for part in outs:
        part.stage3(0)
    pair.wait_recv()
    v32[pl.ds(pl.multiple_of(24 * (1 - h), 8), 24), :] = unstack(vcame[...])
    rows(full_in, xy, RI)[...] = v32[...].astype(BF16)
    for part in ins:
        part.start()
    for part in ins:
        part.second(0)
    for i in (1, 2):
        for part in outs:
            part.stage3(i)
    for part in ins:
        part.stage1()
    for part in outs:
        part.stage3(3)
    for part in ins:
        part.stage2()
    for i in range(4):
        for part in ins:
            part.stage3(i)

    send_x.wait()
    row64 = iota((64, 256), 0)
    lane64 = iota((64, 256), 1)
    picked = [hot(lane64 == 16 * (row64 // 4) + 4 * p + lax.rem(row64, 4)) for p in range(3)]
    xs[0:256, :] = xr[:, :D]
    for p in range(3):
        xs[256:SLOTS, 256 * p : 256 * (p + 1)] = dot(picked[p], xr[:, D:]).astype(BF16)
    xs[SLOTS:, :] = jnp.zeros((SP - SLOTS, D), BF16)
    xt[...] = xs[...].T
    slot_i = iota((SLOTS, 256), 0)
    lane_i = iota((SLOTS, 256), 1)
    slot_from = jnp.where(slot_i < 256, slot_i // 16, (slot_i - 256) // 4)
    slot_at = jnp.where(slot_i < 256, lax.rem(slot_i, 16), 16 + lax.rem(slot_i, 4))
    note_of = [hot(lane_i == 16 * slot_from + 12 + m) for m in range(4)]
    tails = xr[:, D:]
    own_lane = lane_i == slot_at
    gate_col = jnp.sum(jnp.where(own_lane, dot(note_of[0] + note_of[1] + note_of[2], tails), 0.0), axis=1, keepdims=True)
    pair_col = jnp.sum(jnp.where(own_lane, dot(note_of[3], tails), 0.0), axis=1, keepdims=True)
    first_pair = (PAIR * (8 * lax.rem(slot_from, 2) + slot_from // 2))[:, :TOK].astype(F32)
    pair_of = hot(lane_i[:, :TOK].astype(F32) == first_pair + pair_col)

    images.wait()
    imgb[...] = unfold(imgs[...]).astype(BF16)
    for part in ins:
        part.stage4()

    def chunk(n, size):
        return pl.ds(pl.multiple_of(n * size, size), size)

    def forward(n, carry):
        cols = chunk(n, 256)
        value = dot(xs[0:SLOTS, :], full_in[:, cols])
        bell = 0.5 * (1.0 + lax.erf(value * (0.5**0.5)))
        pre[:, cols] = value
        cdf[:, cols] = bell
        act[0:SLOTS, cols] = (value * bell).astype(BF16)
        return carry

    lax.fori_loop(0, HALF // 256, forward, 0)
    act[SLOTS:, :] = jnp.zeros((SP - SLOTS, HALF), BF16)
    for part in outs:
        part.stage4()

    def project(n, carry):
        cols = chunk(n, 256)
        out32[:, cols] = dot(act[0:SLOTS, :], full_out[:, cols])
        return carry

    lax.fori_loop(0, D // 256, project, 0)

    contrib[...] = fold(dot(pair_of, (gate_col * out32[...]).astype(BF16), 0, 0))
    join = pltpu.make_async_remote_copy(
        src_ref=rows(contrib, 1 - core, 128), dst_ref=cjoin, send_sem=s_join.at[0], recv_sem=s_join.at[1],
        device_id=twin, device_id_type=MESH,
    )
    join.start()
    join.wait_recv()
    joined = rows(contrib, core, 128)
    csend[...] = (joined[...].astype(F32) + cjoin[...].astype(F32)).astype(BF16)
    send_c = Exchange(
        chip, c_dev, lambda q: rows(csend, q, 16), lambda s: rows(crecv, s, 16), crecv.at[pl.ds(0, 112)], s_c, 8
    )
    send_c.start()
    rows(crecv, chip, 16)[...] = rows(csend, chip, 16)[...]

    def slope(n, carry):
        cols = chunk(n, 256)
        value = pre[:, cols]
        pre[:, cols] = cdf[:, cols] + value * (jnp.exp(-0.5 * value * value) * 0.3989422804014327)
        return carry

    lax.fori_loop(0, HALF // 256, slope, 0)

    send_c.wait()
    pooled = (token_sum + jnp.sum(unfold(crecv[...]).reshape(8, PAIR, D), axis=0)) * (1.0 / TEXT)
    q_inv = lax.rsqrt(jnp.sum(pooled * pooled, axis=1, keepdims=True) + EPS)
    unit = pooled * q_inv
    rows(tall, xy, 16)[...] = fold(unit)
    send_t = Exchange(xy, p_dev, lambda q: rows(tall, xy, 16), lambda s: rows(tall, s, 16), tall.at[pl.ds(0, 240)], s_t)
    send_t.start()
    actt[...] = act[...].T
    send_t.wait()

    scores = SCALE * dot(unfold(tall[...]).astype(BF16), imgb[...], 1, 1)
    exped = jnp.exp(scores)
    csum[...] = jnp.sum(exped, axis=0, keepdims=True)
    rsum[...] = jnp.sum(exped.T, axis=0, keepdims=True)
    send_r = Exchange(xy, p_dev, lambda q: rsum, lambda s: rrecv.at[s], rrecv.at[pl.ds(0, N - 1)], s_r)
    send_cc = Exchange(j, z_dev, lambda q: csum, lambda s: ccrecv.at[s], ccrecv.at[pl.ds(0, N - 1)], s_cc)
    send_r.start()
    send_cc.start()
    rrecv[pl.ds(xy, 1)] = rsum[...].reshape(1, 1, TOK)
    ccrecv[pl.ds(j, 1)] = csum[...].reshape(1, 1, TOK)
    text_at = iota((TOK, TOK), 0)
    image_at = iota((TOK, TOK), 1)
    diagonal = jnp.where(
        jnp.logical_and(image_at // PAIR == j, text_at == PAIR * xy + lax.rem(image_at, PAIR)), 1.0, 0.0
    )
    send_r.wait()
    send_cc.wait()
    row_total = jnp.broadcast_to(jnp.sum(rrecv[...], axis=0), (TOK, TOK)).T
    col_total = jnp.sum(ccrecv[...], axis=0)
    coefs = (0.5 * (exped / row_total + exped / col_total) - diagonal).astype(BF16)
    tb[...] = fold(SCALE * dot(coefs, imgb[...]))
    send_tb = Exchange(xy, p_dev, lambda q: rows(tb, q, 16), lambda s: rows(tbrecv, s, 16), tbrecv.at[pl.ds(0, 240)], s_tb)
    send_tb.start()
    rows(tbrecv, xy, 16)[...] = rows(tb, xy, 16)[...]
    send_tb.wait()
    text_back = jnp.sum(unfold(tbrecv[...]).reshape(N, PAIR, D), axis=0)
    pooled_back = q_inv * (text_back - unit * jnp.sum(unit * text_back, axis=1, keepdims=True))
    layer_back = pooled_back * (1.0 / TEXT)
    rows(lb, seat, 16)[...] = fold(layer_back)
    send_lb = Exchange(
        chip, c_dev, lambda q: rows(lb, seat, 16), lambda s: rows(lb, 8 * core + s, 16), lb.at[pl.ds(0, 112)], s_lb, 8
    )
    send_lb.start()
    send_lb.wait()
    ours = rows(lb, core, 128)
    share = pltpu.make_async_remote_copy(
        src_ref=ours, dst_ref=ours, send_sem=s_share.at[0], recv_sem=s_share.at[1], device_id=twin, device_id_type=MESH
    )
    share.start()
    share.wait_recv()

    slot_back = dot(pair_of, unfold(lb[...]).astype(BF16))
    ob[0:SLOTS, :] = (gate_col * slot_back).astype(BF16)
    ob[SLOTS:, :] = jnp.zeros((SP - SLOTS, D), BF16)
    pb[SLOTS:, :] = jnp.zeros((SP - SLOTS, HALF), BF16)

    def back(n, carry):
        cols = chunk(n, 256)
        act_back = dot(ob[0:SLOTS, :], full_out[cols, :], 1, 1)
        pb[0:SLOTS, cols] = (act_back * pre[:, cols]).astype(BF16)
        return carry

    def grad_in(n, carry):
        cols = chunk(n, 256)
        gi[:, cols] = dot(xt[...], pb[:, cols]).astype(BF16)
        return carry

    def grad_out(n, carry):
        go[chunk(n, 256), :] = dot(actt[chunk(n, 256), :], ob[...]).astype(BF16)
        return carry

    s_ins = both(Scatter, gi, in_at, 0, halves, fulls, fifteen, rs_sem)
    s_outs = both(Scatter, go, out_at, 2, halves, fulls, fifteen, rs_sem)
    for k in (0, 1):
        lax.fori_loop(3 * k, 3 * k + 3, back, 0)
        lax.fori_loop(3 * k, 3 * k + 3, grad_in, 0)
        s_ins[k].start()

    lax.fori_loop(0, HALF // 256, grad_out, 0)
    for part in s_outs:
        part.start()

    gate_back = jnp.sum(slot_back * out32[...], axis=1, keepdims=True)
    back1 = gate_back.astype(BF16).astype(F32)
    back2 = (gate_back - back1).astype(BF16).astype(F32)
    backs = [back1, back2, gate_back - back1 - back2]
    spread = jnp.zeros((256, 256), F32)
    for m in range(3):
        spread = spread + dot(note_of[m], jnp.where(own_lane, backs[m], 0.0).astype(BF16), 0, 0)
    for p in range(3):
        cols = slice(256 * p, 256 * (p + 1))
        in_back = dot(pb[0:SLOTS, :], full_in[cols, :], 1, 1).astype(BF16)
        ib[:, cols] = in_back[0:256]
        spread = spread + dot(picked[p], in_back[256:SLOTS], 0, 0)
    ib[:, D:] = spread.astype(BF16)
    send_ib = Exchange(j, z_dev, lambda q: rows(ib, q, 16), lambda s: rows(ibrecv, s, 16), ibrecv.at[pl.ds(0, 240)], s_ib)
    send_ib.start()
    rows(ibrecv, j, 16)[...] = rows(ib, j, 16)[...]

    for i in range(4):
        for part in s_ins:
            part.mid(i)
    for i in range(3):
        for part in s_ins:
            part.end(i)
        for part in s_outs:
            part.mid(i)
    v32[...] = jnp.concatenate([part.end(3) for part in s_ins], axis=1)
    vback[...] = stack(v32[pl.ds(pl.multiple_of(24 * (1 - h), 8), 24), :])
    back_pair = pltpu.make_async_remote_copy(
        src_ref=vback, dst_ref=vfinal,
        send_sem=pair2_sem.at[0], recv_sem=pair2_sem.at[1], device_id=other, device_id_type=MESH,
    )
    back_pair.start()
    for part in s_outs:
        part.mid(3)
    for i in range(2):
        for part in s_outs:
            part.end(i)

    send_ib.wait()
    inputs = tok[...].astype(F32)
    centred = inputs - jnp.mean(inputs, axis=1, keepdims=True)
    inverse = lax.rsqrt(jnp.mean(centred * centred, axis=1, keepdims=True) + EPS)
    scaled = centred * inverse
    back_main = dot(jnp.concatenate([main, main], axis=1), ibrecv[:, :D])
    back_tail = [dot(jnp.concatenate([e, e], axis=1), ibrecv[:, D:]) for e in extra]
    normed_back = back_main + jnp.concatenate(back_tail, axis=1)
    gained = normed_back * gain[...].reshape(1, D)
    repeated = jnp.broadcast_to(layer_back.reshape(PAIR, 1, D), (PAIR, TEXT, D)).reshape(TOK, D)
    tg[...] = (
        repeated
        + inverse * (gained - jnp.mean(gained, axis=1, keepdims=True) - scaled * jnp.mean(gained * scaled, axis=1, keepdims=True))
    ).astype(BF16)
    row_i = iota((TOK, 256), 1)
    kind = lax.rem(row_i, 16)
    owner = jnp.logical_and(jnp.logical_and(kind >= 12, kind < 15), lax.rem(row_i // 16, 8).astype(F32) == chosen)
    gathered = dot(hot(owner), ibrecv[:, D:])
    token_gate = jnp.sum(jnp.where(at_slot, gathered, 0.0), axis=1, keepdims=True)
    gg[...] = jnp.broadcast_to(token_gate, (TOK, TOK)).T[0:1]

    for part in s_outs:
        part.end(2)
    for k in (0, 1):
        dwout[48 * k : 48 * (k + 1), :] = s_outs[k].end(3)
    kept = v32[pl.ds(pl.multiple_of(24 * h, 8), 24), :]
    held = []
    for g in range(4):
        hi, lo = split2(kept[:, SP * g : SP * (g + 1)])
        held.append(dot(hi, sel[0], 1, 1) + dot(lo, sel[0], 1, 1))
    back_pair.wait_recv()
    came = unstack(vfinal[...])
    for g in range(4):
        dwin[:, D * g : D * (g + 1)] = held[g] + dot(came[:, SP * g : SP * (g + 1)].astype(BF16), sel[1], 1, 1)

    pair.wait_send()
    join.wait_send()
    share.wait_send()
    back_pair.wait_send()
    for part in outs + ins + s_ins + s_outs:
        part.sent()
    for exchange in (images, send_x, send_c, send_t, send_r, send_cc, send_tb, send_lb, send_ib):
        exchange.sent()


def hand_on(*refs):
    for k in range(4):
        refs[4 + k][...] = refs[k][...]


def body(tokens, expert_ids, gate, ln_gain, w_in, w_out, image_emb):
    vmem = pl.BlockSpec(memory_space=pltpu.VMEM)
    f32 = lambda *shape: pltpu.VMEM(shape, F32)
    b16 = lambda *shape: pltpu.VMEM(shape, BF16)
    sems = lambda *shape: pltpu.SemaphoreType.DMA(shape)
    token_grad, gate_grad, in_grad, out_grad = pl.pallas_call(
        kernel,
        out_shape=(
            jax.ShapeDtypeStruct((TOK, D), BF16),
            jax.ShapeDtypeStruct((1, TOK), F32),
            jax.ShapeDtypeStruct((24, H), F32),
            jax.ShapeDtypeStruct((RO, D), F32),
        ),
        in_specs=[vmem] * 7,
        out_specs=(vmem,) * 4,
        scratch_shapes=[
            b16(2, D, SP),
            b16(RI, D),
            f32(RI, HALF),
            b16(RI, D),
            b16(RI, D),
            b16(RI, D),
            b16(D, HALF),
            b16(HALF, D),
            b16(256, D // 2),
            b16(TOK, D),
            b16(TOK, 1024),
            b16(256, 1024),
            b16(SP, D),
            b16(D, SP),
            f32(SLOTS, HALF),
            f32(SLOTS, HALF),
            b16(SP, HALF),
            b16(HALF, SP),
            f32(SLOTS, D),
            b16(256, D // 2),
            b16(128, D // 2),
            b16(128, D // 2),
            b16(128, D // 2),
            b16(256, D // 2),
            f32(1, TOK),
            f32(N, 1, TOK),
            f32(1, TOK),
            f32(N, 1, TOK),
            b16(256, D // 2),
            b16(256, D // 2),
            b16(256, D // 2),
            b16(SP, D),
            b16(SP, HALF),
            b16(256, 1024),
            b16(256, 1024),
            b16(D, HALF),
            b16(HALF, D),
            b16(4, 5, 2, 48, SP),
            b16(4, 5, 2, 48, D),
            sems(4, 13),
            sems(4, 16),
            sems(2),
            sems(2),
        ]
        + [sems(2)] * 11,
        compiler_params=pltpu.CompilerParams(
            collective_id=0, has_side_effects=True, vmem_limit_bytes=56 * 1024 * 1024
        ),
        cost_estimate=pl.CostEstimate(flops=5_000_000_000, bytes_accessed=2_000_000, transcendentals=1_000_000),
    )(tokens, expert_ids.reshape(1, TOK), gate.reshape(1, TOK), ln_gain, w_in[0], w_out[0], image_emb)
    results = (token_grad, gate_grad, in_grad, out_grad)
    token_grad, gate_grad, in_grad, out_grad = pl.pallas_call(
        hand_on,
        out_shape=tuple(jax.ShapeDtypeStruct(r.shape, r.dtype) for r in results),
        in_specs=[vmem] * 4,
        out_specs=(vmem,) * 4,
    )(*results)
    return token_grad, gate_grad.reshape(TOK), in_grad[None], out_grad[None]


def solution(mesh):
    in_specs = (
        P(("dp", "expert"), None),
        P(("dp", "expert"), None),
        P(("dp", "expert")),
        P(),
        P("expert", "dp", None),
        P("expert", "dp", None),
        P(("dp", "expert"), None),
    )
    out_specs = (
        P(("dp", "expert"), None),
        P(("dp", "expert")),
        P("expert", "dp", None),
        P("expert", "dp", None),
    )
    return jax.shard_map(body, mesh=mesh, in_specs=in_specs, out_specs=out_specs, check_vma=False)
```

```python
import jax
import jax.numpy as jnp
from jax import lax
from jax.experimental import pallas as pl
from jax.experimental.pallas import tpu as pltpu
from jax.sharding import PartitionSpec as P

MESH = pl.DeviceIdType.MESH
F32 = jnp.float32
BF16 = jnp.bfloat16

D = 768
H = 3072
HALF = 1536
TOK = 128
CAP = 20
PAIR = 8
TEXT = 16
N = 16
R = 4
RO = 96
RI = 48
SLOTS = 320
SP = 384
EPS = 1e-6
LINE = (4, 3, 5, 2, 6, 1, 7)
RING = (8, 9, 7, 6, 10, 5, 11, 4, 12, 3, 13, 2, 14, 1, 15)
PLANE = (10, 9, 11, 6, 14, 2, 8, 5, 7, 13, 15, 1, 3, 4, 12)
SCALE = 100.0


def dot(a, b, ca=1, cb=0):
    return lax.dot_general(a, b, (((ca,), (cb,)), ((), ())), preferred_element_type=F32)


def iota(shape, axis):
    return lax.broadcasted_iota(jnp.int32, shape, axis)


def hot(mask):
    return jnp.where(mask, 1.0, 0.0).astype(BF16)


def split2(v):
    hi = v.astype(BF16)
    return hi, (v - hi.astype(F32)).astype(BF16)


def fold(v):
    m = v.shape[0] // 8
    v = v.reshape(m, 8, D)
    return jnp.concatenate([v[:, :, : D // 2], v[:, :, D // 2 :]], axis=1).reshape(16 * m, D // 2).astype(BF16)


def unfold(v):
    m = v.shape[0] // 16
    v = v.astype(F32).reshape(m, 16, D // 2)
    return jnp.concatenate([v[:, :8], v[:, 8:]], axis=2).reshape(8 * m, D)


def stack(v):
    return jnp.concatenate([v[:, :SP], v[:, SP:]], axis=0).astype(BF16)


def unstack(v):
    v = v.astype(F32)
    return jnp.concatenate([v[:24], v[24:]], axis=1)


def wrap(v):
    return lax.rem(v + 2 * R, R)


class Gather:
    def __init__(self, block, c1, c2, dev1, dev2, four, fifteen, sem, g):
        self.block, self.c1, self.c2 = block, c1, c2
        self.dev1, self.dev2, self.sem, self.g = dev1, dev2, sem, g
        self.four, self.fifteen = four, fifteen
        self.bs = [c1, wrap(c1 - 1), wrap(c1 + 1), wrap(c1 + 2)]

    def copy(self, k, ref, dev):
        return pltpu.make_async_remote_copy(
            src_ref=ref, dst_ref=ref, send_sem=self.sem.at[self.g, 12], recv_sem=self.sem.at[self.g, k],
            device_id=dev, device_id_type=MESH,
        )

    def got(self, k, ref):
        self.copy(k, ref, self.dev1(1)).wait_recv()
        return ref

    def at(self, a, b, half=None):
        return self.block(wrap(a), wrap(b), half)

    def second(self, i):
        ref = self.at(self.bs[i], self.c2)
        self.copy(3 + 2 * i, ref, self.dev2(1)).start()
        self.copy(4 + 2 * i, ref, self.dev2(-1)).start()

    def start(self):
        ref = self.at(self.c1, self.c2)
        self.copy(0, ref, self.dev1(1)).start()
        self.copy(1, ref, self.dev1(-1)).start()

    def stage1(self):
        c1, c2 = self.c1, self.c2
        self.got(0, self.at(c1 - 1, c2))
        self.copy(2, self.at(c1 - 1, c2, 0), self.dev1(1)).start()
        self.second(1)
        self.got(1, self.at(c1 + 1, c2))
        self.copy(2, self.at(c1 + 1, c2, 1), self.dev1(-1)).start()
        self.second(2)

    def stage2(self):
        self.got(2, self.at(self.c1 + 2, self.c2))
        self.second(3)

    def stage3(self, i):
        b, c2 = self.bs[i], self.c2
        self.got(3 + 2 * i, self.at(b, c2 - 1))
        self.copy(11, self.at(b, c2 - 1, 0), self.dev2(1)).start()
        self.got(4 + 2 * i, self.at(b, c2 + 1))
        self.copy(11, self.at(b, c2 + 1, 1), self.dev2(-1)).start()

    def stage4(self):
        self.got(11, self.four)

    def sent(self):
        self.copy(12, self.fifteen, self.dev1(1)).wait_send()


class Scatter:
    def __init__(self, block, c1, c2, dev1, dev2, halves, fulls, fifteen, sem, g):
        self.block, self.c1, self.c2 = block, c1, c2
        self.dev1, self.dev2, self.sem, self.g = dev1, dev2, sem, g
        self.halves, self.fulls, self.fifteen = halves.at[g], fulls.at[g], fifteen
        self.bs = [wrap(c2 + 2), wrap(c2 + 1), wrap(c2 - 1), c2]

    def copy(self, k, src, dst, dev):
        return pltpu.make_async_remote_copy(
            src_ref=src, dst_ref=dst, send_sem=self.sem.at[self.g, 15], recv_sem=self.sem.at[self.g, k],
            device_id=dev, device_id_type=MESH,
        )

    def got(self, k, ref):
        self.copy(k, ref, ref, self.dev1(1)).wait_recv()
        return ref

    def at(self, a, b, half=None):
        return self.block(wrap(a), wrap(b), half)

    def add(self, ref, *others):
        total = ref[...].astype(F32)
        for other in others:
            total = total + other[...].astype(F32)
        ref[...] = total.astype(BF16)

    def start(self):
        for i in range(4):
            self.copy(2 * i, self.at(self.c1 + 2, self.bs[i], 0), self.halves.at[i, 0], self.dev1(1)).start()
            self.copy(2 * i + 1, self.at(self.c1 + 2, self.bs[i], 1), self.halves.at[i, 1], self.dev1(-1)).start()

    def mid(self, i):
        b = self.bs[i]
        self.add(self.at(self.c1 + 1, b, 0), self.got(2 * i, self.halves.at[i, 0]))
        self.copy(8 + i, self.at(self.c1 + 1, b), self.fulls.at[i, 0], self.dev1(1)).start()
        self.add(self.at(self.c1 - 1, b, 1), self.got(2 * i + 1, self.halves.at[i, 1]))
        self.copy(8 + i, self.at(self.c1 - 1, b), self.fulls.at[i, 1], self.dev1(-1)).start()

    def end(self, i):
        c1, b = self.c1, self.bs[i]
        self.got(8 + i, self.fulls.at[i])
        first, second = self.fulls.at[i, 0], self.fulls.at[i, 1]
        if i == 0:
            self.add(self.at(c1, b), first, second)
            self.copy(12, self.at(c1, b, 0), self.halves.at[4, 0], self.dev2(1)).start()
            self.copy(13, self.at(c1, b, 1), self.halves.at[4, 1], self.dev2(-1)).start()
        elif i == 1:
            self.add(self.at(c1, b), first, second)
            self.add(self.at(c1, b, 0), self.got(12, self.halves.at[4, 0]))
            self.copy(14, self.at(c1, b), self.fulls.at[4, 0], self.dev2(1)).start()
        elif i == 2:
            self.add(self.at(c1, b), first, second)
            self.add(self.at(c1, b, 1), self.got(13, self.halves.at[4, 1]))
            self.copy(14, self.at(c1, b), self.fulls.at[4, 1], self.dev2(-1)).start()
        else:
            total = self.at(c1, b)[...].astype(F32) + first[...].astype(F32) + second[...].astype(F32)
            self.got(14, self.fulls.at[4])
            for k in (0, 1):
                total = total + self.fulls[4, k].astype(F32)
            return total

    def sent(self):
        self.copy(15, self.fifteen, self.fifteen, self.dev1(1)).wait_send()


def kernel(
    tok, ids, gate, gain, win, wout, img,
    tg, gg, dwin, dwout,
    sel, vsend, v32, vcame, vback, vfinal, full_in, full_out, imgs, imgb,
    xsend, xr, xs, xt, pre, cdf, act, actt, out32,
    contrib, cjoin, csend, crecv, tall, rsum, rrecv, csum, ccrecv, tb, tbrecv, lb, ob, pb,
    ib, ibrecv, mixed, mixes, lball, gi, halves, fulls,
    ag_sem, rs_sem, pair_sem, pair2_sem,
    s_img, s_x, s_c, s_t, s_r, s_cc, s_tb, s_lb, s_ib, s_join, s_share, s_share2, s_m,
):
    dp, ex = lax.axis_index("dp"), lax.axis_index("expert")
    xy, h = dp // 2, lax.rem(dp, 2)
    y, x = xy // R, lax.rem(xy, R)
    j = 8 * h + ex

    def z_dev(q):
        return (2 * xy + q // 8, lax.rem(q, 8))

    def p_dev(k):
        return (2 * k + h, ex)

    chip, core = 4 * h + ex // 2, lax.rem(ex, 2)
    seat = 8 * core + chip

    def c_dev(k):
        return (2 * xy + k // 4, 2 * lax.rem(k, 4) + core)

    twin = (dp, ex + 1 - 2 * core)

    def x_dev(step):
        return p_dev(R * y + wrap(x + step))

    def y_dev(step):
        return p_dev(R * wrap(y + step) + x)

    def each(fn):
        def step(i, carry):
            fn(i)
            return carry

        lax.fori_loop(1, N, step, 0)

    class Exchange:
        def __init__(self, me, dev, src, dst, all_but_one, sem, size=N, order=None):
            self.me, self.dev, self.src, self.dst, self.sem = me, dev, src, dst, sem
            self.order = order
            self.all_but_one, self.size = all_but_one, size

        def copy(self, src, dst, to):
            return pltpu.make_async_remote_copy(
                src_ref=src, dst_ref=dst, send_sem=self.sem.at[0], recv_sem=self.sem.at[1],
                device_id=self.dev(to), device_id_type=MESH,
            )

        def start(self):
            def step(i, carry):
                to = lax.rem(self.me + i, self.size)
                self.copy(self.src(to), self.dst(self.me), to).start()
                return carry

            if self.order is None:
                lax.fori_loop(1, self.size, step, 0)
            else:
                for i in self.order:
                    step(i, 0)

        def wait(self):
            self.copy(self.all_but_one, self.all_but_one, lax.rem(self.me + 1, self.size)).wait_recv()

        def sent(self):
            self.copy(self.all_but_one, self.all_but_one, lax.rem(self.me + 1, self.size)).wait_send()

    def rows(ref, k, n):
        return ref.at[pl.ds(pl.multiple_of(k * n, n), n)]

    barrier = pltpu.get_barrier_semaphore()

    def greet(i):
        pl.semaphore_signal(barrier, inc=1, device_id=z_dev(lax.rem(j + i, N)), device_id_type=MESH)
        pl.semaphore_signal(barrier, inc=1, device_id=p_dev(lax.rem(xy + i, N)), device_id_type=MESH)

    each(greet)

    rows(full_out, xy, RO)[...] = wout[...]
    source = iota((D, SP), 0)
    column = iota((D, SP), 1)
    spot = column + (column // RO) * RO
    sel[0] = hot(source == spot + RO * h)
    sel[1] = hot(source == spot + RO * (1 - h))
    mine, theirs = [], []
    for g in range(4):
        part = win[:, D * g : D * (g + 1)]
        mine.append(dot(part, sel[0]))
        theirs.append(dot(part, sel[1]))
    for k in (0, 1):
        vsend[k] = stack(jnp.concatenate(theirs[2 * k : 2 * k + 2], axis=1))
    for g in range(4):
        v32[pl.ds(pl.multiple_of(24 * h, 8), 24), SP * g : SP * (g + 1)] = mine[g]
    image = img[...].astype(F32)
    image = image * lax.rsqrt(jnp.sum(image * image, axis=1, keepdims=True) + EPS)
    rows(imgs, j, 16)[...] = fold(image)

    inputs = tok[...].astype(F32)
    centred = inputs - jnp.mean(inputs, axis=1, keepdims=True)
    inverse = lax.rsqrt(jnp.mean(centred * centred, axis=1, keepdims=True) + EPS)
    normed = (centred * inverse * gain[...].reshape(1, D)).astype(BF16)
    token_sum = jnp.sum(inputs.reshape(PAIR, TEXT, D), axis=1)

    chosen_row = jnp.broadcast_to(ids[...].astype(F32), (TOK, TOK))
    chosen = chosen_row.T[:, 0:1]
    lane = iota((TOK, TOK), 1).astype(F32)
    onehot = hot(lane == chosen)
    before = dot(hot(iota((TOK, TOK), 0) > iota((TOK, TOK), 1)), onehot)
    slot = jnp.sum(before * onehot.astype(F32), axis=1, keepdims=True)
    is_main = slot < 16.0
    is_extra = jnp.logical_and(slot >= 16.0, slot < float(CAP))
    main = hot(lane == jnp.where(is_main, 16.0 * chosen + slot, -1.0))
    extra = [hot(lane == jnp.where(is_extra, 16.0 * chosen + (4.0 * p - 16.0) + slot, -1.0)) for p in range(3)]
    at_slot = iota((TOK, 256), 1).astype(F32) == jnp.where(slot < float(CAP), slot, -1.0)

    xsend[:, :D] = dot(main.T, normed).astype(BF16)
    tail = dot(extra[0].T, normed[:, 0:256]) + dot(extra[1].T, normed[:, 256:512]) + dot(extra[2].T, normed[:, 512:768])
    gate_row = gate[...]
    gate1 = gate_row.astype(BF16).astype(F32)
    gate2 = (gate_row - gate1).astype(BF16).astype(F32)
    gate3 = gate_row - gate1 - gate2
    line = iota((TOK, TOK), 0)
    kind = lax.rem(line, 16)
    pair_row = (iota((TOK, TOK), 1) // TEXT).astype(F32)
    notes = jnp.where(kind == 12, gate1, jnp.where(kind == 13, gate2, jnp.where(kind == 14, gate3, jnp.where(kind == 15, pair_row, 0.0))))
    notes = jnp.where((line // 16).astype(F32) == chosen_row, notes, 0.0)
    xsend[:, D:] = (tail + dot(notes.astype(BF16), hot(at_slot))).astype(BF16)
    rows(xr, j, 16)[...] = rows(xsend, ex, 16)[...]

    pl.semaphore_wait(barrier, 2 * (N - 1))

    def out_at(buf, part):
        def block(xc, yc, half=None):
            row = pl.multiple_of((R * yc + xc) * RO + 48 * part, 16)
            if half is None:
                return buf.at[pl.ds(row, 48)]
            return buf.at[pl.ds(row, 48), pl.ds(SP * half, SP)]

        return block

    def in_at(buf, part):
        def block(xc, yc, half=None):
            row = pl.multiple_of((R * yc + xc) * RI, 16)
            if half is None:
                return buf.at[pl.ds(row, RI), pl.ds(D * part, D)]
            return buf.at[pl.ds(row, RI), pl.ds(D * part + SP * half, SP)]

        return block

    wide = pl.ds(pl.multiple_of(SP * core, TOK), SP)

    def back_at(buf, part):
        def block(xc, yc, half=None):
            row = pl.multiple_of((R * yc + xc) * TOK + 64 * part, 32)
            if half is None:
                return buf.at[pl.ds(row, 64), wide]
            return buf.at[pl.ds(pl.multiple_of(row + 32 * half, 32), 32), wide]

        return block

    def both(make, buf, at, first, *args):
        other_way = at(buf, 1)
        return (
            make(at(buf, 0), x, y, x_dev, y_dev, *args, first),
            make(lambda a, b, half=None: other_way(b, a, half), y, x, y_dev, x_dev, *args, first + 1),
        )

    fifteen = full_out.at[pl.ds(0, 15 * 48)]
    outs = both(Gather, full_out, out_at, 0, full_out.at[pl.ds(0, 192)], fifteen, ag_sem)
    ins = both(Gather, full_in, in_at, 2, full_in.at[pl.ds(0, 96)], fifteen, ag_sem)

    other = (2 * xy + 1 - h, ex)
    swaps = [
        pltpu.make_async_remote_copy(
            src_ref=vsend.at[k], dst_ref=vcame.at[k], send_sem=pair_sem.at[k], recv_sem=pair_sem.at[2 + k],
            device_id=other, device_id_type=MESH,
        )
        for k in (0, 1)
    ]
    for swap in swaps:
        swap.start()
    for part in outs:
        part.start()
    for part in outs:
        part.second(0)

    images = Exchange(j, z_dev, lambda q: rows(imgs, j, 16), lambda s: rows(imgs, s, 16), imgs.at[pl.ds(0, 240)], s_img)

    send_x = Exchange(j, z_dev, lambda q: rows(xsend, lax.rem(q, 8), 16), lambda s: rows(xr, s, 16), xr.at[pl.ds(0, 240)], s_x)

    for part in outs:
        part.stage1()
    for part in outs:
        part.stage2()
    for k in (0, 1):
        swaps[k].wait_recv()
        half = slice(D * k, D * (k + 1))
        v32[pl.ds(pl.multiple_of(24 * (1 - h), 8), 24), half] = unstack(vcame[k])
        rows(full_in, xy, RI).at[:, half][...] = v32[:, half].astype(BF16)
        ins[k].start()
        outs[k].stage3(0)
    for part in ins:
        part.second(0)
    send_x.start()
    images.start()
    for i in (1, 2):
        for part in outs:
            part.stage3(i)
    for part in ins:
        part.stage1()
    for part in outs:
        part.stage3(3)
    for part in ins:
        part.stage2()
    for i in range(4):
        for part in ins:
            part.stage3(i)

    send_x.wait()
    row64 = iota((64, 256), 0)
    lane64 = iota((64, 256), 1)
    picked = [hot(lane64 == 16 * (row64 // 4) + 4 * p + lax.rem(row64, 4)) for p in range(3)]
    xs[0:256, :] = xr[:, :D]
    for p in range(3):
        xs[256:SLOTS, 256 * p : 256 * (p + 1)] = dot(picked[p], xr[:, D:]).astype(BF16)
    xs[SLOTS:, :] = jnp.zeros((SP - SLOTS, D), BF16)
    xt[...] = xs[...].T
    slot_i = iota((SLOTS, 256), 0)
    lane_i = iota((SLOTS, 256), 1)
    slot_from = jnp.where(slot_i < 256, slot_i // 16, (slot_i - 256) // 4)
    slot_at = jnp.where(slot_i < 256, lax.rem(slot_i, 16), 16 + lax.rem(slot_i, 4))
    note_of = [hot(lane_i == 16 * slot_from + 12 + m) for m in range(4)]
    tails = xr[:, D:]
    own_lane = lane_i == slot_at
    gate_col = jnp.sum(jnp.where(own_lane, dot(note_of[0] + note_of[1] + note_of[2], tails), 0.0), axis=1, keepdims=True)
    pair_col = jnp.sum(jnp.where(own_lane, dot(note_of[3], tails), 0.0), axis=1, keepdims=True)
    first_pair = (PAIR * (8 * lax.rem(slot_from, 2) + slot_from // 2))[:, :TOK].astype(F32)
    pair_of = hot(lane_i[:, :TOK].astype(F32) == first_pair + pair_col)

    images.wait()
    imgb[...] = unfold(imgs[...]).astype(BF16)
    for part in ins:
        part.stage4()

    def chunk(n, size):
        return pl.ds(pl.multiple_of(n * size, size), size)

    def forward(n, carry):
        cols = chunk(n, 256)
        value = dot(xs[0:SLOTS, :], full_in[:, cols])
        bell = 0.5 * (1.0 + lax.erf(value * (0.5**0.5)))
        pre[:, cols] = value
        cdf[:, cols] = bell
        act[0:SLOTS, cols] = (value * bell).astype(BF16)
        return carry

    lax.fori_loop(0, HALF // 256, forward, 0)
    act[SLOTS:, :] = jnp.zeros((SP - SLOTS, HALF), BF16)
    for part in outs:
        part.stage4()

    def project(n, carry):
        cols = chunk(n, 256)
        out32[:, cols] = dot(act[0:SLOTS, :], full_out[:, cols])
        return carry

    lax.fori_loop(0, D // 256, project, 0)

    contrib[...] = fold(dot(pair_of, (gate_col * out32[...]).astype(BF16), 0, 0))
    join = pltpu.make_async_remote_copy(
        src_ref=rows(contrib, 1 - core, 128), dst_ref=cjoin, send_sem=s_join.at[0], recv_sem=s_join.at[1],
        device_id=twin, device_id_type=MESH,
    )
    join.start()
    join.wait_recv()
    joined = rows(contrib, core, 128)
    csend[...] = (joined[...].astype(F32) + cjoin[...].astype(F32)).astype(BF16)
    send_c = Exchange(
        chip, c_dev, lambda q: rows(csend, q, 16), lambda s: rows(crecv, s, 16), crecv.at[pl.ds(0, 112)], s_c, 8, LINE
    )
    send_c.start()
    rows(crecv, chip, 16)[...] = rows(csend, chip, 16)[...]

    actt[...] = act[...].T
    weight1, weight2 = split2(gate_col * pair_of.astype(F32))
    pad = jnp.zeros((SP - SLOTS, TOK), BF16)
    weight1 = jnp.concatenate([weight1, pad], axis=0)
    weight2 = jnp.concatenate([weight2, pad], axis=0)

    def mix(n, carry):
        part = actt[chunk(n, 256), :]
        mixed[chunk(n, 256), :] = (dot(part, weight1) + dot(part, weight2)).astype(BF16)
        return carry

    lax.fori_loop(0, HALF // 256, mix, 0)
    send_m = Exchange(
        xy, p_dev, lambda q: rows(mixed, q, RO), lambda s: mixes.at[s], mixes.at[pl.ds(0, N - 1)], s_m
    )

    def slope(n, carry):
        cols = chunk(n, 256)
        value = pre[:, cols]
        pre[:, cols] = cdf[:, cols] + value * (jnp.exp(-0.5 * value * value) * 0.3989422804014327)
        return carry

    send_c.wait()
    pooled = (token_sum + jnp.sum(unfold(crecv[...]).reshape(8, PAIR, D), axis=0)) * (1.0 / TEXT)
    q_inv = lax.rsqrt(jnp.sum(pooled * pooled, axis=1, keepdims=True) + EPS)
    unit = pooled * q_inv
    rows(tall, xy, 16)[...] = fold(unit)
    send_t = Exchange(xy, p_dev, lambda q: rows(tall, xy, 16), lambda s: rows(tall, s, 16), tall.at[pl.ds(0, 240)], s_t, N, PLANE)
    send_t.start()
    send_m.start()
    mixes[pl.ds(xy, 1)] = rows(mixed, xy, RO)[...].reshape(1, RO, TOK)
    lax.fori_loop(0, 3, slope, 0)
    send_t.wait()

    scores = SCALE * dot(unfold(tall[...]).astype(BF16), imgb[...], 1, 1)
    exped = jnp.exp(scores)
    csum[...] = jnp.sum(exped, axis=0, keepdims=True)
    rsum[...] = jnp.sum(exped.T, axis=0, keepdims=True)
    send_r = Exchange(xy, p_dev, lambda q: rsum, lambda s: rrecv.at[s], rrecv.at[pl.ds(0, N - 1)], s_r, N, PLANE)
    send_cc = Exchange(j, z_dev, lambda q: csum, lambda s: ccrecv.at[s], ccrecv.at[pl.ds(0, N - 1)], s_cc, N, RING)
    send_cc.start()
    send_r.start()
    rrecv[pl.ds(xy, 1)] = rsum[...].reshape(1, 1, TOK)
    ccrecv[pl.ds(j, 1)] = csum[...].reshape(1, 1, TOK)
    text_at = iota((TOK, TOK), 0)
    image_at = iota((TOK, TOK), 1)
    diagonal = jnp.where(
        jnp.logical_and(image_at // PAIR == j, text_at == PAIR * xy + lax.rem(image_at, PAIR)), 1.0, 0.0
    )
    lax.fori_loop(3, 6, slope, 0)
    send_r.wait()
    send_cc.wait()
    row_total = jnp.broadcast_to(jnp.sum(rrecv[...], axis=0), (TOK, TOK)).T
    col_total = jnp.sum(ccrecv[...], axis=0)
    coefs = (0.5 * (exped / row_total + exped / col_total) - diagonal).astype(BF16)
    tb[...] = fold(SCALE * dot(coefs, imgb[...]))
    send_tb = Exchange(xy, p_dev, lambda q: rows(tb, q, 16), lambda s: rows(tbrecv, s, 16), tbrecv.at[pl.ds(0, 240)], s_tb, N, PLANE)
    send_tb.start()
    rows(tbrecv, xy, 16)[...] = rows(tb, xy, 16)[...]
    send_tb.wait()
    text_back = jnp.sum(unfold(tbrecv[...]).reshape(N, PAIR, D), axis=0)
    pooled_back = q_inv * (text_back - unit * jnp.sum(unit * text_back, axis=1, keepdims=True))
    layer_back = pooled_back * (1.0 / TEXT)
    rows(lb, seat, 16)[...] = fold(layer_back)
    send_lb = Exchange(
        chip, c_dev, lambda q: rows(lb, seat, 16), lambda s: rows(lb, 8 * core + s, 16), lb.at[pl.ds(0, 112)], s_lb, 8, LINE
    )
    send_lb.start()
    send_lb.wait()
    ours = rows(lb, core, 128)
    share = pltpu.make_async_remote_copy(
        src_ref=ours, dst_ref=ours, send_sem=s_share.at[0], recv_sem=s_share.at[1], device_id=twin, device_id_type=MESH
    )
    share.start()
    share.wait_recv()

    pairs_back = unfold(lb[...]).astype(BF16)
    rows(lball, xy, TOK).at[:, wide][...] = jnp.where(core == 0, pairs_back[:, :SP], pairs_back[:, SP:])
    g_lbs = both(
        Gather, lball, back_at, 4, lball.at[pl.ds(0, 256), pl.ds(0, SP)], lball.at[pl.ds(0, 960), pl.ds(0, SP)], ag_sem
    )
    for part in g_lbs:
        part.start()
    for part in g_lbs:
        part.second(0)
    slot_back = dot(pair_of, pairs_back)
    ob[...] = (gate_col * slot_back).astype(BF16)
    pb[SLOTS:, :] = jnp.zeros((SP - SLOTS, HALF), BF16)

    def back(n, carry):
        cols = chunk(n, 256)
        act_back = dot(ob[...], full_out[cols, :], 1, 1)
        pb[0:SLOTS, cols] = (act_back * pre[:, cols]).astype(BF16)
        return carry

    def grad_in(n, carry):
        cols = chunk(n, 256)
        gi[:, cols] = dot(xt[...], pb[:, cols]).astype(BF16)
        return carry

    s_ins = both(Scatter, gi, in_at, 0, halves, fulls, fifteen, rs_sem)
    for k in (0, 1):
        lax.fori_loop(3 * k, 3 * k + 3, back, 0)
        lax.fori_loop(3 * k, 3 * k + 3, grad_in, 0)
        s_ins[k].start()

    gate_back = jnp.sum(slot_back * out32[...], axis=1, keepdims=True)
    back1 = gate_back.astype(BF16).astype(F32)
    back2 = (gate_back - back1).astype(BF16).astype(F32)
    backs = [back1, back2, gate_back - back1 - back2]
    spread = jnp.zeros((256, 256), F32)
    for m in range(3):
        spread = spread + dot(note_of[m], jnp.where(own_lane, backs[m], 0.0).astype(BF16), 0, 0)
    for part in g_lbs:
        part.stage1()
    for p in range(3):
        cols = slice(256 * p, 256 * (p + 1))
        in_back = dot(pb[0:SLOTS, :], full_in[cols, :], 1, 1).astype(BF16)
        ib[:, cols] = in_back[0:256]
        spread = spread + dot(picked[p], in_back[256:SLOTS], 0, 0)
        if p < 2:
            for part in s_ins:
                part.mid(p)
    ib[:, D:] = spread.astype(BF16)
    send_ib = Exchange(
        j, z_dev, lambda q: rows(ib, q, 16), lambda s: rows(ibrecv, s, 16), ibrecv.at[pl.ds(0, 240)], s_ib
    )
    send_ib.start()
    rows(ibrecv, j, 16)[...] = rows(ib, j, 16)[...]
    for part in g_lbs:
        part.stage2()
    for i in (2, 3):
        for part in s_ins:
            part.mid(i)
    for i in range(3):
        for part in g_lbs:
            part.stage3(i)
        for part in s_ins:
            part.end(i)
    for part in g_lbs:
        part.stage3(3)
    swaps_back = []
    for k in (0, 1):
        half = slice(D * k, D * (k + 1))
        v32[:, half] = s_ins[k].end(3)
        vback[k] = stack(v32[pl.ds(pl.multiple_of(24 * (1 - h), 8), 24), half])
        swap = pltpu.make_async_remote_copy(
            src_ref=vback.at[k], dst_ref=vfinal.at[k], send_sem=pair2_sem.at[k], recv_sem=pair2_sem.at[2 + k],
            device_id=other, device_id_type=MESH,
        )
        swap.start()
        swaps_back.append(swap)
    for part in g_lbs:
        part.stage4()
    ours = lball.at[:, wide]
    share2 = pltpu.make_async_remote_copy(
        src_ref=ours, dst_ref=ours, send_sem=s_share2.at[0], recv_sem=s_share2.at[1], device_id=twin, device_id_type=MESH
    )
    share2.start()

    send_ib.wait()
    inputs = tok[...].astype(F32)
    centred = inputs - jnp.mean(inputs, axis=1, keepdims=True)
    inverse = lax.rsqrt(jnp.mean(centred * centred, axis=1, keepdims=True) + EPS)
    scaled = centred * inverse
    back_main = dot(jnp.concatenate([main, main], axis=1), ibrecv[:, :D])
    back_tail = [dot(jnp.concatenate([e, e], axis=1), ibrecv[:, D:]) for e in extra]
    normed_back = back_main + jnp.concatenate(back_tail, axis=1)
    gained = normed_back * gain[...].reshape(1, D)
    repeated = jnp.broadcast_to(layer_back.reshape(PAIR, 1, D), (PAIR, TEXT, D)).reshape(TOK, D)
    tg[...] = (
        repeated
        + inverse * (gained - jnp.mean(gained, axis=1, keepdims=True) - scaled * jnp.mean(gained * scaled, axis=1, keepdims=True))
    ).astype(BF16)
    row_i = iota((TOK, 256), 1)
    kind = lax.rem(row_i, 16)
    owner = jnp.logical_and(jnp.logical_and(kind >= 12, kind < 15), lax.rem(row_i // 16, 8).astype(F32) == chosen)
    gathered = dot(hot(owner), ibrecv[:, D:])
    token_gate = jnp.sum(jnp.where(at_slot, gathered, 0.0), axis=1, keepdims=True)
    gg[...] = jnp.broadcast_to(token_gate, (TOK, TOK)).T[0:1]

    send_m.wait()
    factors = jnp.concatenate([mixes[k] for k in range(N)], axis=1)
    dwout[:, wide] = dot(factors, lball[:, wide])
    share2.wait_recv()
    rest = pl.ds(pl.multiple_of(SP * (1 - core), TOK), SP)
    dwout[:, rest] = dot(factors, lball[:, rest])
    kept = v32[pl.ds(pl.multiple_of(24 * h, 8), 24), :]
    held = []
    for g in range(4):
        hi, lo = split2(kept[:, SP * g : SP * (g + 1)])
        held.append(dot(hi, sel[0], 1, 1) + dot(lo, sel[0], 1, 1))
    for k in (0, 1):
        swaps_back[k].wait_recv()
        came = unstack(vfinal[k])
        for g in (0, 1):
            at = D * (2 * k + g)
            dwin[:, at : at + D] = held[2 * k + g] + dot(came[:, SP * g : SP * (g + 1)].astype(BF16), sel[1], 1, 1)

    for swap in swaps + swaps_back:
        swap.wait_send()
    join.wait_send()
    share.wait_send()
    share2.wait_send()
    for part in outs + ins + g_lbs + s_ins:
        part.sent()
    for exchange in (images, send_x, send_c, send_m, send_t, send_r, send_cc, send_tb, send_lb, send_ib):
        exchange.sent()


def hand_on(*refs):
    for k in range(4):
        refs[4 + k][...] = refs[k][...]


def body(tokens, expert_ids, gate, ln_gain, w_in, w_out, image_emb):
    vmem = pl.BlockSpec(memory_space=pltpu.VMEM)
    f32 = lambda *shape: pltpu.VMEM(shape, F32)
    b16 = lambda *shape: pltpu.VMEM(shape, BF16)
    sems = lambda *shape: pltpu.SemaphoreType.DMA(shape)
    token_grad, gate_grad, in_grad, out_grad = pl.pallas_call(
        kernel,
        out_shape=(
            jax.ShapeDtypeStruct((TOK, D), BF16),
            jax.ShapeDtypeStruct((1, TOK), F32),
            jax.ShapeDtypeStruct((24, H), F32),
            jax.ShapeDtypeStruct((RO, D), F32),
        ),
        in_specs=[vmem] * 7,
        out_specs=(vmem,) * 4,
        scratch_shapes=[
            b16(2, D, SP),
            b16(2, 48, SP),
            f32(RI, HALF),
            b16(2, 48, SP),
            b16(2, 48, SP),
            b16(2, 48, SP),
            b16(D, HALF),
            b16(HALF, D),
            b16(256, D // 2),
            b16(TOK, D),
            b16(TOK, 1024),
            b16(256, 1024),
            b16(SP, D),
            b16(D, SP),
            f32(SLOTS, HALF),
            f32(SLOTS, HALF),
            b16(SP, HALF),
            b16(HALF, SP),
            f32(SLOTS, D),
            b16(256, D // 2),
            b16(128, D // 2),
            b16(128, D // 2),
            b16(128, D // 2),
            b16(256, D // 2),
            f32(1, TOK),
            f32(N, 1, TOK),
            f32(1, TOK),
            f32(N, 1, TOK),
            b16(256, D // 2),
            b16(256, D // 2),
            b16(256, D // 2),
            b16(SLOTS, D),
            b16(SP, HALF),
            b16(256, 1024),
            b16(256, 1024),
            b16(HALF, TOK),
            b16(N, RO, TOK),
            b16(N * TOK, D),
            b16(D, HALF),
            b16(2, 5, 2, 48, SP),
            b16(2, 5, 2, 48, D),
            sems(6, 13),
            sems(2, 16),
            sems(4),
            sems(4),
        ]
        + [sems(2)] * 13,
        compiler_params=pltpu.CompilerParams(
            collective_id=0, has_side_effects=True, vmem_limit_bytes=56 * 1024 * 1024
        ),
        cost_estimate=pl.CostEstimate(flops=5_000_000_000, bytes_accessed=2_000_000, transcendentals=1_000_000),
    )(tokens, expert_ids.reshape(1, TOK), gate.reshape(1, TOK), ln_gain, w_in[0], w_out[0], image_emb)
    results = (token_grad, gate_grad, in_grad, out_grad)
    token_grad, gate_grad, in_grad, out_grad = pl.pallas_call(
        hand_on,
        out_shape=tuple(jax.ShapeDtypeStruct(r.shape, r.dtype) for r in results),
        in_specs=[vmem] * 4,
        out_specs=(vmem,) * 4,
    )(*results)
    return token_grad, gate_grad.reshape(TOK), in_grad[None], out_grad[None]


def solution(mesh):
    in_specs = (
        P(("dp", "expert"), None),
        P(("dp", "expert"), None),
        P(("dp", "expert")),
        P(),
        P("expert", "dp", None),
        P("expert", "dp", None),
        P(("dp", "expert"), None),
    )
    out_specs = (
        P(("dp", "expert"), None),
        P(("dp", "expert")),
        P("expert", "dp", None),
        P("expert", "dp", None),
    )
    return jax.shard_map(body, mesh=mesh, in_specs=in_specs, out_specs=out_specs, check_vma=False)
```

```python
import jax
import jax.numpy as jnp
from jax import lax
from jax.experimental import pallas as pl
from jax.experimental.pallas import tpu as pltpu
from jax.sharding import PartitionSpec as P

MESH = pl.DeviceIdType.MESH
F32 = jnp.float32
BF16 = jnp.bfloat16

D = 768
H = 3072
HALF = 1536
TOK = 128
CAP = 20
PAIR = 8
TEXT = 16
N = 16
R = 4
RO = 96
RI = 48
SLOTS = 320
SP = 384
EPS = 1e-6
LINE = (4, 3, 5, 2, 6, 1, 7)
RING = (8, 9, 7, 6, 10, 5, 11, 4, 12, 3, 13, 2, 14, 1, 15)
PLANE = (10, 9, 11, 6, 14, 2, 8, 5, 7, 13, 15, 1, 3, 4, 12)
SCALE = 100.0


def dot(a, b, ca=1, cb=0):
    return lax.dot_general(a, b, (((ca,), (cb,)), ((), ())), preferred_element_type=F32)


def iota(shape, axis):
    return lax.broadcasted_iota(jnp.int32, shape, axis)


def hot(mask):
    return jnp.where(mask, 1.0, 0.0).astype(BF16)


def split2(v):
    hi = v.astype(BF16)
    return hi, (v - hi.astype(F32)).astype(BF16)


def fold(v):
    m = v.shape[0] // 8
    v = v.reshape(m, 8, D)
    return jnp.concatenate([v[:, :, : D // 2], v[:, :, D // 2 :]], axis=1).reshape(16 * m, D // 2).astype(BF16)


def unfold(v):
    m = v.shape[0] // 16
    v = v.astype(F32).reshape(m, 16, D // 2)
    return jnp.concatenate([v[:, :8], v[:, 8:]], axis=2).reshape(8 * m, D)


def stack(v):
    return jnp.concatenate([v[:, :SP], v[:, SP:]], axis=0).astype(BF16)


def unstack(v):
    v = v.astype(F32)
    return jnp.concatenate([v[:24], v[24:]], axis=1)


def wrap(v):
    return lax.rem(v + 2 * R, R)


class Gather:
    def __init__(self, block, c1, c2, dev1, dev2, four, fifteen, sem, g):
        self.block, self.c1, self.c2 = block, c1, c2
        self.dev1, self.dev2, self.sem, self.g = dev1, dev2, sem, g
        self.four, self.fifteen = four, fifteen
        self.bs = [c1, wrap(c1 - 1), wrap(c1 + 1), wrap(c1 + 2)]

    def copy(self, k, ref, dev):
        return pltpu.make_async_remote_copy(
            src_ref=ref, dst_ref=ref, send_sem=self.sem.at[self.g, 12], recv_sem=self.sem.at[self.g, k],
            device_id=dev, device_id_type=MESH,
        )

    def got(self, k, ref):
        self.copy(k, ref, self.dev1(1)).wait_recv()
        return ref

    def at(self, a, b, half=None):
        return self.block(wrap(a), wrap(b), half)

    def second(self, i):
        ref = self.at(self.bs[i], self.c2)
        self.copy(3 + 2 * i, ref, self.dev2(1)).start()
        self.copy(4 + 2 * i, ref, self.dev2(-1)).start()

    def start(self):
        ref = self.at(self.c1, self.c2)
        self.copy(0, ref, self.dev1(1)).start()
        self.copy(1, ref, self.dev1(-1)).start()

    def stage1(self):
        c1, c2 = self.c1, self.c2
        self.got(0, self.at(c1 - 1, c2))
        self.copy(2, self.at(c1 - 1, c2, 0), self.dev1(1)).start()
        self.second(1)
        self.got(1, self.at(c1 + 1, c2))
        self.copy(2, self.at(c1 + 1, c2, 1), self.dev1(-1)).start()
        self.second(2)

    def stage2(self):
        self.got(2, self.at(self.c1 + 2, self.c2))
        self.second(3)

    def stage3(self, i):
        b, c2 = self.bs[i], self.c2
        self.got(3 + 2 * i, self.at(b, c2 - 1))
        self.copy(11, self.at(b, c2 - 1, 0), self.dev2(1)).start()
        self.got(4 + 2 * i, self.at(b, c2 + 1))
        self.copy(11, self.at(b, c2 + 1, 1), self.dev2(-1)).start()

    def stage4(self):
        self.got(11, self.four)

    def sent(self):
        self.copy(12, self.fifteen, self.dev1(1)).wait_send()


class Scatter:
    def __init__(self, block, c1, c2, dev1, dev2, halves, fulls, fifteen, sem, g):
        self.block, self.c1, self.c2 = block, c1, c2
        self.dev1, self.dev2, self.sem, self.g = dev1, dev2, sem, g
        self.halves, self.fulls, self.fifteen = halves.at[g], fulls.at[g], fifteen
        self.bs = [wrap(c2 + 2), wrap(c2 + 1), wrap(c2 - 1), c2]

    def copy(self, k, src, dst, dev):
        return pltpu.make_async_remote_copy(
            src_ref=src, dst_ref=dst, send_sem=self.sem.at[self.g, 15], recv_sem=self.sem.at[self.g, k],
            device_id=dev, device_id_type=MESH,
        )

    def got(self, k, ref):
        self.copy(k, ref, ref, self.dev1(1)).wait_recv()
        return ref

    def at(self, a, b, half=None):
        return self.block(wrap(a), wrap(b), half)

    def add(self, ref, *others):
        total = ref[...].astype(F32)
        for other in others:
            total = total + other[...].astype(F32)
        ref[...] = total.astype(BF16)

    def start(self):
        for i in range(4):
            self.copy(2 * i, self.at(self.c1 + 2, self.bs[i], 0), self.halves.at[i, 0], self.dev1(1)).start()
            self.copy(2 * i + 1, self.at(self.c1 + 2, self.bs[i], 1), self.halves.at[i, 1], self.dev1(-1)).start()

    def mid(self, i):
        b = self.bs[i]
        self.add(self.at(self.c1 + 1, b, 0), self.got(2 * i, self.halves.at[i, 0]))
        self.copy(8 + i, self.at(self.c1 + 1, b), self.fulls.at[i, 0], self.dev1(1)).start()
        self.add(self.at(self.c1 - 1, b, 1), self.got(2 * i + 1, self.halves.at[i, 1]))
        self.copy(8 + i, self.at(self.c1 - 1, b), self.fulls.at[i, 1], self.dev1(-1)).start()

    def end(self, i):
        c1, b = self.c1, self.bs[i]
        self.got(8 + i, self.fulls.at[i])
        first, second = self.fulls.at[i, 0], self.fulls.at[i, 1]
        if i == 0:
            self.add(self.at(c1, b), first, second)
            self.copy(12, self.at(c1, b, 0), self.halves.at[4, 0], self.dev2(1)).start()
            self.copy(13, self.at(c1, b, 1), self.halves.at[4, 1], self.dev2(-1)).start()
        elif i == 1:
            self.add(self.at(c1, b), first, second)
            self.add(self.at(c1, b, 0), self.got(12, self.halves.at[4, 0]))
            self.copy(14, self.at(c1, b), self.fulls.at[4, 0], self.dev2(1)).start()
        elif i == 2:
            self.add(self.at(c1, b), first, second)
            self.add(self.at(c1, b, 1), self.got(13, self.halves.at[4, 1]))
            self.copy(14, self.at(c1, b), self.fulls.at[4, 1], self.dev2(-1)).start()
        else:
            total = self.at(c1, b)[...].astype(F32) + first[...].astype(F32) + second[...].astype(F32)
            self.got(14, self.fulls.at[4])
            for k in (0, 1):
                total = total + self.fulls[4, k].astype(F32)
            return total

    def sent(self):
        self.copy(15, self.fifteen, self.fifteen, self.dev1(1)).wait_send()


def kernel(
    tok_in, ids_in, gate_in, gain_in, win_in, wout_in, img_in,
    tg, gg, dwin, dwout,
    tok, ids, gate, gain, win, wout, img, s_in,
    sel, vsend, v32, vcame, vback, vfinal, full_in, full_out, imgs, imgb,
    xsend, xr, xs, xt, pre, cdf, act, actt, out32,
    contrib, cjoin, csend, crecv, tall, rsum, rrecv, csum, ccrecv, tb, tbrecv, lb, ob, pb,
    ib, ibrecv, mixed, mixes, lball, gi, halves, fulls,
    ag_sem, rs_sem, pair_sem, pair2_sem,
    s_img, s_x, s_c, s_t, s_r, s_cc, s_tb, s_lb, s_ib, s_join, s_share, s_share2, s_m,
):
    dp, ex = lax.axis_index("dp"), lax.axis_index("expert")
    xy, h = dp // 2, lax.rem(dp, 2)
    y, x = xy // R, lax.rem(xy, R)
    j = 8 * h + ex

    def z_dev(q):
        return (2 * xy + q // 8, lax.rem(q, 8))

    def p_dev(k):
        return (2 * k + h, ex)

    chip, core = 4 * h + ex // 2, lax.rem(ex, 2)
    seat = 8 * core + chip

    def c_dev(k):
        return (2 * xy + k // 4, 2 * lax.rem(k, 4) + core)

    twin = (dp, ex + 1 - 2 * core)

    def x_dev(step):
        return p_dev(R * y + wrap(x + step))

    def y_dev(step):
        return p_dev(R * wrap(y + step) + x)

    class Exchange:
        def __init__(self, me, dev, src, dst, all_but_one, sem, size=N, order=None):
            self.me, self.dev, self.src, self.dst, self.sem = me, dev, src, dst, sem
            self.order = order
            self.all_but_one, self.size = all_but_one, size

        def copy(self, src, dst, to):
            return pltpu.make_async_remote_copy(
                src_ref=src, dst_ref=dst, send_sem=self.sem.at[0], recv_sem=self.sem.at[1],
                device_id=self.dev(to), device_id_type=MESH,
            )

        def start(self):
            def step(i, carry):
                to = lax.rem(self.me + i, self.size)
                self.copy(self.src(to), self.dst(self.me), to).start()
                return carry

            if self.order is None:
                lax.fori_loop(1, self.size, step, 0)
            else:
                for i in self.order:
                    step(i, 0)

        def wait(self):
            self.copy(self.all_but_one, self.all_but_one, lax.rem(self.me + 1, self.size)).wait_recv()

        def sent(self):
            self.copy(self.all_but_one, self.all_but_one, lax.rem(self.me + 1, self.size)).wait_send()

    def rows(ref, k, n):
        return ref.at[pl.ds(pl.multiple_of(k * n, n), n)]

    barrier = pltpu.get_barrier_semaphore()

    for k in range(N - 1):
        pl.semaphore_signal(barrier, inc=1, device_id=z_dev(lax.rem(j + RING[k], N)), device_id_type=MESH)
        pl.semaphore_signal(barrier, inc=1, device_id=p_dev(lax.rem(xy + PLANE[k], N)), device_id_type=MESH)

    loads = [
        pltpu.make_async_copy(src, dst, s_in.at[k])
        for k, (src, dst) in enumerate(
            zip((win_in, tok_in, ids_in, gate_in, gain_in, img_in, wout_in), (win, tok, ids, gate, gain, img, wout))
        )
    ]
    for load in loads:
        load.start()
    for load in loads:
        load.wait()
    rows(full_out, xy, RO)[...] = wout[...]
    source = iota((D, SP), 0)
    column = iota((D, SP), 1)
    spot = column + (column // RO) * RO
    sel[0] = hot(source == spot + RO * h)
    sel[1] = hot(source == spot + RO * (1 - h))
    mine, theirs = [], []
    for g in range(4):
        part = win[:, D * g : D * (g + 1)]
        mine.append(dot(part, sel[0]))
        theirs.append(dot(part, sel[1]))
    for k in (0, 1):
        vsend[k] = stack(jnp.concatenate(theirs[2 * k : 2 * k + 2], axis=1))
    for g in range(4):
        v32[pl.ds(pl.multiple_of(24 * h, 8), 24), SP * g : SP * (g + 1)] = mine[g]
    image = img[...].astype(F32)
    image = image * lax.rsqrt(jnp.sum(image * image, axis=1, keepdims=True) + EPS)
    rows(imgs, j, 16)[...] = fold(image)

    inputs = tok[...].astype(F32)
    centred = inputs - jnp.mean(inputs, axis=1, keepdims=True)
    inverse = lax.rsqrt(jnp.mean(centred * centred, axis=1, keepdims=True) + EPS)
    normed = (centred * inverse * gain[...].reshape(1, D)).astype(BF16)
    token_sum = jnp.sum(inputs.reshape(PAIR, TEXT, D), axis=1)

    chosen_row = jnp.broadcast_to(ids[...].astype(F32), (TOK, TOK))
    chosen = chosen_row.T[:, 0:1]
    lane = iota((TOK, TOK), 1).astype(F32)
    onehot = hot(lane == chosen)
    before = dot(hot(iota((TOK, TOK), 0) > iota((TOK, TOK), 1)), onehot)
    slot = jnp.sum(before * onehot.astype(F32), axis=1, keepdims=True)
    is_main = slot < 16.0
    is_extra = jnp.logical_and(slot >= 16.0, slot < float(CAP))
    main = hot(lane == jnp.where(is_main, 16.0 * chosen + slot, -1.0))
    extra = [hot(lane == jnp.where(is_extra, 16.0 * chosen + (4.0 * p - 16.0) + slot, -1.0)) for p in range(3)]
    at_slot = iota((TOK, 256), 1).astype(F32) == jnp.where(slot < float(CAP), slot, -1.0)

    xsend[:, :D] = dot(main.T, normed).astype(BF16)
    tail = dot(extra[0].T, normed[:, 0:256]) + dot(extra[1].T, normed[:, 256:512]) + dot(extra[2].T, normed[:, 512:768])
    gate_row = gate[...]
    gate1 = gate_row.astype(BF16).astype(F32)
    gate2 = (gate_row - gate1).astype(BF16).astype(F32)
    gate3 = gate_row - gate1 - gate2
    line = iota((TOK, TOK), 0)
    kind = lax.rem(line, 16)
    pair_row = (iota((TOK, TOK), 1) // TEXT).astype(F32)
    notes = jnp.where(kind == 12, gate1, jnp.where(kind == 13, gate2, jnp.where(kind == 14, gate3, jnp.where(kind == 15, pair_row, 0.0))))
    notes = jnp.where((line // 16).astype(F32) == chosen_row, notes, 0.0)
    xsend[:, D:] = (tail + dot(notes.astype(BF16), hot(at_slot))).astype(BF16)
    rows(xr, j, 16)[...] = rows(xsend, ex, 16)[...]

    pl.semaphore_wait(barrier, 2 * (N - 1))

    def out_at(buf, part):
        def block(xc, yc, half=None):
            row = pl.multiple_of((R * yc + xc) * RO + 48 * part, 16)
            if half is None:
                return buf.at[pl.ds(row, 48)]
            return buf.at[pl.ds(row, 48), pl.ds(SP * half, SP)]

        return block

    def in_at(buf, part):
        def block(xc, yc, half=None):
            row = pl.multiple_of((R * yc + xc) * RI, 16)
            if half is None:
                return buf.at[pl.ds(row, RI), pl.ds(D * part, D)]
            return buf.at[pl.ds(row, RI), pl.ds(D * part + SP * half, SP)]

        return block

    wide = pl.ds(pl.multiple_of(SP * core, TOK), SP)

    def back_at(buf, part):
        def block(xc, yc, half=None):
            row = pl.multiple_of((R * yc + xc) * TOK + 64 * part, 32)
            if half is None:
                return buf.at[pl.ds(row, 64), wide]
            return buf.at[pl.ds(pl.multiple_of(row + 32 * half, 32), 32), wide]

        return block

    def both(make, buf, at, first, *args):
        other_way = at(buf, 1)
        return (
            make(at(buf, 0), x, y, x_dev, y_dev, *args, first),
            make(lambda a, b, half=None: other_way(b, a, half), y, x, y_dev, x_dev, *args, first + 1),
        )

    fifteen = full_out.at[pl.ds(0, 15 * 48)]
    outs = both(Gather, full_out, out_at, 0, full_out.at[pl.ds(0, 192)], fifteen, ag_sem)
    ins = both(Gather, full_in, in_at, 2, full_in.at[pl.ds(0, 96)], fifteen, ag_sem)

    other = (2 * xy + 1 - h, ex)
    swaps = [
        pltpu.make_async_remote_copy(
            src_ref=vsend.at[k], dst_ref=vcame.at[k], send_sem=pair_sem.at[k], recv_sem=pair_sem.at[2 + k],
            device_id=other, device_id_type=MESH,
        )
        for k in (0, 1)
    ]
    for swap in swaps:
        swap.start()
    for part in outs:
        part.start()
    for part in outs:
        part.second(0)

    images = Exchange(j, z_dev, lambda q: rows(imgs, j, 16), lambda s: rows(imgs, s, 16), imgs.at[pl.ds(0, 240)], s_img)

    send_x = Exchange(j, z_dev, lambda q: rows(xsend, lax.rem(q, 8), 16), lambda s: rows(xr, s, 16), xr.at[pl.ds(0, 240)], s_x)

    for part in outs:
        part.stage1()
    for part in outs:
        part.stage2()
    for k in (0, 1):
        swaps[k].wait_recv()
        half = slice(D * k, D * (k + 1))
        v32[pl.ds(pl.multiple_of(24 * (1 - h), 8), 24), half] = unstack(vcame[k])
        rows(full_in, xy, RI).at[:, half][...] = v32[:, half].astype(BF16)
        ins[k].start()
        outs[k].stage3(0)
    for part in ins:
        part.second(0)
    send_x.start()
    images.start()
    for i in (1, 2):
        for part in outs:
            part.stage3(i)
    for part in ins:
        part.stage1()
    for part in outs:
        part.stage3(3)
    for part in ins:
        part.stage2()
    for i in range(4):
        for part in ins:
            part.stage3(i)

    send_x.wait()
    row64 = iota((64, 256), 0)
    lane64 = iota((64, 256), 1)
    picked = [hot(lane64 == 16 * (row64 // 4) + 4 * p + lax.rem(row64, 4)) for p in range(3)]
    xs[0:256, :] = xr[:, :D]
    for p in range(3):
        xs[256:SLOTS, 256 * p : 256 * (p + 1)] = dot(picked[p], xr[:, D:]).astype(BF16)
    xs[SLOTS:, :] = jnp.zeros((SP - SLOTS, D), BF16)
    xt[...] = xs[...].T
    slot_i = iota((SLOTS, 256), 0)
    lane_i = iota((SLOTS, 256), 1)
    slot_from = jnp.where(slot_i < 256, slot_i // 16, (slot_i - 256) // 4)
    slot_at = jnp.where(slot_i < 256, lax.rem(slot_i, 16), 16 + lax.rem(slot_i, 4))
    note_of = [hot(lane_i == 16 * slot_from + 12 + m) for m in range(4)]
    tails = xr[:, D:]
    own_lane = lane_i == slot_at
    gate_col = jnp.sum(jnp.where(own_lane, dot(note_of[0] + note_of[1] + note_of[2], tails), 0.0), axis=1, keepdims=True)
    pair_col = jnp.sum(jnp.where(own_lane, dot(note_of[3], tails), 0.0), axis=1, keepdims=True)
    first_pair = (PAIR * (8 * lax.rem(slot_from, 2) + slot_from // 2))[:, :TOK].astype(F32)
    pair_of = hot(lane_i[:, :TOK].astype(F32) == first_pair + pair_col)

    images.wait()
    imgb[...] = unfold(imgs[...]).astype(BF16)
    for part in ins:
        part.stage4()

    def chunk(n, size):
        return pl.ds(pl.multiple_of(n * size, size), size)

    def forward(n, carry):
        cols = chunk(n, 256)
        value = dot(xs[0:SLOTS, :], full_in[:, cols])
        bell = 0.5 * (1.0 + lax.erf(value * (0.5**0.5)))
        pre[:, cols] = value
        cdf[:, cols] = bell
        act[0:SLOTS, cols] = (value * bell).astype(BF16)
        return carry

    lax.fori_loop(0, HALF // 256, forward, 0)
    act[SLOTS:, :] = jnp.zeros((SP - SLOTS, HALF), BF16)
    for part in outs:
        part.stage4()

    def project(n, carry):
        cols = chunk(n, 256)
        out32[:, cols] = dot(act[0:SLOTS, :], full_out[:, cols])
        return carry

    lax.fori_loop(0, D // 256, project, 0)

    contrib[...] = fold(dot(pair_of, (gate_col * out32[...]).astype(BF16), 0, 0))
    join = pltpu.make_async_remote_copy(
        src_ref=rows(contrib, 1 - core, 128), dst_ref=cjoin, send_sem=s_join.at[0], recv_sem=s_join.at[1],
        device_id=twin, device_id_type=MESH,
    )
    join.start()
    join.wait_recv()
    joined = rows(contrib, core, 128)
    csend[...] = (joined[...].astype(F32) + cjoin[...].astype(F32)).astype(BF16)
    send_c = Exchange(
        chip, c_dev, lambda q: rows(csend, q, 16), lambda s: rows(crecv, s, 16), crecv.at[pl.ds(0, 112)], s_c, 8, LINE
    )
    send_c.start()
    rows(crecv, chip, 16)[...] = rows(csend, chip, 16)[...]

    actt[...] = act[...].T
    weight1, weight2 = split2(gate_col * pair_of.astype(F32))
    pad = jnp.zeros((SP - SLOTS, TOK), BF16)
    weight1 = jnp.concatenate([weight1, pad], axis=0)
    weight2 = jnp.concatenate([weight2, pad], axis=0)

    def mix(n, carry):
        part = actt[chunk(n, 256), :]
        mixed[chunk(n, 256), :] = (dot(part, weight1) + dot(part, weight2)).astype(BF16)
        return carry

    lax.fori_loop(0, HALF // 256, mix, 0)
    send_m = Exchange(
        xy, p_dev, lambda q: rows(mixed, q, RO), lambda s: mixes.at[s], mixes.at[pl.ds(0, N - 1)], s_m
    )

    def slope(n, carry):
        cols = chunk(n, 256)
        value = pre[:, cols]
        pre[:, cols] = cdf[:, cols] + value * (jnp.exp(-0.5 * value * value) * 0.3989422804014327)
        return carry

    send_c.wait()
    pooled = (token_sum + jnp.sum(unfold(crecv[...]).reshape(8, PAIR, D), axis=0)) * (1.0 / TEXT)
    q_inv = lax.rsqrt(jnp.sum(pooled * pooled, axis=1, keepdims=True) + EPS)
    unit = pooled * q_inv
    rows(tall, xy, 16)[...] = fold(unit)
    send_t = Exchange(xy, p_dev, lambda q: rows(tall, xy, 16), lambda s: rows(tall, s, 16), tall.at[pl.ds(0, 240)], s_t, N, PLANE)
    send_t.start()
    lax.fori_loop(0, 3, slope, 0)
    send_t.wait()

    scores = SCALE * dot(unfold(tall[...]).astype(BF16), imgb[...], 1, 1)
    exped = jnp.exp(scores)
    csum[...] = jnp.sum(exped, axis=0, keepdims=True)
    rsum[...] = jnp.sum(exped.T, axis=0, keepdims=True)
    send_r = Exchange(xy, p_dev, lambda q: rsum, lambda s: rrecv.at[s], rrecv.at[pl.ds(0, N - 1)], s_r, N, PLANE)
    send_cc = Exchange(j, z_dev, lambda q: csum, lambda s: ccrecv.at[s], ccrecv.at[pl.ds(0, N - 1)], s_cc, N, RING)
    send_cc.start()
    send_r.start()
    rrecv[pl.ds(xy, 1)] = rsum[...].reshape(1, 1, TOK)
    ccrecv[pl.ds(j, 1)] = csum[...].reshape(1, 1, TOK)
    text_at = iota((TOK, TOK), 0)
    image_at = iota((TOK, TOK), 1)
    diagonal = jnp.where(
        jnp.logical_and(image_at // PAIR == j, text_at == PAIR * xy + lax.rem(image_at, PAIR)), 1.0, 0.0
    )
    lax.fori_loop(3, 6, slope, 0)
    send_r.wait()
    send_cc.wait()
    row_total = jnp.broadcast_to(jnp.sum(rrecv[...], axis=0), (TOK, TOK)).T
    col_total = jnp.sum(ccrecv[...], axis=0)
    coefs = (0.5 * (exped / row_total + exped / col_total) - diagonal).astype(BF16)
    tb[...] = fold(SCALE * dot(coefs, imgb[...]))
    send_tb = Exchange(xy, p_dev, lambda q: rows(tb, q, 16), lambda s: rows(tbrecv, s, 16), tbrecv.at[pl.ds(0, 240)], s_tb, N, PLANE)
    send_tb.start()
    rows(tbrecv, xy, 16)[...] = rows(tb, xy, 16)[...]
    send_tb.wait()
    text_back = jnp.sum(unfold(tbrecv[...]).reshape(N, PAIR, D), axis=0)
    pooled_back = q_inv * (text_back - unit * jnp.sum(unit * text_back, axis=1, keepdims=True))
    layer_back = pooled_back * (1.0 / TEXT)
    rows(lb, seat, 16)[...] = fold(layer_back)
    send_lb = Exchange(
        chip, c_dev, lambda q: rows(lb, seat, 16), lambda s: rows(lb, 8 * core + s, 16), lb.at[pl.ds(0, 112)], s_lb, 8, LINE
    )
    send_lb.start()
    send_m.start()
    mixes[pl.ds(xy, 1)] = rows(mixed, xy, RO)[...].reshape(1, RO, TOK)
    send_lb.wait()
    ours = rows(lb, core, 128)
    share = pltpu.make_async_remote_copy(
        src_ref=ours, dst_ref=ours, send_sem=s_share.at[0], recv_sem=s_share.at[1], device_id=twin, device_id_type=MESH
    )
    share.start()
    share.wait_recv()

    pairs_back = unfold(lb[...]).astype(BF16)
    rows(lball, xy, TOK).at[:, wide][...] = jnp.where(core == 0, pairs_back[:, :SP], pairs_back[:, SP:])
    g_lbs = both(
        Gather, lball, back_at, 4, lball.at[pl.ds(0, 256), pl.ds(0, SP)], lball.at[pl.ds(0, 960), pl.ds(0, SP)], ag_sem
    )
    for part in g_lbs:
        part.start()
    for part in g_lbs:
        part.second(0)
    slot_back = dot(pair_of, pairs_back)
    ob[...] = (gate_col * slot_back).astype(BF16)
    pb[SLOTS:, :] = jnp.zeros((SP - SLOTS, HALF), BF16)

    def back(n, carry):
        cols = chunk(n, 256)
        act_back = dot(ob[...], full_out[cols, :], 1, 1)
        pb[0:SLOTS, cols] = (act_back * pre[:, cols]).astype(BF16)
        return carry

    def grad_in(k, step):
        spots = [(wrap(x + step), b) if k == 0 else (b, wrap(y + step)) for b in range(R)]
        starts = [pl.multiple_of((R * yc + xc) * RI, 16) for xc, yc in spots]
        left = jnp.concatenate([xt[pl.ds(at, RI), :] for at in starts], axis=0)
        value = dot(left, pb[:, D * k : D * (k + 1)]).astype(BF16)
        for b in range(R):
            gi[pl.ds(starts[b], RI), D * k : D * (k + 1)] = value[RI * b : RI * (b + 1)]

    s_ins = both(Scatter, gi, in_at, 0, halves, fulls, fifteen, rs_sem)
    for k in (0, 1):
        lax.fori_loop(3 * k, 3 * k + 3, back, 0)
        grad_in(k, 2)
        s_ins[k].start()
        for step in (1, -1, 0):
            grad_in(k, step)

    for part in g_lbs:
        part.stage1()
    extras = []
    for p in range(3):
        cols = slice(256 * p, 256 * (p + 1))
        in_back = dot(pb[0:SLOTS, :], full_in[cols, :], 1, 1).astype(BF16)
        ib[:, cols] = in_back[0:256]
        extras.append(in_back[256:SLOTS])
        if p < 2:
            for part in s_ins:
                part.mid(p)
    gate_back = jnp.sum(slot_back * out32[...], axis=1, keepdims=True)
    back1 = gate_back.astype(BF16).astype(F32)
    back2 = (gate_back - back1).astype(BF16).astype(F32)
    backs = [back1, back2, gate_back - back1 - back2]
    spread = jnp.zeros((256, 256), F32)
    for m in range(3):
        spread = spread + dot(note_of[m], jnp.where(own_lane, backs[m], 0.0).astype(BF16), 0, 0)
        spread = spread + dot(picked[m], extras[m], 0, 0)
    ib[:, D:] = spread.astype(BF16)
    send_ib = Exchange(
        j, z_dev, lambda q: rows(ib, q, 16), lambda s: rows(ibrecv, s, 16), ibrecv.at[pl.ds(0, 240)], s_ib
    )
    send_ib.start()
    rows(ibrecv, j, 16)[...] = rows(ib, j, 16)[...]
    for part in g_lbs:
        part.stage2()
    for i in (2, 3):
        for part in s_ins:
            part.mid(i)
    for i in range(3):
        for part in g_lbs:
            part.stage3(i)
        for part in s_ins:
            part.end(i)
    for part in g_lbs:
        part.stage3(3)
    swaps_back = []
    for k in (0, 1):
        half = slice(D * k, D * (k + 1))
        v32[:, half] = s_ins[k].end(3)
        vback[k] = stack(v32[pl.ds(pl.multiple_of(24 * (1 - h), 8), 24), half])
        swap = pltpu.make_async_remote_copy(
            src_ref=vback.at[k], dst_ref=vfinal.at[k], send_sem=pair2_sem.at[k], recv_sem=pair2_sem.at[2 + k],
            device_id=other, device_id_type=MESH,
        )
        swap.start()
        swaps_back.append(swap)
    for part in g_lbs:
        part.stage4()
    ours = lball.at[:, wide]
    share2 = pltpu.make_async_remote_copy(
        src_ref=ours, dst_ref=ours, send_sem=s_share2.at[0], recv_sem=s_share2.at[1], device_id=twin, device_id_type=MESH
    )
    share2.start()

    send_ib.wait()
    inputs = tok[...].astype(F32)
    centred = inputs - jnp.mean(inputs, axis=1, keepdims=True)
    inverse = lax.rsqrt(jnp.mean(centred * centred, axis=1, keepdims=True) + EPS)
    scaled = centred * inverse
    back_main = dot(jnp.concatenate([main, main], axis=1), ibrecv[:, :D])
    back_tail = [dot(jnp.concatenate([e, e], axis=1), ibrecv[:, D:]) for e in extra]
    normed_back = back_main + jnp.concatenate(back_tail, axis=1)
    gained = normed_back * gain[...].reshape(1, D)
    repeated = jnp.broadcast_to(layer_back.reshape(PAIR, 1, D), (PAIR, TEXT, D)).reshape(TOK, D)
    tg[...] = (
        repeated
        + inverse * (gained - jnp.mean(gained, axis=1, keepdims=True) - scaled * jnp.mean(gained * scaled, axis=1, keepdims=True))
    ).astype(BF16)
    row_i = iota((TOK, 256), 1)
    kind = lax.rem(row_i, 16)
    owner = jnp.logical_and(jnp.logical_and(kind >= 12, kind < 15), lax.rem(row_i // 16, 8).astype(F32) == chosen)
    gathered = dot(hot(owner), ibrecv[:, D:])
    token_gate = jnp.sum(jnp.where(at_slot, gathered, 0.0), axis=1, keepdims=True)
    gg[...] = jnp.broadcast_to(token_gate, (TOK, TOK)).T[0:1]

    send_m.wait()
    factors = jnp.concatenate([mixes[k] for k in range(N)], axis=1)
    dwout[:, wide] = dot(factors, lball[:, wide])
    share2.wait_recv()
    rest = pl.ds(pl.multiple_of(SP * (1 - core), TOK), SP)
    dwout[:, rest] = dot(factors, lball[:, rest])
    kept = v32[pl.ds(pl.multiple_of(24 * h, 8), 24), :]
    held = []
    for g in range(4):
        hi, lo = split2(kept[:, SP * g : SP * (g + 1)])
        held.append(dot(hi, sel[0], 1, 1) + dot(lo, sel[0], 1, 1))
    for k in (0, 1):
        swaps_back[k].wait_recv()
        came = unstack(vfinal[k])
        for g in (0, 1):
            at = D * (2 * k + g)
            dwin[:, at : at + D] = held[2 * k + g] + dot(came[:, SP * g : SP * (g + 1)].astype(BF16), sel[1], 1, 1)

    for swap in swaps + swaps_back:
        swap.wait_send()
    join.wait_send()
    share.wait_send()
    share2.wait_send()
    for part in outs + ins + g_lbs + s_ins:
        part.sent()
    for exchange in (images, send_x, send_c, send_m, send_t, send_r, send_cc, send_tb, send_lb, send_ib):
        exchange.sent()


def hand_on(*refs):
    for k in range(4):
        refs[4 + k][...] = refs[k][...]


def body(tokens, expert_ids, gate, ln_gain, w_in, w_out, image_emb):
    vmem = pl.BlockSpec(memory_space=pltpu.VMEM)
    f32 = lambda *shape: pltpu.VMEM(shape, F32)
    b16 = lambda *shape: pltpu.VMEM(shape, BF16)
    sems = lambda *shape: pltpu.SemaphoreType.DMA(shape)
    token_grad, gate_grad, in_grad, out_grad = pl.pallas_call(
        kernel,
        out_shape=(
            jax.ShapeDtypeStruct((TOK, D), BF16),
            jax.ShapeDtypeStruct((1, TOK), F32),
            jax.ShapeDtypeStruct((24, H), F32),
            jax.ShapeDtypeStruct((RO, D), F32),
        ),
        in_specs=[pl.BlockSpec(memory_space=pl.ANY)] * 7,
        out_specs=(vmem,) * 4,
        scratch_shapes=[
            b16(TOK, D),
            pltpu.VMEM((1, TOK), jnp.int32),
            f32(1, TOK),
            f32(D),
            b16(24, H),
            b16(RO, D),
            b16(PAIR, D),
            sems(7),
            b16(2, D, SP),
            b16(2, 48, SP),
            f32(RI, HALF),
            b16(2, 48, SP),
            b16(2, 48, SP),
            b16(2, 48, SP),
            b16(D, HALF),
            b16(HALF, D),
            b16(256, D // 2),
            b16(TOK, D),
            b16(TOK, 1024),
            b16(256, 1024),
            b16(SP, D),
            b16(D, SP),
            f32(SLOTS, HALF),
            f32(SLOTS, HALF),
            b16(SP, HALF),
            b16(HALF, SP),
            f32(SLOTS, D),
            b16(256, D // 2),
            b16(128, D // 2),
            b16(128, D // 2),
            b16(128, D // 2),
            b16(256, D // 2),
            f32(1, TOK),
            f32(N, 1, TOK),
            f32(1, TOK),
            f32(N, 1, TOK),
            b16(256, D // 2),
            b16(256, D // 2),
            b16(256, D // 2),
            b16(SLOTS, D),
            b16(SP, HALF),
            b16(256, 1024),
            b16(256, 1024),
            b16(HALF, TOK),
            b16(N, RO, TOK),
            b16(N * TOK, D),
            b16(D, HALF),
            b16(2, 5, 2, 48, SP),
            b16(2, 5, 2, 48, D),
            sems(6, 13),
            sems(2, 16),
            sems(4),
            sems(4),
        ]
        + [sems(2)] * 13,
        compiler_params=pltpu.CompilerParams(
            collective_id=0, has_side_effects=True, vmem_limit_bytes=56 * 1024 * 1024
        ),
        cost_estimate=pl.CostEstimate(flops=5_000_000_000, bytes_accessed=2_000_000, transcendentals=1_000_000),
    )(tokens, expert_ids.reshape(1, TOK), gate.reshape(1, TOK), ln_gain, w_in[0], w_out[0], image_emb)
    results = (token_grad, gate_grad, in_grad, out_grad)
    token_grad, gate_grad, in_grad, out_grad = pl.pallas_call(
        hand_on,
        out_shape=tuple(jax.ShapeDtypeStruct(r.shape, r.dtype) for r in results),
        in_specs=[vmem] * 4,
        out_specs=(vmem,) * 4,
    )(*results)
    return token_grad, gate_grad.reshape(TOK), in_grad[None], out_grad[None]


def solution(mesh):
    in_specs = (
        P(("dp", "expert"), None),
        P(("dp", "expert"), None),
        P(("dp", "expert")),
        P(),
        P("expert", "dp", None),
        P("expert", "dp", None),
        P(("dp", "expert"), None),
    )
    out_specs = (
        P(("dp", "expert"), None),
        P(("dp", "expert")),
        P("expert", "dp", None),
        P("expert", "dp", None),
    )
    return jax.shard_map(body, mesh=mesh, in_specs=in_specs, out_specs=out_specs, check_vma=False)
```

```python
import jax
import jax.numpy as jnp
from jax import lax
from jax.experimental import pallas as pl
from jax.experimental.pallas import tpu as pltpu
from jax.sharding import PartitionSpec as P

MESH = pl.DeviceIdType.MESH
F32 = jnp.float32
BF16 = jnp.bfloat16

D = 768
H = 3072
HALF = 1536
TOK = 128
CAP = 20
PAIR = 8
TEXT = 16
N = 16
R = 4
RO = 96
RI = 48
SLOTS = 320
SP = 384
EPS = 1e-6
LINE = (4, 3, 5, 2, 6, 1, 7)
RING = (8, 9, 7, 6, 10, 5, 11, 4, 12, 3, 13, 2, 14, 1, 15)
PLANE = (10, 9, 11, 6, 14, 2, 8, 5, 7, 13, 15, 1, 3, 4, 12)
SCALE = 100.0


def dot(a, b, ca=1, cb=0):
    return lax.dot_general(a, b, (((ca,), (cb,)), ((), ())), preferred_element_type=F32)


def iota(shape, axis):
    return lax.broadcasted_iota(jnp.int32, shape, axis)


def hot(mask):
    return jnp.where(mask, 1.0, 0.0).astype(BF16)


def split2(v):
    hi = v.astype(BF16)
    return hi, (v - hi.astype(F32)).astype(BF16)


def fold(v):
    m = v.shape[0] // 8
    v = v.reshape(m, 8, D)
    return jnp.concatenate([v[:, :, : D // 2], v[:, :, D // 2 :]], axis=1).reshape(16 * m, D // 2).astype(BF16)


def unfold(v):
    m = v.shape[0] // 16
    v = v.astype(F32).reshape(m, 16, D // 2)
    return jnp.concatenate([v[:, :8], v[:, 8:]], axis=2).reshape(8 * m, D)


def stack(v):
    return jnp.concatenate([v[:, :SP], v[:, SP:]], axis=0).astype(BF16)


def unstack(v):
    v = v.astype(F32)
    return jnp.concatenate([v[:24], v[24:]], axis=1)


def wrap(v):
    return lax.rem(v + 2 * R, R)


class Gather:
    def __init__(self, block, c1, c2, dev1, dev2, four, fifteen, sem, g):
        self.block, self.c1, self.c2 = block, c1, c2
        self.dev1, self.dev2, self.sem, self.g = dev1, dev2, sem, g
        self.four, self.fifteen = four, fifteen
        self.bs = [c1, wrap(c1 - 1), wrap(c1 + 1), wrap(c1 + 2)]

    def copy(self, k, ref, dev):
        return pltpu.make_async_remote_copy(
            src_ref=ref, dst_ref=ref, send_sem=self.sem.at[self.g, 12], recv_sem=self.sem.at[self.g, k],
            device_id=dev, device_id_type=MESH,
        )

    def got(self, k, ref):
        self.copy(k, ref, self.dev1(1)).wait_recv()
        return ref

    def at(self, a, b, half=None):
        return self.block(wrap(a), wrap(b), half)

    def second(self, i):
        ref = self.at(self.bs[i], self.c2)
        self.copy(3 + 2 * i, ref, self.dev2(1)).start()
        self.copy(4 + 2 * i, ref, self.dev2(-1)).start()

    def start(self):
        ref = self.at(self.c1, self.c2)
        self.copy(0, ref, self.dev1(1)).start()
        self.copy(1, ref, self.dev1(-1)).start()

    def stage1(self):
        c1, c2 = self.c1, self.c2
        self.got(0, self.at(c1 - 1, c2))
        self.copy(2, self.at(c1 - 1, c2, 0), self.dev1(1)).start()
        self.second(1)
        self.got(1, self.at(c1 + 1, c2))
        self.copy(2, self.at(c1 + 1, c2, 1), self.dev1(-1)).start()
        self.second(2)

    def stage2(self):
        self.got(2, self.at(self.c1 + 2, self.c2))
        self.second(3)

    def stage3(self, i):
        b, c2 = self.bs[i], self.c2
        self.got(3 + 2 * i, self.at(b, c2 - 1))
        self.copy(11, self.at(b, c2 - 1, 0), self.dev2(1)).start()
        self.got(4 + 2 * i, self.at(b, c2 + 1))
        self.copy(11, self.at(b, c2 + 1, 1), self.dev2(-1)).start()

    def stage4(self):
        self.got(11, self.four)

    def sent(self):
        self.copy(12, self.fifteen, self.dev1(1)).wait_send()


class Scatter:
    def __init__(self, block, c1, c2, dev1, dev2, halves, fulls, fifteen, sem, g):
        self.block, self.c1, self.c2 = block, c1, c2
        self.dev1, self.dev2, self.sem, self.g = dev1, dev2, sem, g
        self.halves, self.fulls, self.fifteen = halves.at[g], fulls.at[g], fifteen
        self.bs = [wrap(c2 + 2), wrap(c2 + 1), wrap(c2 - 1), c2]

    def copy(self, k, src, dst, dev):
        return pltpu.make_async_remote_copy(
            src_ref=src, dst_ref=dst, send_sem=self.sem.at[self.g, 15], recv_sem=self.sem.at[self.g, k],
            device_id=dev, device_id_type=MESH,
        )

    def got(self, k, ref):
        self.copy(k, ref, ref, self.dev1(1)).wait_recv()
        return ref

    def at(self, a, b, half=None):
        return self.block(wrap(a), wrap(b), half)

    def add(self, ref, *others):
        total = ref[...].astype(F32)
        for other in others:
            total = total + other[...].astype(F32)
        ref[...] = total.astype(BF16)

    def start(self):
        for i in range(4):
            self.copy(2 * i, self.at(self.c1 + 2, self.bs[i], 0), self.halves.at[i, 0], self.dev1(1)).start()
            self.copy(2 * i + 1, self.at(self.c1 + 2, self.bs[i], 1), self.halves.at[i, 1], self.dev1(-1)).start()

    def mid(self, i):
        b = self.bs[i]
        self.add(self.at(self.c1 + 1, b, 0), self.got(2 * i, self.halves.at[i, 0]))
        self.copy(8 + i, self.at(self.c1 + 1, b), self.fulls.at[i, 0], self.dev1(1)).start()
        self.add(self.at(self.c1 - 1, b, 1), self.got(2 * i + 1, self.halves.at[i, 1]))
        self.copy(8 + i, self.at(self.c1 - 1, b), self.fulls.at[i, 1], self.dev1(-1)).start()

    def end(self, i):
        c1, b = self.c1, self.bs[i]
        self.got(8 + i, self.fulls.at[i])
        first, second = self.fulls.at[i, 0], self.fulls.at[i, 1]
        if i == 0:
            self.add(self.at(c1, b), first, second)
            self.copy(12, self.at(c1, b, 0), self.halves.at[4, 0], self.dev2(1)).start()
            self.copy(13, self.at(c1, b, 1), self.halves.at[4, 1], self.dev2(-1)).start()
        elif i == 1:
            self.add(self.at(c1, b), first, second)
            self.add(self.at(c1, b, 0), self.got(12, self.halves.at[4, 0]))
            self.copy(14, self.at(c1, b), self.fulls.at[4, 0], self.dev2(1)).start()
        elif i == 2:
            self.add(self.at(c1, b), first, second)
            self.add(self.at(c1, b, 1), self.got(13, self.halves.at[4, 1]))
            self.copy(14, self.at(c1, b), self.fulls.at[4, 1], self.dev2(-1)).start()
        else:
            total = self.at(c1, b)[...].astype(F32) + first[...].astype(F32) + second[...].astype(F32)
            self.got(14, self.fulls.at[4])
            for k in (0, 1):
                total = total + self.fulls[4, k].astype(F32)
            return total

    def sent(self):
        self.copy(15, self.fifteen, self.fifteen, self.dev1(1)).wait_send()


def kernel(
    tok_in, ids_in, gate_in, gain_in, win_in, wout_in, img_in,
    tg, gg, dwin, dwout,
    tok, ids, gate, gain, win, wout, img, s_in,
    sel, vsend, v32, vcame, vback, vfinal, full_in, full_out, imgs, imgb,
    xsend, xr, xs, xt, pre, cdf, act, actt, out32,
    contrib, cjoin, csend, crecv, tall, rsum, rrecv, csum, ccrecv, tb, tbrecv, lb, ob, pb,
    ib, ibrecv, mixed, mixes, lball, gi, halves, fulls,
    ag_sem, rs_sem, pair_sem, pair2_sem,
    s_img, s_x, s_c, s_t, s_r, s_cc, s_tb, s_lb, s_ib, s_join, s_share, s_share2, s_m,
):
    dp, ex = lax.axis_index("dp"), lax.axis_index("expert")
    xy, h = dp // 2, lax.rem(dp, 2)
    y, x = xy // R, lax.rem(xy, R)
    j = 8 * h + ex

    def z_dev(q):
        return (2 * xy + q // 8, lax.rem(q, 8))

    def p_dev(k):
        return (2 * k + h, ex)

    chip, core = 4 * h + ex // 2, lax.rem(ex, 2)
    seat = 8 * core + chip

    def c_dev(k):
        return (2 * xy + k // 4, 2 * lax.rem(k, 4) + core)

    twin = (dp, ex + 1 - 2 * core)

    def x_dev(step):
        return p_dev(R * y + wrap(x + step))

    def y_dev(step):
        return p_dev(R * wrap(y + step) + x)

    class Exchange:
        def __init__(self, me, dev, src, dst, all_but_one, sem, size=N, order=None):
            self.me, self.dev, self.src, self.dst, self.sem = me, dev, src, dst, sem
            self.order = order
            self.all_but_one, self.size = all_but_one, size

        def copy(self, src, dst, to):
            return pltpu.make_async_remote_copy(
                src_ref=src, dst_ref=dst, send_sem=self.sem.at[0], recv_sem=self.sem.at[1],
                device_id=self.dev(to), device_id_type=MESH,
            )

        def start(self):
            def step(i, carry):
                to = lax.rem(self.me + i, self.size)
                self.copy(self.src(to), self.dst(self.me), to).start()
                return carry

            if self.order is None:
                lax.fori_loop(1, self.size, step, 0)
            else:
                for i in self.order:
                    step(i, 0)

        def wait(self):
            self.copy(self.all_but_one, self.all_but_one, lax.rem(self.me + 1, self.size)).wait_recv()

        def sent(self):
            self.copy(self.all_but_one, self.all_but_one, lax.rem(self.me + 1, self.size)).wait_send()

    def rows(ref, k, n):
        return ref.at[pl.ds(pl.multiple_of(k * n, n), n)]

    barrier = pltpu.get_barrier_semaphore()

    for k in range(N - 1):
        pl.semaphore_signal(barrier, inc=1, device_id=z_dev(lax.rem(j + RING[k], N)), device_id_type=MESH)
        pl.semaphore_signal(barrier, inc=1, device_id=p_dev(lax.rem(xy + PLANE[k], N)), device_id_type=MESH)

    loads = [
        pltpu.make_async_copy(src, dst, s_in.at[k])
        for k, (src, dst) in enumerate(
            zip((win_in, tok_in, ids_in, gate_in, gain_in, img_in, wout_in), (win, tok, ids, gate, gain, img, wout))
        )
    ]
    for load in loads:
        load.start()
    for load in loads:
        load.wait()
    rows(full_out, xy, RO)[...] = wout[...]
    source = iota((D, SP), 0)
    column = iota((D, SP), 1)
    spot = column + (column // RO) * RO
    sel[0] = hot(source == spot + RO * h)
    sel[1] = hot(source == spot + RO * (1 - h))
    mine, theirs = [], []
    for g in range(4):
        part = win[:, D * g : D * (g + 1)]
        mine.append(dot(part, sel[0]))
        theirs.append(dot(part, sel[1]))
    for k in (0, 1):
        vsend[k] = stack(jnp.concatenate(theirs[2 * k : 2 * k + 2], axis=1))
    for g in range(4):
        v32[pl.ds(pl.multiple_of(24 * h, 8), 24), SP * g : SP * (g + 1)] = mine[g]
    image = img[...].astype(F32)
    image = image * lax.rsqrt(jnp.sum(image * image, axis=1, keepdims=True) + EPS)
    rows(imgs, j, 16)[...] = fold(image)

    inputs = tok[...].astype(F32)
    centred = inputs - jnp.mean(inputs, axis=1, keepdims=True)
    inverse = lax.rsqrt(jnp.mean(centred * centred, axis=1, keepdims=True) + EPS)
    normed = (centred * inverse * gain[...].reshape(1, D)).astype(BF16)
    token_sum = jnp.sum(inputs.reshape(PAIR, TEXT, D), axis=1)

    chosen_row = jnp.broadcast_to(ids[...].astype(F32), (TOK, TOK))
    chosen = chosen_row.T[:, 0:1]
    lane = iota((TOK, TOK), 1).astype(F32)
    onehot = hot(lane == chosen)
    before = dot(hot(iota((TOK, TOK), 0) > iota((TOK, TOK), 1)), onehot)
    slot = jnp.sum(before * onehot.astype(F32), axis=1, keepdims=True)
    is_main = slot < 16.0
    is_extra = jnp.logical_and(slot >= 16.0, slot < float(CAP))
    main = hot(lane == jnp.where(is_main, 16.0 * chosen + slot, -1.0))
    extra = [hot(lane == jnp.where(is_extra, 16.0 * chosen + (4.0 * p - 16.0) + slot, -1.0)) for p in range(3)]
    at_slot = iota((TOK, 256), 1).astype(F32) == jnp.where(slot < float(CAP), slot, -1.0)

    xsend[:, :D] = dot(main.T, normed).astype(BF16)
    tail = dot(extra[0].T, normed[:, 0:256]) + dot(extra[1].T, normed[:, 256:512]) + dot(extra[2].T, normed[:, 512:768])
    gate_row = gate[...]
    gate1 = gate_row.astype(BF16).astype(F32)
    gate2 = (gate_row - gate1).astype(BF16).astype(F32)
    gate3 = gate_row - gate1 - gate2
    line = iota((TOK, TOK), 0)
    kind = lax.rem(line, 16)
    pair_row = (iota((TOK, TOK), 1) // TEXT).astype(F32)
    notes = jnp.where(kind == 12, gate1, jnp.where(kind == 13, gate2, jnp.where(kind == 14, gate3, jnp.where(kind == 15, pair_row, 0.0))))
    notes = jnp.where((line // 16).astype(F32) == chosen_row, notes, 0.0)
    xsend[:, D:] = (tail + dot(notes.astype(BF16), hot(at_slot))).astype(BF16)
    rows(xr, j, 16)[...] = rows(xsend, ex, 16)[...]

    pl.semaphore_wait(barrier, 2 * (N - 1))

    def out_at(buf, part):
        def block(xc, yc, half=None):
            row = pl.multiple_of((R * yc + xc) * RO + 48 * part, 16)
            if half is None:
                return buf.at[pl.ds(row, 48)]
            return buf.at[pl.ds(row, 48), pl.ds(SP * half, SP)]

        return block

    def in_at(buf, part):
        def block(xc, yc, half=None):
            row = pl.multiple_of((R * yc + xc) * RI, 16)
            if half is None:
                return buf.at[pl.ds(row, RI), pl.ds(D * part, D)]
            return buf.at[pl.ds(row, RI), pl.ds(D * part + SP * half, SP)]

        return block

    wide = pl.ds(pl.multiple_of(SP * core, TOK), SP)

    def back_at(buf, part):
        def block(xc, yc, half=None):
            row = pl.multiple_of((R * yc + xc) * TOK + 64 * part, 32)
            if half is None:
                return buf.at[pl.ds(row, 64), wide]
            return buf.at[pl.ds(pl.multiple_of(row + 32 * half, 32), 32), wide]

        return block

    def both(make, buf, at, first, *args):
        other_way = at(buf, 1)
        return (
            make(at(buf, 0), x, y, x_dev, y_dev, *args, first),
            make(lambda a, b, half=None: other_way(b, a, half), y, x, y_dev, x_dev, *args, first + 1),
        )

    fifteen = full_out.at[pl.ds(0, 15 * 48)]
    outs = both(Gather, full_out, out_at, 0, full_out.at[pl.ds(0, 192)], fifteen, ag_sem)
    ins = both(Gather, full_in, in_at, 2, full_in.at[pl.ds(0, 96)], fifteen, ag_sem)

    other = (2 * xy + 1 - h, ex)
    swaps = [
        pltpu.make_async_remote_copy(
            src_ref=vsend.at[k], dst_ref=vcame.at[k], send_sem=pair_sem.at[k], recv_sem=pair_sem.at[2 + k],
            device_id=other, device_id_type=MESH,
        )
        for k in (0, 1)
    ]
    for swap in swaps:
        swap.start()
    for part in outs:
        part.start()
    for part in outs:
        part.second(0)

    images = Exchange(j, z_dev, lambda q: rows(imgs, j, 16), lambda s: rows(imgs, s, 16), imgs.at[pl.ds(0, 240)], s_img)

    send_x = Exchange(j, z_dev, lambda q: rows(xsend, lax.rem(q, 8), 16), lambda s: rows(xr, s, 16), xr.at[pl.ds(0, 240)], s_x)

    for part in outs:
        part.stage1()
    for part in outs:
        part.stage2()
    for k in (0, 1):
        swaps[k].wait_recv()
        half = slice(D * k, D * (k + 1))
        v32[pl.ds(pl.multiple_of(24 * (1 - h), 8), 24), half] = unstack(vcame[k])
        rows(full_in, xy, RI).at[:, half][...] = v32[:, half].astype(BF16)
        ins[k].start()
        outs[k].stage3(0)
    for part in ins:
        part.second(0)
    send_x.start()
    images.start()
    for i in (1, 2):
        for part in outs:
            part.stage3(i)
    for part in ins:
        part.stage1()
    for part in outs:
        part.stage3(3)
    for part in ins:
        part.stage2()
    for i in range(4):
        for part in ins:
            part.stage3(i)

    send_x.wait()
    row64 = iota((64, 256), 0)
    lane64 = iota((64, 256), 1)
    picked = [hot(lane64 == 16 * (row64 // 4) + 4 * p + lax.rem(row64, 4)) for p in range(3)]
    xs[0:256, :] = xr[:, :D]
    for p in range(3):
        xs[256:SLOTS, 256 * p : 256 * (p + 1)] = dot(picked[p], xr[:, D:]).astype(BF16)
    xs[SLOTS:, :] = jnp.zeros((SP - SLOTS, D), BF16)
    xt[...] = xs[...].T
    slot_i = iota((SLOTS, 256), 0)
    lane_i = iota((SLOTS, 256), 1)
    slot_from = jnp.where(slot_i < 256, slot_i // 16, (slot_i - 256) // 4)
    slot_at = jnp.where(slot_i < 256, lax.rem(slot_i, 16), 16 + lax.rem(slot_i, 4))
    note_of = [hot(lane_i == 16 * slot_from + 12 + m) for m in range(4)]
    tails = xr[:, D:]
    own_lane = lane_i == slot_at
    gate_col = jnp.sum(jnp.where(own_lane, dot(note_of[0] + note_of[1] + note_of[2], tails), 0.0), axis=1, keepdims=True)
    pair_col = jnp.sum(jnp.where(own_lane, dot(note_of[3], tails), 0.0), axis=1, keepdims=True)
    first_pair = (PAIR * (8 * lax.rem(slot_from, 2) + slot_from // 2))[:, :TOK].astype(F32)
    pair_of = hot(lane_i[:, :TOK].astype(F32) == first_pair + pair_col)

    images.wait()
    imgb[...] = unfold(imgs[...]).astype(BF16)
    for part in ins:
        part.stage4()

    def chunk(n, size):
        return pl.ds(pl.multiple_of(n * size, size), size)

    def forward(n, carry):
        cols = chunk(n, 256)
        value = dot(xs[0:SLOTS, :], full_in[:, cols])
        bell = 0.5 * (1.0 + lax.erf(value * (0.5**0.5)))
        pre[:, cols] = value
        cdf[:, cols] = bell
        act[0:SLOTS, cols] = (value * bell).astype(BF16)
        return carry

    lax.fori_loop(0, HALF // 256, forward, 0)
    act[SLOTS:, :] = jnp.zeros((SP - SLOTS, HALF), BF16)
    for part in outs:
        part.stage4()

    def project(n, carry):
        cols = chunk(n, 256)
        out32[:, cols] = dot(act[0:SLOTS, :], full_out[:, cols])
        return carry

    lax.fori_loop(0, D // 256, project, 0)

    contrib[...] = fold(dot(pair_of, (gate_col * out32[...]).astype(BF16), 0, 0))
    join = pltpu.make_async_remote_copy(
        src_ref=rows(contrib, 1 - core, 128), dst_ref=cjoin, send_sem=s_join.at[0], recv_sem=s_join.at[1],
        device_id=twin, device_id_type=MESH,
    )
    join.start()
    join.wait_recv()
    joined = rows(contrib, core, 128)
    csend[...] = (joined[...].astype(F32) + cjoin[...].astype(F32)).astype(BF16)
    send_c = Exchange(
        chip, c_dev, lambda q: rows(csend, q, 16), lambda s: rows(crecv, s, 16), crecv.at[pl.ds(0, 112)], s_c, 8, LINE
    )
    send_c.start()
    rows(crecv, chip, 16)[...] = rows(csend, chip, 16)[...]

    actt[...] = act[...].T
    weight1, weight2 = split2(gate_col * pair_of.astype(F32))
    pad = jnp.zeros((SP - SLOTS, TOK), BF16)
    weight1 = jnp.concatenate([weight1, pad], axis=0)
    weight2 = jnp.concatenate([weight2, pad], axis=0)

    def mix(n, carry):
        part = actt[chunk(n, 256), :]
        mixed[chunk(n, 256), :] = (dot(part, weight1) + dot(part, weight2)).astype(BF16)
        return carry

    lax.fori_loop(0, HALF // 256, mix, 0)
    send_m = Exchange(
        xy, p_dev, lambda q: rows(mixed, q, RO), lambda s: mixes.at[s], mixes.at[pl.ds(0, N - 1)], s_m
    )

    def slope(n, carry):
        cols = chunk(n, 256)
        value = pre[:, cols]
        pre[:, cols] = cdf[:, cols] + value * (jnp.exp(-0.5 * value * value) * 0.3989422804014327)
        return carry

    send_c.wait()
    pooled = (token_sum + jnp.sum(unfold(crecv[...]).reshape(8, PAIR, D), axis=0)) * (1.0 / TEXT)
    q_inv = lax.rsqrt(jnp.sum(pooled * pooled, axis=1, keepdims=True) + EPS)
    unit = pooled * q_inv
    rows(tall, xy, 16)[...] = fold(unit)
    send_t = Exchange(xy, p_dev, lambda q: rows(tall, xy, 16), lambda s: rows(tall, s, 16), tall.at[pl.ds(0, 240)], s_t, N, PLANE)
    send_t.start()
    lax.fori_loop(0, 3, slope, 0)
    send_t.wait()

    scores = SCALE * dot(unfold(tall[...]).astype(BF16), imgb[...], 1, 1)
    exped = jnp.exp(scores)
    csum[...] = jnp.sum(exped, axis=0, keepdims=True)
    rsum[...] = jnp.sum(exped.T, axis=0, keepdims=True)
    send_r = Exchange(xy, p_dev, lambda q: rsum, lambda s: rrecv.at[s], rrecv.at[pl.ds(0, N - 1)], s_r, N, PLANE)
    send_cc = Exchange(j, z_dev, lambda q: csum, lambda s: ccrecv.at[s], ccrecv.at[pl.ds(0, N - 1)], s_cc, N, RING)
    send_cc.start()
    send_r.start()
    rrecv[pl.ds(xy, 1)] = rsum[...].reshape(1, 1, TOK)
    ccrecv[pl.ds(j, 1)] = csum[...].reshape(1, 1, TOK)
    text_at = iota((TOK, TOK), 0)
    image_at = iota((TOK, TOK), 1)
    diagonal = jnp.where(
        jnp.logical_and(image_at // PAIR == j, text_at == PAIR * xy + lax.rem(image_at, PAIR)), 1.0, 0.0
    )
    lax.fori_loop(3, 6, slope, 0)
    send_r.wait()
    send_cc.wait()
    row_total = jnp.broadcast_to(jnp.sum(rrecv[...], axis=0), (TOK, TOK)).T
    col_total = jnp.sum(ccrecv[...], axis=0)
    coefs = (0.5 * (exped / row_total + exped / col_total) - diagonal).astype(BF16)
    tb[...] = fold(SCALE * dot(coefs, imgb[...]))
    send_tb = Exchange(xy, p_dev, lambda q: rows(tb, q, 16), lambda s: rows(tbrecv, s, 16), tbrecv.at[pl.ds(0, 240)], s_tb, N, PLANE)
    send_tb.start()
    rows(tbrecv, xy, 16)[...] = rows(tb, xy, 16)[...]
    send_tb.wait()
    text_back = jnp.sum(unfold(tbrecv[...]).reshape(N, PAIR, D), axis=0)
    pooled_back = q_inv * (text_back - unit * jnp.sum(unit * text_back, axis=1, keepdims=True))
    layer_back = pooled_back * (1.0 / TEXT)
    rows(lb, seat, 16)[...] = fold(layer_back)
    send_lb = Exchange(
        chip, c_dev, lambda q: rows(lb, seat, 16), lambda s: rows(lb, 8 * core + s, 16), lb.at[pl.ds(0, 112)], s_lb, 8, LINE
    )
    send_lb.start()
    send_m.start()
    mixes[pl.ds(xy, 1)] = rows(mixed, xy, RO)[...].reshape(1, RO, TOK)
    send_lb.wait()
    ours = rows(lb, core, 128)
    share = pltpu.make_async_remote_copy(
        src_ref=ours, dst_ref=ours, send_sem=s_share.at[0], recv_sem=s_share.at[1], device_id=twin, device_id_type=MESH
    )
    share.start()
    share.wait_recv()

    pairs_back = unfold(lb[...]).astype(BF16)
    rows(lball, xy, TOK).at[:, wide][...] = jnp.where(core == 0, pairs_back[:, :SP], pairs_back[:, SP:])
    g_lbs = both(
        Gather, lball, back_at, 4, lball.at[pl.ds(0, 256), pl.ds(0, SP)], lball.at[pl.ds(0, 960), pl.ds(0, SP)], ag_sem
    )
    for part in g_lbs:
        part.start()
    for part in g_lbs:
        part.second(0)
    slot_back = dot(pair_of, pairs_back)
    ob[...] = (gate_col * slot_back).astype(BF16)
    pb[SLOTS:, :] = jnp.zeros((SP - SLOTS, HALF), BF16)

    def back(n, carry):
        cols = chunk(n, 256)
        act_back = dot(ob[...], full_out[cols, :], 1, 1)
        pb[0:SLOTS, cols] = (act_back * pre[:, cols]).astype(BF16)
        return carry

    def grad_in(k, step):
        spots = [(wrap(x + step), b) if k == 0 else (b, wrap(y + step)) for b in range(R)]
        starts = [pl.multiple_of((R * yc + xc) * RI, 16) for xc, yc in spots]
        left = jnp.concatenate([xt[pl.ds(at, RI), :] for at in starts], axis=0)
        value = dot(left, pb[:, D * k : D * (k + 1)]).astype(BF16)
        for b in range(R):
            gi[pl.ds(starts[b], RI), D * k : D * (k + 1)] = value[RI * b : RI * (b + 1)]

    s_ins = both(Scatter, gi, in_at, 0, halves, fulls, fifteen, rs_sem)
    for k in (0, 1):
        lax.fori_loop(3 * k, 3 * k + 3, back, 0)
        grad_in(k, 2)
        s_ins[k].start()
    for step in (1, -1, 0):
        for k in (0, 1):
            grad_in(k, step)

    for part in g_lbs:
        part.stage1()
    extras = []
    for p in range(3):
        cols = slice(256 * p, 256 * (p + 1))
        in_back = dot(pb[0:SLOTS, :], full_in[cols, :], 1, 1).astype(BF16)
        ib[:, cols] = in_back[0:256]
        extras.append(in_back[256:SLOTS])
        if p < 2:
            for part in s_ins:
                part.mid(p)
    gate_back = jnp.sum(slot_back * out32[...], axis=1, keepdims=True)
    back1 = gate_back.astype(BF16).astype(F32)
    back2 = (gate_back - back1).astype(BF16).astype(F32)
    backs = [back1, back2, gate_back - back1 - back2]
    spread = jnp.zeros((256, 256), F32)
    for m in range(3):
        spread = spread + dot(note_of[m], jnp.where(own_lane, backs[m], 0.0).astype(BF16), 0, 0)
        spread = spread + dot(picked[m], extras[m], 0, 0)
    ib[:, D:] = spread.astype(BF16)
    send_ib = Exchange(
        j, z_dev, lambda q: rows(ib, q, 16), lambda s: rows(ibrecv, s, 16), ibrecv.at[pl.ds(0, 240)], s_ib
    )
    send_ib.start()
    rows(ibrecv, j, 16)[...] = rows(ib, j, 16)[...]
    for part in g_lbs:
        part.stage2()
    for i in (2, 3):
        for part in s_ins:
            part.mid(i)
    for i in range(3):
        for part in g_lbs:
            part.stage3(i)
        for part in s_ins:
            part.end(i)
    for part in g_lbs:
        part.stage3(3)
    swaps_back = []
    for k in (0, 1):
        half = slice(D * k, D * (k + 1))
        v32[:, half] = s_ins[k].end(3)
        vback[k] = stack(v32[pl.ds(pl.multiple_of(24 * (1 - h), 8), 24), half])
        swap = pltpu.make_async_remote_copy(
            src_ref=vback.at[k], dst_ref=vfinal.at[k], send_sem=pair2_sem.at[k], recv_sem=pair2_sem.at[2 + k],
            device_id=other, device_id_type=MESH,
        )
        swap.start()
        swaps_back.append(swap)
    for part in g_lbs:
        part.stage4()
    ours = lball.at[:, wide]
    share2 = pltpu.make_async_remote_copy(
        src_ref=ours, dst_ref=ours, send_sem=s_share2.at[0], recv_sem=s_share2.at[1], device_id=twin, device_id_type=MESH
    )
    share2.start()

    send_ib.wait()
    inputs = tok[...].astype(F32)
    centred = inputs - jnp.mean(inputs, axis=1, keepdims=True)
    inverse = lax.rsqrt(jnp.mean(centred * centred, axis=1, keepdims=True) + EPS)
    scaled = centred * inverse
    back_main = dot(jnp.concatenate([main, main], axis=1), ibrecv[:, :D])
    back_tail = [dot(jnp.concatenate([e, e], axis=1), ibrecv[:, D:]) for e in extra]
    normed_back = back_main + jnp.concatenate(back_tail, axis=1)
    gained = normed_back * gain[...].reshape(1, D)
    repeated = jnp.broadcast_to(layer_back.reshape(PAIR, 1, D), (PAIR, TEXT, D)).reshape(TOK, D)
    tg[...] = (
        repeated
        + inverse * (gained - jnp.mean(gained, axis=1, keepdims=True) - scaled * jnp.mean(gained * scaled, axis=1, keepdims=True))
    ).astype(BF16)
    row_i = iota((TOK, 256), 1)
    kind = lax.rem(row_i, 16)
    owner = jnp.logical_and(jnp.logical_and(kind >= 12, kind < 15), lax.rem(row_i // 16, 8).astype(F32) == chosen)
    gathered = dot(hot(owner), ibrecv[:, D:])
    token_gate = jnp.sum(jnp.where(at_slot, gathered, 0.0), axis=1, keepdims=True)
    gg[...] = jnp.broadcast_to(token_gate, (TOK, TOK)).T[0:1]

    send_m.wait()
    factors = jnp.concatenate([mixes[k] for k in range(N)], axis=1)
    dwout[:, wide] = dot(factors, lball[:, wide])
    share2.wait_recv()
    rest = pl.ds(pl.multiple_of(SP * (1 - core), TOK), SP)
    dwout[:, rest] = dot(factors, lball[:, rest])
    kept = v32[pl.ds(pl.multiple_of(24 * h, 8), 24), :]
    held = []
    for g in range(4):
        hi, lo = split2(kept[:, SP * g : SP * (g + 1)])
        held.append(dot(hi, sel[0], 1, 1) + dot(lo, sel[0], 1, 1))
    for k in (0, 1):
        swaps_back[k].wait_recv()
        came = unstack(vfinal[k])
        for g in (0, 1):
            at = D * (2 * k + g)
            dwin[:, at : at + D] = held[2 * k + g] + dot(came[:, SP * g : SP * (g + 1)].astype(BF16), sel[1], 1, 1)

    for swap in swaps + swaps_back:
        swap.wait_send()
    join.wait_send()
    share.wait_send()
    share2.wait_send()
    for part in outs + ins + g_lbs + s_ins:
        part.sent()
    for exchange in (images, send_x, send_c, send_m, send_t, send_r, send_cc, send_tb, send_lb, send_ib):
        exchange.sent()


def hand_on(*refs):
    for k in range(4):
        refs[4 + k][...] = refs[k][...]


def body(tokens, expert_ids, gate, ln_gain, w_in, w_out, image_emb):
    vmem = pl.BlockSpec(memory_space=pltpu.VMEM)
    f32 = lambda *shape: pltpu.VMEM(shape, F32)
    b16 = lambda *shape: pltpu.VMEM(shape, BF16)
    sems = lambda *shape: pltpu.SemaphoreType.DMA(shape)
    token_grad, gate_grad, in_grad, out_grad = pl.pallas_call(
        kernel,
        out_shape=(
            jax.ShapeDtypeStruct((TOK, D), BF16),
            jax.ShapeDtypeStruct((1, TOK), F32),
            jax.ShapeDtypeStruct((24, H), F32),
            jax.ShapeDtypeStruct((RO, D), F32),
        ),
        in_specs=[pl.BlockSpec(memory_space=pl.ANY)] * 7,
        out_specs=(vmem,) * 4,
        scratch_shapes=[
            b16(TOK, D),
            pltpu.VMEM((1, TOK), jnp.int32),
            f32(1, TOK),
            f32(D),
            b16(24, H),
            b16(RO, D),
            b16(PAIR, D),
            sems(7),
            b16(2, D, SP),
            b16(2, 48, SP),
            f32(RI, HALF),
            b16(2, 48, SP),
            b16(2, 48, SP),
            b16(2, 48, SP),
            b16(D, HALF),
            b16(HALF, D),
            b16(256, D // 2),
            b16(TOK, D),
            b16(TOK, 1024),
            b16(256, 1024),
            b16(SP, D),
            b16(D, SP),
            f32(SLOTS, HALF),
            f32(SLOTS, HALF),
            b16(SP, HALF),
            b16(HALF, SP),
            f32(SLOTS, D),
            b16(256, D // 2),
            b16(128, D // 2),
            b16(128, D // 2),
            b16(128, D // 2),
            b16(256, D // 2),
            f32(1, TOK),
            f32(N, 1, TOK),
            f32(1, TOK),
            f32(N, 1, TOK),
            b16(256, D // 2),
            b16(256, D // 2),
            b16(256, D // 2),
            b16(SLOTS, D),
            b16(SP, HALF),
            b16(256, 1024),
            b16(256, 1024),
            b16(HALF, TOK),
            b16(N, RO, TOK),
            b16(N * TOK, D),
            b16(D, HALF),
            b16(2, 5, 2, 48, SP),
            b16(2, 5, 2, 48, D),
            sems(6, 13),
            sems(2, 16),
            sems(4),
            sems(4),
        ]
        + [sems(2)] * 13,
        compiler_params=pltpu.CompilerParams(
            collective_id=0, has_side_effects=True, vmem_limit_bytes=56 * 1024 * 1024
        ),
        cost_estimate=pl.CostEstimate(flops=5_000_000_000, bytes_accessed=2_000_000, transcendentals=1_000_000),
    )(tokens, expert_ids.reshape(1, TOK), gate.reshape(1, TOK), ln_gain, w_in[0], w_out[0], image_emb)
    results = (token_grad, gate_grad, in_grad, out_grad)
    token_grad, gate_grad, in_grad, out_grad = pl.pallas_call(
        hand_on,
        out_shape=tuple(jax.ShapeDtypeStruct(r.shape, r.dtype) for r in results),
        in_specs=[vmem] * 4,
        out_specs=(vmem,) * 4,
    )(*results)
    return token_grad, gate_grad.reshape(TOK), in_grad[None], out_grad[None]


def solution(mesh):
    in_specs = (
        P(("dp", "expert"), None),
        P(("dp", "expert"), None),
        P(("dp", "expert")),
        P(),
        P("expert", "dp", None),
        P("expert", "dp", None),
        P(("dp", "expert"), None),
    )
    out_specs = (
        P(("dp", "expert"), None),
        P(("dp", "expert")),
        P("expert", "dp", None),
        P("expert", "dp", None),
    )
    return jax.shard_map(body, mesh=mesh, in_specs=in_specs, out_specs=out_specs, check_vma=False)
```

```python
import jax
import jax.numpy as jnp
from jax import lax
from jax.experimental import pallas as pl
from jax.experimental.pallas import tpu as pltpu
from jax.sharding import PartitionSpec as P

MESH = pl.DeviceIdType.MESH
F32 = jnp.float32
BF16 = jnp.bfloat16

D = 768
H = 3072
HALF = 1536
TOK = 128
CAP = 20
PAIR = 8
TEXT = 16
N = 16
R = 4
RO = 96
RI = 48
SLOTS = 320
SP = 384
EPS = 1e-6
LINE = (4, 3, 5, 2, 6, 1, 7)
RING = (8, 9, 7, 6, 10, 5, 11, 4, 12, 3, 13, 2, 14, 1, 15)
PLANE = (10, 9, 11, 6, 14, 2, 8, 5, 7, 13, 15, 1, 3, 4, 12)
SCALE = 100.0


def dot(a, b, ca=1, cb=0):
    return lax.dot_general(a, b, (((ca,), (cb,)), ((), ())), preferred_element_type=F32)


def iota(shape, axis):
    return lax.broadcasted_iota(jnp.int32, shape, axis)


def hot(mask):
    return jnp.where(mask, 1.0, 0.0).astype(BF16)


def split2(v):
    hi = v.astype(BF16)
    return hi, (v - hi.astype(F32)).astype(BF16)


def fold(v):
    m = v.shape[0] // 8
    v = v.reshape(m, 8, D)
    return jnp.concatenate([v[:, :, : D // 2], v[:, :, D // 2 :]], axis=1).reshape(16 * m, D // 2).astype(BF16)


def unfold(v):
    m = v.shape[0] // 16
    v = v.astype(F32).reshape(m, 16, D // 2)
    return jnp.concatenate([v[:, :8], v[:, 8:]], axis=2).reshape(8 * m, D)


def stack(v):
    return jnp.concatenate([v[:, :SP], v[:, SP:]], axis=0).astype(BF16)


def unstack(v):
    v = v.astype(F32)
    return jnp.concatenate([v[:24], v[24:]], axis=1)


def wrap(v):
    return lax.rem(v + 2 * R, R)


class Gather:
    def __init__(self, block, c1, c2, dev1, dev2, four, fifteen, sem, g):
        self.block, self.c1, self.c2 = block, c1, c2
        self.dev1, self.dev2, self.sem, self.g = dev1, dev2, sem, g
        self.four, self.fifteen = four, fifteen
        self.bs = [c1, wrap(c1 - 1), wrap(c1 + 1), wrap(c1 + 2)]

    def copy(self, k, ref, dev):
        return pltpu.make_async_remote_copy(
            src_ref=ref, dst_ref=ref, send_sem=self.sem.at[self.g, 12], recv_sem=self.sem.at[self.g, k],
            device_id=dev, device_id_type=MESH,
        )

    def got(self, k, ref):
        self.copy(k, ref, self.dev1(1)).wait_recv()
        return ref

    def at(self, a, b, half=None):
        return self.block(wrap(a), wrap(b), half)

    def second(self, i):
        ref = self.at(self.bs[i], self.c2)
        self.copy(3 + 2 * i, ref, self.dev2(1)).start()
        self.copy(4 + 2 * i, ref, self.dev2(-1)).start()

    def start(self):
        ref = self.at(self.c1, self.c2)
        self.copy(0, ref, self.dev1(1)).start()
        self.copy(1, ref, self.dev1(-1)).start()

    def stage1(self):
        c1, c2 = self.c1, self.c2
        self.got(0, self.at(c1 - 1, c2))
        self.copy(2, self.at(c1 - 1, c2, 0), self.dev1(1)).start()
        self.second(1)
        self.got(1, self.at(c1 + 1, c2))
        self.copy(2, self.at(c1 + 1, c2, 1), self.dev1(-1)).start()
        self.second(2)

    def stage2(self):
        self.got(2, self.at(self.c1 + 2, self.c2))
        self.second(3)

    def stage3(self, i):
        b, c2 = self.bs[i], self.c2
        self.got(3 + 2 * i, self.at(b, c2 - 1))
        self.copy(11, self.at(b, c2 - 1, 0), self.dev2(1)).start()
        self.got(4 + 2 * i, self.at(b, c2 + 1))
        self.copy(11, self.at(b, c2 + 1, 1), self.dev2(-1)).start()

    def stage4(self):
        self.got(11, self.four)

    def sent(self):
        self.copy(12, self.fifteen, self.dev1(1)).wait_send()


class Scatter:
    def __init__(self, block, c1, c2, dev1, dev2, halves, fulls, fifteen, sem, g):
        self.block, self.c1, self.c2 = block, c1, c2
        self.dev1, self.dev2, self.sem, self.g = dev1, dev2, sem, g
        self.halves, self.fulls, self.fifteen = halves.at[g], fulls.at[g], fifteen
        self.bs = [wrap(c2 + 2), wrap(c2 + 1), wrap(c2 - 1), c2]

    def copy(self, k, src, dst, dev):
        return pltpu.make_async_remote_copy(
            src_ref=src, dst_ref=dst, send_sem=self.sem.at[self.g, 15], recv_sem=self.sem.at[self.g, k],
            device_id=dev, device_id_type=MESH,
        )

    def got(self, k, ref):
        self.copy(k, ref, ref, self.dev1(1)).wait_recv()
        return ref

    def at(self, a, b, half=None):
        return self.block(wrap(a), wrap(b), half)

    def add(self, ref, *others):
        total = ref[...].astype(F32)
        for other in others:
            total = total + other[...].astype(F32)
        ref[...] = total.astype(BF16)

    def start(self):
        for i in range(4):
            self.copy(2 * i, self.at(self.c1 + 2, self.bs[i], 0), self.halves.at[i, 0], self.dev1(1)).start()
            self.copy(2 * i + 1, self.at(self.c1 + 2, self.bs[i], 1), self.halves.at[i, 1], self.dev1(-1)).start()

    def mid(self, i):
        b = self.bs[i]
        self.add(self.at(self.c1 + 1, b, 0), self.got(2 * i, self.halves.at[i, 0]))
        self.copy(8 + i, self.at(self.c1 + 1, b), self.fulls.at[i, 0], self.dev1(1)).start()
        self.add(self.at(self.c1 - 1, b, 1), self.got(2 * i + 1, self.halves.at[i, 1]))
        self.copy(8 + i, self.at(self.c1 - 1, b), self.fulls.at[i, 1], self.dev1(-1)).start()

    def end(self, i):
        c1, b = self.c1, self.bs[i]
        self.got(8 + i, self.fulls.at[i])
        first, second = self.fulls.at[i, 0], self.fulls.at[i, 1]
        if i == 0:
            self.add(self.at(c1, b), first, second)
            self.copy(12, self.at(c1, b, 0), self.halves.at[4, 0], self.dev2(1)).start()
            self.copy(13, self.at(c1, b, 1), self.halves.at[4, 1], self.dev2(-1)).start()
        elif i == 1:
            self.add(self.at(c1, b), first, second)
            self.add(self.at(c1, b, 0), self.got(12, self.halves.at[4, 0]))
            self.copy(14, self.at(c1, b), self.fulls.at[4, 0], self.dev2(1)).start()
        elif i == 2:
            self.add(self.at(c1, b), first, second)
            self.add(self.at(c1, b, 1), self.got(13, self.halves.at[4, 1]))
            self.copy(14, self.at(c1, b), self.fulls.at[4, 1], self.dev2(-1)).start()
        else:
            total = self.at(c1, b)[...].astype(F32) + first[...].astype(F32) + second[...].astype(F32)
            self.got(14, self.fulls.at[4])
            for k in (0, 1):
                total = total + self.fulls[4, k].astype(F32)
            return total

    def sent(self):
        self.copy(15, self.fifteen, self.fifteen, self.dev1(1)).wait_send()


def kernel(
    tok_in, ids_in, gate_in, gain_in, win_in, wout_in, img_in,
    tg, gg, dwin, dwout,
    tok, ids, gate, gain, win, wout, img, s_in,
    sel, vsend, v32, vcame, vback, vfinal, full_in, full_out, imgs, imgb,
    xsend, xr, xs, xt, pre, cdf, act, actt, out32,
    contrib, cjoin, csend, crecv, tall, rsum, rrecv, csum, ccrecv, tb, tbrecv, lb, ob, pb,
    ib, ibrecv, mixed, mixes, lball, gi, halves, fulls,
    ag_sem, rs_sem, pair_sem, pair2_sem,
    s_img, s_x, s_c, s_t, s_r, s_cc, s_tb, s_lb, s_ib, s_join, s_share, s_share2, s_m,
):
    dp, ex = lax.axis_index("dp"), lax.axis_index("expert")
    xy, h = dp // 2, lax.rem(dp, 2)
    y, x = xy // R, lax.rem(xy, R)
    j = 8 * h + ex

    def z_dev(q):
        return (2 * xy + q // 8, lax.rem(q, 8))

    def p_dev(k):
        return (2 * k + h, ex)

    chip, core = 4 * h + ex // 2, lax.rem(ex, 2)
    seat = 8 * core + chip

    def c_dev(k):
        return (2 * xy + k // 4, 2 * lax.rem(k, 4) + core)

    twin = (dp, ex + 1 - 2 * core)

    def x_dev(step):
        return p_dev(R * y + wrap(x + step))

    def y_dev(step):
        return p_dev(R * wrap(y + step) + x)

    class Exchange:
        def __init__(self, me, dev, src, dst, all_but_one, sem, size=N, order=None):
            self.me, self.dev, self.src, self.dst, self.sem = me, dev, src, dst, sem
            self.order = order
            self.all_but_one, self.size = all_but_one, size

        def copy(self, src, dst, to):
            return pltpu.make_async_remote_copy(
                src_ref=src, dst_ref=dst, send_sem=self.sem.at[0], recv_sem=self.sem.at[1],
                device_id=self.dev(to), device_id_type=MESH,
            )

        def start(self):
            def step(i, carry):
                to = lax.rem(self.me + i, self.size)
                self.copy(self.src(to), self.dst(self.me), to).start()
                return carry

            if self.order is None:
                lax.fori_loop(1, self.size, step, 0)
            else:
                for i in self.order:
                    step(i, 0)

        def wait(self):
            self.copy(self.all_but_one, self.all_but_one, lax.rem(self.me + 1, self.size)).wait_recv()

        def sent(self):
            self.copy(self.all_but_one, self.all_but_one, lax.rem(self.me + 1, self.size)).wait_send()

    def rows(ref, k, n):
        return ref.at[pl.ds(pl.multiple_of(k * n, n), n)]

    barrier = pltpu.get_barrier_semaphore()

    for k in range(N - 1):
        pl.semaphore_signal(barrier, inc=1, device_id=z_dev(lax.rem(j + RING[k], N)), device_id_type=MESH)
        pl.semaphore_signal(barrier, inc=1, device_id=p_dev(lax.rem(xy + PLANE[k], N)), device_id_type=MESH)

    loads = [
        pltpu.make_async_copy(src, dst, s_in.at[k])
        for k, (src, dst) in enumerate(
            zip((win_in, tok_in, ids_in, gate_in, gain_in, img_in, wout_in), (win, tok, ids, gate, gain, img, wout))
        )
    ]
    for load in loads:
        load.start()
    for load in loads:
        load.wait()
    rows(full_out, xy, RO)[...] = wout[...]
    source = iota((D, SP), 0)
    column = iota((D, SP), 1)
    spot = column + (column // RO) * RO
    sel[0] = hot(source == spot + RO * h)
    sel[1] = hot(source == spot + RO * (1 - h))
    mine, theirs = [], []
    for g in range(4):
        part = win[:, D * g : D * (g + 1)]
        mine.append(dot(part, sel[0]))
        theirs.append(dot(part, sel[1]))
    for k in (0, 1):
        vsend[k] = stack(jnp.concatenate(theirs[2 * k : 2 * k + 2], axis=1))
    for g in range(4):
        v32[pl.ds(pl.multiple_of(24 * h, 8), 24), SP * g : SP * (g + 1)] = mine[g]
    image = img[...].astype(F32)
    image = image * lax.rsqrt(jnp.sum(image * image, axis=1, keepdims=True) + EPS)
    rows(imgs, j, 16)[...] = fold(image)

    inputs = tok[...].astype(F32)
    centred = inputs - jnp.mean(inputs, axis=1, keepdims=True)
    inverse = lax.rsqrt(jnp.mean(centred * centred, axis=1, keepdims=True) + EPS)
    normed = (centred * inverse * gain[...].reshape(1, D)).astype(BF16)
    token_sum = jnp.sum(inputs.reshape(PAIR, TEXT, D), axis=1)

    chosen_row = jnp.broadcast_to(ids[...].astype(F32), (TOK, TOK))
    chosen = chosen_row.T[:, 0:1]
    lane = iota((TOK, TOK), 1).astype(F32)
    onehot = hot(lane == chosen)
    before = dot(hot(iota((TOK, TOK), 0) > iota((TOK, TOK), 1)), onehot)
    slot = jnp.sum(before * onehot.astype(F32), axis=1, keepdims=True)
    is_main = slot < 16.0
    is_extra = jnp.logical_and(slot >= 16.0, slot < float(CAP))
    main = hot(lane == jnp.where(is_main, 16.0 * chosen + slot, -1.0))
    extra = [hot(lane == jnp.where(is_extra, 16.0 * chosen + (4.0 * p - 16.0) + slot, -1.0)) for p in range(3)]
    at_slot = iota((TOK, 256), 1).astype(F32) == jnp.where(slot < float(CAP), slot, -1.0)

    xsend[:, :D] = dot(main.T, normed).astype(BF16)
    tail = dot(extra[0].T, normed[:, 0:256]) + dot(extra[1].T, normed[:, 256:512]) + dot(extra[2].T, normed[:, 512:768])
    gate_row = gate[...]
    gate1 = gate_row.astype(BF16).astype(F32)
    gate2 = (gate_row - gate1).astype(BF16).astype(F32)
    gate3 = gate_row - gate1 - gate2
    line = iota((TOK, TOK), 0)
    kind = lax.rem(line, 16)
    pair_row = (iota((TOK, TOK), 1) // TEXT).astype(F32)
    notes = jnp.where(kind == 12, gate1, jnp.where(kind == 13, gate2, jnp.where(kind == 14, gate3, jnp.where(kind == 15, pair_row, 0.0))))
    notes = jnp.where((line // 16).astype(F32) == chosen_row, notes, 0.0)
    xsend[:, D:] = (tail + dot(notes.astype(BF16), hot(at_slot))).astype(BF16)
    rows(xr, j, 16)[...] = rows(xsend, ex, 16)[...]

    pl.semaphore_wait(barrier, 2 * (N - 1))

    def out_at(buf, part):
        def block(xc, yc, half=None):
            row = pl.multiple_of((R * yc + xc) * RO + 48 * part, 16)
            if half is None:
                return buf.at[pl.ds(row, 48)]
            return buf.at[pl.ds(row, 48), pl.ds(SP * half, SP)]

        return block

    def in_at(buf, part):
        def block(xc, yc, half=None):
            row = pl.multiple_of((R * yc + xc) * RI, 16)
            if half is None:
                return buf.at[pl.ds(row, RI), pl.ds(D * part, D)]
            return buf.at[pl.ds(row, RI), pl.ds(D * part + SP * half, SP)]

        return block

    wide = pl.ds(pl.multiple_of(SP * core, TOK), SP)

    def back_at(buf, part):
        def block(xc, yc, half=None):
            row = pl.multiple_of((R * yc + xc) * TOK + 64 * part, 32)
            if half is None:
                return buf.at[pl.ds(row, 64), wide]
            return buf.at[pl.ds(pl.multiple_of(row + 32 * half, 32), 32), wide]

        return block

    def both(make, buf, at, first, *args):
        other_way = at(buf, 1)
        return (
            make(at(buf, 0), x, y, x_dev, y_dev, *args, first),
            make(lambda a, b, half=None: other_way(b, a, half), y, x, y_dev, x_dev, *args, first + 1),
        )

    fifteen = full_out.at[pl.ds(0, 15 * 48)]
    outs = both(Gather, full_out, out_at, 0, full_out.at[pl.ds(0, 192)], fifteen, ag_sem)
    ins = both(Gather, full_in, in_at, 2, full_in.at[pl.ds(0, 96)], fifteen, ag_sem)

    other = (2 * xy + 1 - h, ex)
    swaps = [
        pltpu.make_async_remote_copy(
            src_ref=vsend.at[k], dst_ref=vcame.at[k], send_sem=pair_sem.at[k], recv_sem=pair_sem.at[2 + k],
            device_id=other, device_id_type=MESH,
        )
        for k in (0, 1)
    ]
    for swap in swaps:
        swap.start()
    for part in outs:
        part.start()
    for part in outs:
        part.second(0)

    images = Exchange(j, z_dev, lambda q: rows(imgs, j, 16), lambda s: rows(imgs, s, 16), imgs.at[pl.ds(0, 240)], s_img)

    send_x = Exchange(j, z_dev, lambda q: rows(xsend, lax.rem(q, 8), 16), lambda s: rows(xr, s, 16), xr.at[pl.ds(0, 240)], s_x)

    for part in outs:
        part.stage1()
    for part in outs:
        part.stage2()
    for k in (0, 1):
        swaps[k].wait_recv()
        half = slice(D * k, D * (k + 1))
        v32[pl.ds(pl.multiple_of(24 * (1 - h), 8), 24), half] = unstack(vcame[k])
        rows(full_in, xy, RI).at[:, half][...] = v32[:, half].astype(BF16)
        ins[k].start()
        outs[k].stage3(0)
    for part in ins:
        part.second(0)
    send_x.start()
    images.start()
    for i in (1, 2):
        for part in outs:
            part.stage3(i)
    for part in ins:
        part.stage1()
    for part in outs:
        part.stage3(3)
    for part in ins:
        part.stage2()
    for i in range(4):
        for part in ins:
            part.stage3(i)

    send_x.wait()
    row64 = iota((64, 256), 0)
    lane64 = iota((64, 256), 1)
    picked = [hot(lane64 == 16 * (row64 // 4) + 4 * p + lax.rem(row64, 4)) for p in range(3)]
    xs[0:256, :] = xr[:, :D]
    for p in range(3):
        xs[256:SLOTS, 256 * p : 256 * (p + 1)] = dot(picked[p], xr[:, D:]).astype(BF16)
    xs[SLOTS:, :] = jnp.zeros((SP - SLOTS, D), BF16)
    xt[...] = xs[...].T
    slot_i = iota((SLOTS, 256), 0)
    lane_i = iota((SLOTS, 256), 1)
    slot_from = jnp.where(slot_i < 256, slot_i // 16, (slot_i - 256) // 4)
    slot_at = jnp.where(slot_i < 256, lax.rem(slot_i, 16), 16 + lax.rem(slot_i, 4))
    note_of = [hot(lane_i == 16 * slot_from + 12 + m) for m in range(4)]
    tails = xr[:, D:]
    own_lane = lane_i == slot_at
    gate_col = jnp.sum(jnp.where(own_lane, dot(note_of[0] + note_of[1] + note_of[2], tails), 0.0), axis=1, keepdims=True)
    pair_col = jnp.sum(jnp.where(own_lane, dot(note_of[3], tails), 0.0), axis=1, keepdims=True)
    first_pair = (PAIR * (8 * lax.rem(slot_from, 2) + slot_from // 2))[:, :TOK].astype(F32)
    pair_of = hot(lane_i[:, :TOK].astype(F32) == first_pair + pair_col)

    images.wait()
    imgb[...] = unfold(imgs[...]).astype(BF16)
    for part in ins:
        part.stage4()

    def chunk(n, size):
        return pl.ds(pl.multiple_of(n * size, size), size)

    def forward(n, carry):
        cols = chunk(n, 256)
        value = dot(xs[0:SLOTS, :], full_in[:, cols])
        bell = 0.5 * (1.0 + lax.erf(value * (0.5**0.5)))
        pre[:, cols] = value
        cdf[:, cols] = bell
        act[0:SLOTS, cols] = (value * bell).astype(BF16)
        return carry

    lax.fori_loop(0, HALF // 256, forward, 0)
    act[SLOTS:, :] = jnp.zeros((SP - SLOTS, HALF), BF16)
    for part in outs:
        part.stage4()

    def project(n, carry):
        cols = chunk(n, 256)
        out32[:, cols] = dot(act[0:SLOTS, :], full_out[:, cols])
        return carry

    lax.fori_loop(0, D // 256, project, 0)

    contrib[...] = fold(dot(pair_of, (gate_col * out32[...]).astype(BF16), 0, 0))
    join = pltpu.make_async_remote_copy(
        src_ref=rows(contrib, 1 - core, 128), dst_ref=cjoin, send_sem=s_join.at[0], recv_sem=s_join.at[1],
        device_id=twin, device_id_type=MESH,
    )
    join.start()
    join.wait_recv()
    joined = rows(contrib, core, 128)
    csend[...] = (joined[...].astype(F32) + cjoin[...].astype(F32)).astype(BF16)
    send_c = Exchange(
        chip, c_dev, lambda q: rows(csend, q, 16), lambda s: rows(crecv, s, 16), crecv.at[pl.ds(0, 112)], s_c, 8, LINE
    )
    send_c.start()
    rows(crecv, chip, 16)[...] = rows(csend, chip, 16)[...]

    actt[...] = act[...].T
    pb[SLOTS:, :] = jnp.zeros((SP - SLOTS, HALF), BF16)
    weight1, weight2 = split2(gate_col * pair_of.astype(F32))
    pad = jnp.zeros((SP - SLOTS, TOK), BF16)
    weight1 = jnp.concatenate([weight1, pad], axis=0)
    weight2 = jnp.concatenate([weight2, pad], axis=0)

    def mix(n, carry):
        part = actt[chunk(n, 256), :]
        mixed[chunk(n, 256), :] = (dot(part, weight1) + dot(part, weight2)).astype(BF16)
        return carry

    lax.fori_loop(0, HALF // 256, mix, 0)
    send_m = Exchange(
        xy, p_dev, lambda q: rows(mixed, q, RO), lambda s: mixes.at[s], mixes.at[pl.ds(0, N - 1)], s_m
    )

    def slope(n, carry):
        cols = chunk(n, 256)
        value = pre[:, cols]
        pre[:, cols] = cdf[:, cols] + value * (jnp.exp(-0.5 * value * value) * 0.3989422804014327)
        return carry

    send_c.wait()
    pooled = (token_sum + jnp.sum(unfold(crecv[...]).reshape(8, PAIR, D), axis=0)) * (1.0 / TEXT)
    q_inv = lax.rsqrt(jnp.sum(pooled * pooled, axis=1, keepdims=True) + EPS)
    unit = pooled * q_inv
    rows(tall, xy, 16)[...] = fold(unit)
    send_t = Exchange(xy, p_dev, lambda q: rows(tall, xy, 16), lambda s: rows(tall, s, 16), tall.at[pl.ds(0, 240)], s_t, N, PLANE)
    send_t.start()
    lax.fori_loop(0, 3, slope, 0)
    send_t.wait()

    scores = SCALE * dot(unfold(tall[...]).astype(BF16), imgb[...], 1, 1)
    exped = jnp.exp(scores)
    csum[...] = jnp.sum(exped, axis=0, keepdims=True)
    send_cc = Exchange(j, z_dev, lambda q: csum, lambda s: ccrecv.at[s], ccrecv.at[pl.ds(0, N - 1)], s_cc, N, RING)
    send_cc.start()
    rsum[...] = jnp.sum(exped.T, axis=0, keepdims=True)
    send_r = Exchange(xy, p_dev, lambda q: rsum, lambda s: rrecv.at[s], rrecv.at[pl.ds(0, N - 1)], s_r, N, PLANE)
    send_r.start()
    rrecv[pl.ds(xy, 1)] = rsum[...].reshape(1, 1, TOK)
    ccrecv[pl.ds(j, 1)] = csum[...].reshape(1, 1, TOK)
    text_at = iota((TOK, TOK), 0)
    image_at = iota((TOK, TOK), 1)
    diagonal = jnp.where(
        jnp.logical_and(image_at // PAIR == j, text_at == PAIR * xy + lax.rem(image_at, PAIR)), 1.0, 0.0
    )
    lax.fori_loop(3, 6, slope, 0)
    send_r.wait()
    send_cc.wait()
    row_total = jnp.broadcast_to(jnp.sum(rrecv[...], axis=0), (TOK, TOK)).T
    col_total = jnp.sum(ccrecv[...], axis=0)
    coefs = (0.5 * (exped / row_total + exped / col_total) - diagonal).astype(BF16)
    tb[...] = fold(SCALE * dot(coefs, imgb[...]))
    send_tb = Exchange(xy, p_dev, lambda q: rows(tb, q, 16), lambda s: rows(tbrecv, s, 16), tbrecv.at[pl.ds(0, 240)], s_tb, N, PLANE)
    send_tb.start()
    rows(tbrecv, xy, 16)[...] = rows(tb, xy, 16)[...]
    send_tb.wait()
    text_back = jnp.sum(unfold(tbrecv[...]).reshape(N, PAIR, D), axis=0)
    pooled_back = q_inv * (text_back - unit * jnp.sum(unit * text_back, axis=1, keepdims=True))
    layer_back = pooled_back * (1.0 / TEXT)
    rows(lb, seat, 16)[...] = fold(layer_back)
    send_lb = Exchange(
        chip, c_dev, lambda q: rows(lb, seat, 16), lambda s: rows(lb, 8 * core + s, 16), lb.at[pl.ds(0, 112)], s_lb, 8, LINE
    )
    send_lb.start()
    send_m.start()
    mixes[pl.ds(xy, 1)] = rows(mixed, xy, RO)[...].reshape(1, RO, TOK)
    send_lb.wait()
    ours = rows(lb, core, 128)
    share = pltpu.make_async_remote_copy(
        src_ref=ours, dst_ref=ours, send_sem=s_share.at[0], recv_sem=s_share.at[1], device_id=twin, device_id_type=MESH
    )
    share.start()
    share.wait_recv()

    pairs_back = unfold(lb[...]).astype(BF16)
    rows(lball, xy, TOK).at[:, wide][...] = jnp.where(core == 0, pairs_back[:, :SP], pairs_back[:, SP:])
    g_lbs = both(
        Gather, lball, back_at, 4, lball.at[pl.ds(0, 256), pl.ds(0, SP)], lball.at[pl.ds(0, 960), pl.ds(0, SP)], ag_sem
    )
    for part in g_lbs:
        part.start()
    for part in g_lbs:
        part.second(0)
    slot_back = dot(pair_of, pairs_back)
    ob[...] = (gate_col * slot_back).astype(BF16)

    def back(n, carry):
        cols = chunk(n, 256)
        act_back = dot(ob[...], full_out[cols, :], 1, 1)
        pb[0:SLOTS, cols] = (act_back * pre[:, cols]).astype(BF16)
        return carry

    def grad_in(k, step):
        spots = [(wrap(x + step), b) if k == 0 else (b, wrap(y + step)) for b in range(R)]
        starts = [pl.multiple_of((R * yc + xc) * RI, 16) for xc, yc in spots]
        left = jnp.concatenate([xt[pl.ds(at, RI), :] for at in starts], axis=0)
        value = dot(left, pb[:, D * k : D * (k + 1)]).astype(BF16)
        for b in range(R):
            gi[pl.ds(starts[b], RI), D * k : D * (k + 1)] = value[RI * b : RI * (b + 1)]

    s_ins = both(Scatter, gi, in_at, 0, halves, fulls, fifteen, rs_sem)
    for k in (0, 1):
        lax.fori_loop(3 * k, 3 * k + 3, back, 0)
        grad_in(k, 2)
        s_ins[k].start()
    for step in (1, -1, 0):
        for k in (0, 1):
            grad_in(k, step)

    for part in g_lbs:
        part.stage1()
    extras = []
    for p in range(3):
        cols = slice(256 * p, 256 * (p + 1))
        in_back = dot(pb[0:SLOTS, :], full_in[cols, :], 1, 1).astype(BF16)
        ib[:, cols] = in_back[0:256]
        extras.append(in_back[256:SLOTS])
        if p < 2:
            for part in s_ins:
                part.mid(p)
    gate_back = jnp.sum(slot_back * out32[...], axis=1, keepdims=True)
    back1 = gate_back.astype(BF16).astype(F32)
    back2 = (gate_back - back1).astype(BF16).astype(F32)
    backs = [back1, back2, gate_back - back1 - back2]
    spread = jnp.zeros((256, 256), F32)
    for m in range(3):
        spread = spread + dot(note_of[m], jnp.where(own_lane, backs[m], 0.0).astype(BF16), 0, 0)
        spread = spread + dot(picked[m], extras[m], 0, 0)
    ib[:, D:] = spread.astype(BF16)
    send_ib = Exchange(
        j, z_dev, lambda q: rows(ib, q, 16), lambda s: rows(ibrecv, s, 16), ibrecv.at[pl.ds(0, 240)], s_ib
    )
    send_ib.start()
    rows(ibrecv, j, 16)[...] = rows(ib, j, 16)[...]
    for part in g_lbs:
        part.stage2()
    for i in (2, 3):
        for part in s_ins:
            part.mid(i)
    for i in range(3):
        for part in g_lbs:
            part.stage3(i)
        for part in s_ins:
            part.end(i)
    for part in g_lbs:
        part.stage3(3)
    swaps_back = []
    for k in (0, 1):
        half = slice(D * k, D * (k + 1))
        v32[:, half] = s_ins[k].end(3)
        vback[k] = stack(v32[pl.ds(pl.multiple_of(24 * (1 - h), 8), 24), half])
        swap = pltpu.make_async_remote_copy(
            src_ref=vback.at[k], dst_ref=vfinal.at[k], send_sem=pair2_sem.at[k], recv_sem=pair2_sem.at[2 + k],
            device_id=other, device_id_type=MESH,
        )
        swap.start()
        swaps_back.append(swap)
    for part in g_lbs:
        part.stage4()
    ours = lball.at[:, wide]
    share2 = pltpu.make_async_remote_copy(
        src_ref=ours, dst_ref=ours, send_sem=s_share2.at[0], recv_sem=s_share2.at[1], device_id=twin, device_id_type=MESH
    )
    share2.start()

    send_ib.wait()
    inputs = tok[...].astype(F32)
    centred = inputs - jnp.mean(inputs, axis=1, keepdims=True)
    inverse = lax.rsqrt(jnp.mean(centred * centred, axis=1, keepdims=True) + EPS)
    scaled = centred * inverse
    back_main = dot(jnp.concatenate([main, main], axis=1), ibrecv[:, :D])
    back_tail = [dot(jnp.concatenate([e, e], axis=1), ibrecv[:, D:]) for e in extra]
    normed_back = back_main + jnp.concatenate(back_tail, axis=1)
    gained = normed_back * gain[...].reshape(1, D)
    repeated = jnp.broadcast_to(layer_back.reshape(PAIR, 1, D), (PAIR, TEXT, D)).reshape(TOK, D)
    tg[...] = (
        repeated
        + inverse * (gained - jnp.mean(gained, axis=1, keepdims=True) - scaled * jnp.mean(gained * scaled, axis=1, keepdims=True))
    ).astype(BF16)
    row_i = iota((TOK, 256), 1)
    kind = lax.rem(row_i, 16)
    owner = jnp.logical_and(jnp.logical_and(kind >= 12, kind < 15), lax.rem(row_i // 16, 8).astype(F32) == chosen)
    gathered = dot(hot(owner), ibrecv[:, D:])
    token_gate = jnp.sum(jnp.where(at_slot, gathered, 0.0), axis=1, keepdims=True)
    gg[...] = jnp.broadcast_to(token_gate, (TOK, TOK)).T[0:1]

    send_m.wait()
    factors = jnp.concatenate([mixes[k] for k in range(N)], axis=1)
    dwout[:, wide] = dot(factors, lball[:, wide])
    share2.wait_recv()
    rest = pl.ds(pl.multiple_of(SP * (1 - core), TOK), SP)
    dwout[:, rest] = dot(factors, lball[:, rest])
    kept = v32[pl.ds(pl.multiple_of(24 * h, 8), 24), :]
    held = []
    for g in range(4):
        hi, lo = split2(kept[:, SP * g : SP * (g + 1)])
        held.append(dot(hi, sel[0], 1, 1) + dot(lo, sel[0], 1, 1))
    for k in (0, 1):
        swaps_back[k].wait_recv()
        came = unstack(vfinal[k])
        for g in (0, 1):
            at = D * (2 * k + g)
            dwin[:, at : at + D] = held[2 * k + g] + dot(came[:, SP * g : SP * (g + 1)].astype(BF16), sel[1], 1, 1)

    for swap in swaps + swaps_back:
        swap.wait_send()
    join.wait_send()
    share.wait_send()
    share2.wait_send()
    for part in outs + ins + g_lbs + s_ins:
        part.sent()
    for exchange in (images, send_x, send_c, send_m, send_t, send_r, send_cc, send_tb, send_lb, send_ib):
        exchange.sent()


def hand_on(*refs):
    for k in range(4):
        refs[4 + k][...] = refs[k][...]


def body(tokens, expert_ids, gate, ln_gain, w_in, w_out, image_emb):
    vmem = pl.BlockSpec(memory_space=pltpu.VMEM)
    f32 = lambda *shape: pltpu.VMEM(shape, F32)
    b16 = lambda *shape: pltpu.VMEM(shape, BF16)
    sems = lambda *shape: pltpu.SemaphoreType.DMA(shape)
    token_grad, gate_grad, in_grad, out_grad = pl.pallas_call(
        kernel,
        out_shape=(
            jax.ShapeDtypeStruct((TOK, D), BF16),
            jax.ShapeDtypeStruct((1, TOK), F32),
            jax.ShapeDtypeStruct((24, H), F32),
            jax.ShapeDtypeStruct((RO, D), F32),
        ),
        in_specs=[pl.BlockSpec(memory_space=pl.ANY)] * 7,
        out_specs=(vmem,) * 4,
        scratch_shapes=[
            b16(TOK, D),
            pltpu.VMEM((1, TOK), jnp.int32),
            f32(1, TOK),
            f32(D),
            b16(24, H),
            b16(RO, D),
            b16(PAIR, D),
            sems(7),
            b16(2, D, SP),
            b16(2, 48, SP),
            f32(RI, HALF),
            b16(2, 48, SP),
            b16(2, 48, SP),
            b16(2, 48, SP),
            b16(D, HALF),
            b16(HALF, D),
            b16(256, D // 2),
            b16(TOK, D),
            b16(TOK, 1024),
            b16(256, 1024),
            b16(SP, D),
            b16(D, SP),
            f32(SLOTS, HALF),
            f32(SLOTS, HALF),
            b16(SP, HALF),
            b16(HALF, SP),
            f32(SLOTS, D),
            b16(256, D // 2),
            b16(128, D // 2),
            b16(128, D // 2),
            b16(128, D // 2),
            b16(256, D // 2),
            f32(1, TOK),
            f32(N, 1, TOK),
            f32(1, TOK),
            f32(N, 1, TOK),
            b16(256, D // 2),
            b16(256, D // 2),
            b16(256, D // 2),
            b16(SLOTS, D),
            b16(SP, HALF),
            b16(256, 1024),
            b16(256, 1024),
            b16(HALF, TOK),
            b16(N, RO, TOK),
            b16(N * TOK, D),
            b16(D, HALF),
            b16(2, 5, 2, 48, SP),
            b16(2, 5, 2, 48, D),
            sems(6, 13),
            sems(2, 16),
            sems(4),
            sems(4),
        ]
        + [sems(2)] * 13,
        compiler_params=pltpu.CompilerParams(
            collective_id=0, has_side_effects=True, vmem_limit_bytes=56 * 1024 * 1024
        ),
        cost_estimate=pl.CostEstimate(flops=5_000_000_000, bytes_accessed=2_000_000, transcendentals=1_000_000),
    )(tokens, expert_ids.reshape(1, TOK), gate.reshape(1, TOK), ln_gain, w_in[0], w_out[0], image_emb)
    results = (token_grad, gate_grad, in_grad, out_grad)
    token_grad, gate_grad, in_grad, out_grad = pl.pallas_call(
        hand_on,
        out_shape=tuple(jax.ShapeDtypeStruct(r.shape, r.dtype) for r in results),
        in_specs=[vmem] * 4,
        out_specs=(vmem,) * 4,
    )(*results)
    return token_grad, gate_grad.reshape(TOK), in_grad[None], out_grad[None]


def solution(mesh):
    in_specs = (
        P(("dp", "expert"), None),
        P(("dp", "expert"), None),
        P(("dp", "expert")),
        P(),
        P("expert", "dp", None),
        P("expert", "dp", None),
        P(("dp", "expert"), None),
    )
    out_specs = (
        P(("dp", "expert"), None),
        P(("dp", "expert")),
        P("expert", "dp", None),
        P("expert", "dp", None),
    )
    return jax.shard_map(body, mesh=mesh, in_specs=in_specs, out_specs=out_specs, check_vma=False)
```
